32 devices in a mesh: fsdp: 4 (over x, core), seq: 8 (over z, y).
Axes of the slice: x: 2, y: 2, z: 4, core: 2. Of those that a mesh axis runs over, the one named last changes fastest.
Arguments:
- tokens: bfloat16 [4096, 1024], P(('fsdp', 'seq')), may hold values from -6 to 6
- attn_gain: bfloat16 [1024], P('fsdp'), may hold values from 0.099609375 to 1.8984375
- w_query: bfloat16 [1024, 1024], P('fsdp'), may hold values from -0.375 to 0.375
- w_latent: bfloat16 [1024, 512], P('fsdp'), may hold values from -0.1875 to 0.1875
- w_key_up: bfloat16 [256, 1024], P(None, 'fsdp'), may hold values from -0.375 to 0.375
- w_value_up: bfloat16 [256, 1024], P(None, 'fsdp'), may hold values from -0.375 to 0.375
- w_out: bfloat16 [1024, 1024], P('fsdp'), may hold values from -0.75 to 0.75
- mlp_gain: bfloat16 [1024], P('fsdp'), may hold values from 0.099609375 to 1.8984375
- w_gate: bfloat16 [1024, 2816], P('fsdp'), may hold values from -0.1875 to 0.1875
- w_up: bfloat16 [1024, 2816], P('fsdp'), may hold values from -0.1875 to 0.1875
- w_down: bfloat16 [2816, 1024], P('fsdp'), may hold values from -0.109375 to 0.109375
- lengths: int32 [4, 4], P('fsdp'), may hold values from 1 to 1021, as said below
- cotangent: bfloat16 [4096, 1024], P(('fsdp', 'seq')), may hold values from -6 to 6
Outputs:
- output: bfloat16 [4096, 1024], P(('fsdp', 'seq'))
- tokens_grad: bfloat16 [4096, 1024], P(('fsdp', 'seq'))
- grad_attn_gain: float32 [1024], P(('fsdp', 'seq'))
- grad_query: float32 [1024, 1024], P('fsdp', 'seq')
- grad_latent: float32 [1024, 512], P('fsdp', 'seq')
- grad_key_up: float32 [256, 1024], P(None, ('fsdp', 'seq'))
- grad_value_up: float32 [256, 1024], P(None, ('fsdp', 'seq'))
- grad_out: float32 [1024, 1024], P('seq', 'fsdp')
- grad_mlp_gain: float32 [1024], P(('fsdp', 'seq'))
- grad_gate: float32 [1024, 2816], P('fsdp', 'seq')
- grad_up: float32 [1024, 2816], P('fsdp', 'seq')
- grad_down: float32 [2816, 1024], P('seq', 'fsdp')
The draws below stay inside these ranges and needn't reach their ends.
Inputs may be any that keep to these rules, and one draw needn't show every extreme that they name: In each row, 4 document lengths that sum to 1024; the second document starts within the group's first 128 rows and ends within its last 128 rows.
All inputs are finite; a program needn't handle non-finite values.
Results may differ from the reference program's by a relative error of at most 0.018.
Values may be sent and summed in bfloat16 or wider, within the bound.
No kernel may reach another device: no remote copies, remote signals or barrier semaphores. Data moves between devices by JAX's collectives and lax.ppermute only.
A program may use at most 256 MiB of HBM per device.

```python
import jax
import jax.numpy as jnp
from jax import lax

D = 1024
HEADS = 16
HD = 64
GROUPS = 2
LAT_HEAD = 256
FF = 2816
TOK_DEV = 128
QW = 1024
GQ = 8
LATENT = 512
GSTREAM = 1024
TOKENS = 4096
N_FSDP = 4


def draw_lengths(key, part):
    key = jax.random.fold_in(key, 7)
    keys = jax.random.split(key, 4)
    chosen = jax.random.randint(keys[3], (), 0, N_FSDP)
    picked = jnp.arange(N_FSDP) == chosen
    first_doc = jax.random.randint(keys[0], (N_FSDP,), 1, TOK_DEV // 2 + 1)
    first_doc = jnp.where(picked, 1, first_doc)
    last_piece = jax.random.randint(keys[1], (N_FSDP,), TOK_DEV // 4, TOK_DEV - 1)
    last_piece = jnp.where(picked, TOK_DEV - 2, last_piece)
    tail_total = TOK_DEV - last_piece
    third_doc = jax.random.randint(keys[2], (N_FSDP,), 1, tail_total)
    third_doc = jnp.where(picked, 1, third_doc)
    second_doc = GSTREAM - first_doc - tail_total
    return jnp.stack([first_doc, second_doc, third_doc, tail_total - third_doc], axis=1).astype(jnp.int32)


def block_scale(own_key, dims, shards, smallest, largest):
    def one(position, blocks):
        steps = jax.random.uniform(jax.random.fold_in(jax.random.fold_in(own_key, 6), position), (blocks,), jnp.float32, smallest / len(shards), largest / len(shards))
        return jnp.repeat(jnp.exp(steps), dims[position] // blocks).reshape((-1,) + (1,) * (len(dims) - position - 1))

    factor_of = one(*shards[0])
    for cut in shards[1:]:
        factor_of = factor_of * one(*cut)
    return factor_of


def centred(rng, dims, scale, most, cuts=(), held_as=jnp.bfloat16):
    factor_of = block_scale(rng, dims, cuts, -0.22, 0.18) if cuts else 1.0
    drawn = jax.random.normal(rng, dims, jnp.float32) * scale * factor_of
    return jnp.minimum(jnp.maximum(drawn, -most), most).astype(held_as)


def setup_inputs(seed: int = 0) -> dict:
    key_of = jax.random.split(jax.random.key(seed), 14)
    tokens = centred(key_of[0], (TOKENS, D), 1.0, 6.0, ((0, 32),))
    attn_gain = jnp.clip(1.0 + 0.18 * jax.random.normal(key_of[1], (D,), jnp.float32), 0.099609375, 1.8984375).astype(jnp.bfloat16)
    w_query = centred(key_of[2], (D, QW), (D // 4) ** -0.5, 0.375, ((0, 4),))
    w_latent = centred(key_of[3], (D, LATENT), D ** -0.5, 0.1875, ((0, 4),))
    w_key_up = centred(key_of[4], (LAT_HEAD, QW), LAT_HEAD ** -0.5, 0.375, ((1, 4),))
    w_value_up = centred(key_of[5], (LAT_HEAD, QW), LAT_HEAD ** -0.5, 0.375, ((1, 4),))
    w_out = centred(key_of[6], (QW, D), (QW // 16) ** -0.5, 0.75, ((0, 4),))
    mlp_gain = jnp.clip(1.0 + 0.18 * jax.random.normal(key_of[7], (D,), jnp.float32), 0.099609375, 1.8984375).astype(jnp.bfloat16)
    w_gate = centred(key_of[8], (D, FF), D ** -0.5, 0.1875, ((0, 4),))
    w_up = centred(key_of[9], (D, FF), D ** -0.5, 0.1875, ((0, 4),))
    w_down = centred(key_of[10], (FF, D), FF ** -0.5, 0.109375, ((0, 4),))
    lengths = draw_lengths(jax.random.fold_in(key_of[13], 71), 0)
    cotangent = centred(key_of[12], (TOKENS, D), 1.0, 6.0, ((0, 32),))
    return {"tokens": tokens, "attn_gain": attn_gain, "w_query": w_query, "w_latent": w_latent, "w_key_up": w_key_up, "w_value_up": w_value_up, "w_out": w_out, "mlp_gain": mlp_gain, "w_gate": w_gate, "w_up": w_up, "w_down": w_down, "lengths": lengths, "cotangent": cotangent}


@jax.custom_vjp
def low(v):
    return lax.optimization_barrier(v.astype(jnp.bfloat16)).astype(jnp.float32)

@jax.custom_vjp
def low_back(v):
    return v

def low_keep(v):
    return (low(v), None)

def low_pass(kept, grad):
    return (grad,)

def back_keep(v):
    return (v, None)

def back_low(kept, grad):
    return (low(grad),)
low.defvjp(low_keep, low_pass)
low_back.defvjp(back_keep, back_low)
epsilon = 1e-06
highest = lax.Precision.HIGHEST

def product(left, right):
    return jnp.dot(left, right, precision=highest)

def normalize(values, gain):
    return values * lax.rsqrt(lax.optimization_barrier(jnp.mean(values * values, axis=-1, keepdims=True)) + epsilon) * gain

def doc_numbers(lengths_row, count):
    bounds = jnp.cumsum(lengths_row.astype(jnp.int32)).astype(jnp.int32)
    places = jnp.arange(count, dtype=jnp.int32)
    return lax.optimization_barrier(jnp.sum((places[:, None] >= bounds[None, :-1]).astype(jnp.int32), axis=1)).astype(jnp.int32)

def group_attention(queries, latent, key_up, value_up, doc_ids):
    count = queries.shape[0]
    head_width = GQ * HD
    key_list = []
    value_list = []
    for group_idx in range(GROUPS):
        latent_part = latent[:, group_idx * LAT_HEAD:(group_idx + 1) * LAT_HEAD]
        key_list.append(low(product(latent_part, key_up[:, group_idx * head_width:(group_idx + 1) * head_width])))
        value_list.append(low(product(latent_part, value_up[:, group_idx * head_width:(group_idx + 1) * head_width])))
    key_rows = jnp.concatenate(key_list, axis=1).reshape(count, HEADS, HD)
    value_rows = jnp.concatenate(value_list, axis=1).reshape(count, HEADS, HD)
    block_rows = min(256, count)
    places = jnp.arange(count, dtype=jnp.int32)

    @jax.checkpoint
    def one_block(pieces):
        query_block, docs_block, places_block = pieces
        scores = low_back(jnp.einsum('qhd,khd->hqk', query_block, key_rows, precision=highest) * 0.125)
        allowed = (docs_block[:, None] == doc_ids[None, :]) & (places_block[:, None] >= places[None, :])
        scores = jnp.where(allowed[None], scores, -1e+30)
        row_max = lax.optimization_barrier(jnp.max(scores, axis=-1, keepdims=True))
        row_total = row_max + jnp.log(lax.optimization_barrier(jnp.sum(jnp.exp(scores - row_max), axis=-1, keepdims=True)))
        attn_probs = low(jnp.exp(scores - row_total))
        mixed = jnp.einsum('hqk,khd->qhd', attn_probs, value_rows, precision=highest)
        return mixed.reshape(block_rows, HEADS * HD)
    steps_count = count // block_rows
    blocks = lax.map(one_block, (queries.reshape(steps_count, block_rows, HEADS, HD), doc_ids.reshape(steps_count, block_rows), places.reshape(steps_count, block_rows)))
    return blocks.reshape(count, HEADS * HD)

def forward(tokens_f, gain_a, w_query, w_latent, w_key_up, w_value_up, w_out, gain_m, w_gate, w_up, w_down, doc_ids):
    normed = low(normalize(tokens_f, gain_a))
    queries = low_back(low(product(normed, w_query)))
    latent = low_back(low(product(normed, w_latent)))

    def per_group(pieces):
        return group_attention(pieces[0], pieces[1], w_key_up, w_value_up, pieces[2])
    mixed = lax.map(per_group, (queries.reshape(N_FSDP, GSTREAM, QW), latent.reshape(N_FSDP, GSTREAM, LATENT), doc_ids))
    mixed = low_back(low(mixed.reshape(TOKENS, QW)))
    resid = tokens_f + low_back(product(mixed, w_out))
    normed_m = low(normalize(resid, gain_m))
    gate_pre = low_back(product(normed_m, w_gate))
    upward = low_back(product(normed_m, w_up))
    hidden = low_back(low(jax.nn.silu(gate_pre) * upward))
    return resid + product(hidden, w_down)

def reference(tokens, attn_gain, w_query, w_latent, w_key_up, w_value_up, w_out, mlp_gain, w_gate, w_up, w_down, lengths, cotangent):
    doc_ids = jnp.stack([doc_numbers(lengths[group_idx], GSTREAM) for group_idx in range(N_FSDP)])
    floats = [operand.astype(jnp.float32) for operand in (tokens, attn_gain, w_query, w_latent, w_key_up, w_value_up, w_out, mlp_gain, w_gate, w_up, w_down)]

    def layer(*operands):
        return forward(*operands, doc_ids)
    result, pull_back = jax.vjp(layer, *floats)
    gradients = pull_back(cotangent.astype(jnp.float32))
    return (result.astype(jnp.bfloat16), gradients[0].astype(jnp.bfloat16), gradients[1], gradients[2], gradients[3], gradients[4], gradients[5], gradients[6], gradients[7], gradients[8], gradients[9], gradients[10])
```

```python
import functools

import jax
import jax.numpy as jnp
from jax import lax
from jax.experimental import pallas as pl
from jax.experimental.pallas import tpu as pltpu
from jax.sharding import Mesh
from jax.sharding import PartitionSpec as P

HEADS = 16
HD = 64
GROUPS = 2
LAT_HEAD = 256
KEYBLK = 1024
QW = 1024
GQ = 8


epsilon = 1e-06


def normalize(values, gain):
    return values * lax.rsqrt(jnp.mean(values * values, axis=-1, keepdims=True) + epsilon) * gain


def doc_numbers(lengths_row, count):
    bounds = jnp.cumsum(lengths_row)
    places = jnp.arange(count, dtype=jnp.int32)
    return jnp.sum((places[:, None] >= bounds[None, :-1]).astype(jnp.int32), axis=1)


def contract_rows(left, right):
    return lax.dot_general(
        left, right, (((0,), (0,)), ((), ())), preferred_element_type=jnp.float32
    )


def contract_cols(left, right):
    return lax.dot_general(
        left, right, (((1,), (1,)), ((), ())), preferred_element_type=jnp.float32
    )


def split_parts(values):
    upper = values.astype(jnp.bfloat16)
    lower = (values - upper.astype(jnp.float32)).astype(jnp.bfloat16)
    return (upper, lower)


def gated_unit(gate_pre, upward):
    return jax.nn.silu(gate_pre) * upward


def body(
    tokens,
    attn_gain,
    w_query,
    w_latent,
    w_key_up,
    w_value_up,
    w_out,
    mlp_gain,
    w_gate,
    w_up,
    w_down,
    lengths,
    cotangent,
):
    attn_gain, w_query, w_latent, w_key_up, w_value_up, w_out, mlp_gain, w_gate, w_up, w_down = (
        lax.all_gather(attn_gain, "fsdp", axis=0, tiled=True),
        lax.all_gather(w_query, "fsdp", axis=0, tiled=True),
        lax.all_gather(w_latent, "fsdp", axis=0, tiled=True),
        lax.all_gather(w_key_up, "fsdp", axis=1, tiled=True),
        lax.all_gather(w_value_up, "fsdp", axis=1, tiled=True),
        lax.all_gather(w_out, "fsdp", axis=0, tiled=True),
        lax.all_gather(mlp_gain, "fsdp", axis=0, tiled=True),
        lax.all_gather(w_gate, "fsdp", axis=0, tiled=True),
        lax.all_gather(w_up, "fsdp", axis=0, tiled=True),
        lax.all_gather(w_down, "fsdp", axis=0, tiled=True),
    )
    row_count = tokens.shape[0]
    seq_rank = lax.axis_index("seq")
    stream_len = row_count * lax.axis_size("seq")
    head_width = GQ * HD
    doc_ids = doc_numbers(lengths[0], stream_len)
    row_start = seq_rank * row_count
    own_docs = lax.dynamic_slice_in_dim(doc_ids, row_start, row_count)
    own_places = row_start + jnp.arange(row_count, dtype=jnp.int32)
    block_count = (row_start + row_count - 1) // KEYBLK + 1
    tokens_f = tokens.astype(jnp.float32)
    gain_a = attn_gain.astype(jnp.float32)
    gain_m = mlp_gain.astype(jnp.float32)
    normed = normalize(tokens_f, gain_a).astype(jnp.bfloat16)
    queries = jnp.dot(normed, w_query, preferred_element_type=jnp.float32).astype(jnp.bfloat16)
    latent = jnp.dot(normed, w_latent, preferred_element_type=jnp.float32).astype(jnp.bfloat16)
    gathered = lax.all_gather(latent, "seq", axis=0, tiled=True)
    query_heads = queries.reshape(row_count, HEADS, HD)

    def key_block(source, block_idx, group_idx, with_values):
        latent_part = lax.dynamic_slice(
            source, (block_idx * KEYBLK, group_idx * LAT_HEAD), (KEYBLK, LAT_HEAD)
        )
        low_col = group_idx * head_width
        key_rows = (
            jnp.dot(
                latent_part,
                w_key_up[:, low_col : low_col + head_width],
                preferred_element_type=jnp.float32,
            )
            .astype(jnp.bfloat16)
            .reshape(KEYBLK, GQ, HD)
        )
        value_rows = None
        if with_values:
            value_rows = (
                jnp.dot(
                    latent_part,
                    w_value_up[:, low_col : low_col + head_width],
                    preferred_element_type=jnp.float32,
                )
                .astype(jnp.bfloat16)
                .reshape(KEYBLK, GQ, HD)
            )
        key_docs = lax.dynamic_slice_in_dim(doc_ids, block_idx * KEYBLK, KEYBLK)
        key_places = block_idx * KEYBLK + jnp.arange(KEYBLK, dtype=jnp.int32)
        allowed = (own_docs[:, None] == key_docs[None, :]) & (
            own_places[:, None] >= key_places[None, :]
        )
        return (latent_part, key_rows, value_rows, allowed)

    def block_scores(group_idx, key_rows):
        group_query = query_heads[:, group_idx * GQ : (group_idx + 1) * GQ]
        return (
            jnp.einsum("qhd,khd->hqk", group_query, key_rows, preferred_element_type=jnp.float32)
            * 0.125
        )

    def first_pass(block_idx, carried):
        row_max, row_total = carried
        max_list = []
        total_list = []
        for group_idx in range(GROUPS):
            _, key_rows, _, allowed = key_block(gathered, block_idx, group_idx, False)
            masked = jnp.where(allowed[None], block_scores(group_idx, key_rows), -1e30)
            old_max = row_max[group_idx * GQ : (group_idx + 1) * GQ]
            new_max = jnp.maximum(old_max, jnp.max(masked, axis=-1))
            row_mass = jnp.sum(
                jnp.where(allowed[None], jnp.exp(masked - new_max[:, :, None]), 0.0), axis=-1
            )
            max_list.append(new_max)
            total_list.append(
                row_total[group_idx * GQ : (group_idx + 1) * GQ] * jnp.exp(old_max - new_max)
                + row_mass
            )
        return (jnp.concatenate(max_list, axis=0), jnp.concatenate(total_list, axis=0))

    start_max = jnp.full((HEADS, row_count), -1e30, jnp.float32)
    start_total = jnp.zeros((HEADS, row_count), jnp.float32)
    row_max, row_total = lax.fori_loop(0, block_count, first_pass, (start_max, start_total))
    logsum = row_max + jnp.log(row_total)

    def block_probs(group_idx, key_rows, allowed):
        group_logsum = logsum[group_idx * GQ : (group_idx + 1) * GQ]
        return jnp.where(
            allowed[None],
            jnp.exp(block_scores(group_idx, key_rows) - group_logsum[:, :, None]),
            0.0,
        )

    def second_pass(block_idx, carried):
        rounded_sum, exact_sum = carried
        rounded_list = []
        exact_list = []
        for group_idx in range(GROUPS):
            _, key_rows, value_rows, allowed = key_block(gathered, block_idx, group_idx, True)
            attn_probs = block_probs(group_idx, key_rows, allowed)
            probs_upper, probs_lower = split_parts(attn_probs)
            rounded_part = jnp.einsum(
                "hqk,khd->qhd", probs_upper, value_rows, preferred_element_type=jnp.float32
            )
            rounded_list.append(rounded_part)
            exact_list.append(
                rounded_part
                + jnp.einsum(
                    "hqk,khd->qhd", probs_lower, value_rows, preferred_element_type=jnp.float32
                )
            )
        return (
            rounded_sum + jnp.concatenate(rounded_list, axis=1),
            exact_sum + jnp.concatenate(exact_list, axis=1),
        )

    head_zeros = jnp.zeros((row_count, HEADS, HD), jnp.float32)
    rounded_sum, exact_sum = lax.fori_loop(0, block_count, second_pass, (head_zeros, head_zeros))
    mixed = rounded_sum.reshape(row_count, QW).astype(jnp.bfloat16)
    resid = tokens_f + jnp.dot(mixed, w_out, preferred_element_type=jnp.float32)
    normed_m = normalize(resid, gain_m).astype(jnp.bfloat16)
    gate_pre = jnp.dot(normed_m, w_gate, preferred_element_type=jnp.float32)
    upward = jnp.dot(normed_m, w_up, preferred_element_type=jnp.float32)
    hidden = gated_unit(gate_pre, upward).astype(jnp.bfloat16)
    output = (resid + jnp.dot(hidden, w_down, preferred_element_type=jnp.float32)).astype(
        jnp.bfloat16
    )
    dhidden = contract_cols(cotangent, w_down).astype(jnp.bfloat16)
    _, pull_unit = jax.vjp(gated_unit, gate_pre, upward)
    dgate, dupward = pull_unit(dhidden.astype(jnp.float32))
    dgate = dgate.astype(jnp.bfloat16)
    dupward = dupward.astype(jnp.bfloat16)
    dnormed_m = contract_cols(dgate, w_gate) + contract_cols(dupward, w_up)
    _, pull_norm_m = jax.vjp(normalize, resid, gain_m)
    dresid_norm, grad_mlp_gain = pull_norm_m(dnormed_m)
    dresid = cotangent.astype(jnp.float32) + dresid_norm
    dattn = dresid.astype(jnp.bfloat16)
    dmixed = contract_cols(dattn, w_out).astype(jnp.bfloat16)
    grad_heads = dmixed.reshape(row_count, HEADS, HD)
    row_delta = jnp.einsum("qhd,qhd->hq", grad_heads.astype(jnp.float32), exact_sum)
    source = gathered

    def backward_pass(block_idx, carried):
        dqueries, dlatent, grad_ku, grad_vu = carried
        query_list = []
        fresh_latent = []
        for group_idx in range(GROUPS):
            latent_part, key_rows, value_rows, allowed = key_block(
                source, block_idx, group_idx, True
            )
            low_col = group_idx * head_width
            group_query = query_heads[:, group_idx * GQ : (group_idx + 1) * GQ]
            group_grad = grad_heads[:, group_idx * GQ : (group_idx + 1) * GQ]
            attn_probs = block_probs(group_idx, key_rows, allowed)
            prob_grad = jnp.einsum(
                "qhd,khd->hqk", group_grad, value_rows, preferred_element_type=jnp.float32
            )
            group_delta = row_delta[group_idx * GQ : (group_idx + 1) * GQ]
            score_grad = (attn_probs * (prob_grad - group_delta[:, :, None])).astype(jnp.bfloat16)
            query_list.append(
                jnp.einsum("hqk,khd->qhd", score_grad, key_rows, preferred_element_type=jnp.float32)
                * 0.125
            )
            key_grad = (
                jnp.einsum(
                    "hqk,qhd->khd", score_grad, group_query, preferred_element_type=jnp.float32
                )
                * 0.125
            ).reshape(KEYBLK, head_width)
            value_grad = jnp.einsum(
                "hqk,qhd->khd",
                attn_probs.astype(jnp.bfloat16),
                group_grad,
                preferred_element_type=jnp.float32,
            ).reshape(KEYBLK, head_width)
            key_upper, key_lower = split_parts(key_grad)
            value_upper, value_lower = split_parts(value_grad)
            key_weight = w_key_up[:, low_col : low_col + head_width]
            value_weight = w_value_up[:, low_col : low_col + head_width]
            latent_grad = (
                contract_cols(key_upper, key_weight)
                + contract_cols(key_lower, key_weight)
                + contract_cols(value_upper, value_weight)
                + contract_cols(value_lower, value_weight)
            )
            fresh_latent.append(
                lax.dynamic_update_slice_in_dim(
                    dlatent[group_idx], latent_grad, block_idx * KEYBLK, 0
                )
            )
            grad_ku = grad_ku.at[:, low_col : low_col + head_width].add(
                contract_rows(latent_part, key_upper) + contract_rows(latent_part, key_lower)
            )
            grad_vu = grad_vu.at[:, low_col : low_col + head_width].add(
                contract_rows(latent_part, value_upper) + contract_rows(latent_part, value_lower)
            )
        return (
            dqueries + jnp.concatenate(query_list, axis=1),
            tuple(fresh_latent),
            grad_ku,
            grad_vu,
        )

    latent_zeros = tuple(
        (jnp.zeros((stream_len, LAT_HEAD), jnp.float32) for group_idx in range(GROUPS))
    )
    weight_zeros = jnp.zeros((LAT_HEAD, QW), jnp.float32)
    dqueries, dlatent, grad_key_up, grad_value_up = lax.fori_loop(
        0, block_count, backward_pass, (head_zeros, latent_zeros, weight_zeros, weight_zeros)
    )
    dqueries = dqueries.reshape(row_count, QW).astype(jnp.bfloat16)
    shares = (
        lax.psum_scatter(dlatent[0], "seq", scatter_dimension=0, tiled=True),
        lax.psum_scatter(dlatent[1], "seq", scatter_dimension=0, tiled=True),
    )
    dlatent_own = jnp.concatenate(shares, axis=1).astype(jnp.bfloat16)
    dnormed = contract_cols(dqueries, w_query) + contract_cols(dlatent_own, w_latent)
    _, pull_norm_a = jax.vjp(normalize, tokens_f, gain_a)
    dtokens_norm, grad_attn_gain = pull_norm_a(dnormed)
    tokens_grad = (dresid + dtokens_norm).astype(jnp.bfloat16)
    normed_all, normed_m_all, cotangent_all, dattn_all = (
        lax.all_gather(normed, "seq", axis=0, tiled=True),
        lax.all_gather(normed_m, "seq", axis=0, tiled=True),
        lax.all_gather(cotangent, "seq", axis=0, tiled=True),
        lax.all_gather(dattn, "seq", axis=0, tiled=True),
    )
    hidden_cols, dgate_cols, dupward_cols, mixed_cols, dquery_cols, dlatent_cols = (
        lax.all_to_all(hidden, "seq", split_axis=1, concat_axis=0, tiled=True),
        lax.all_to_all(dgate, "seq", split_axis=1, concat_axis=0, tiled=True),
        lax.all_to_all(dupward, "seq", split_axis=1, concat_axis=0, tiled=True),
        lax.all_to_all(mixed, "seq", split_axis=1, concat_axis=0, tiled=True),
        lax.all_to_all(dqueries, "seq", split_axis=1, concat_axis=0, tiled=True),
        lax.all_to_all(dlatent_own, "seq", split_axis=1, concat_axis=0, tiled=True),
    )
    part_query = contract_rows(normed_all, dquery_cols)
    part_latent = contract_rows(normed_all, dlatent_cols)
    part_out = contract_rows(mixed_cols, dattn_all)
    part_gate = contract_rows(normed_m_all, dgate_cols)
    part_up = contract_rows(normed_m_all, dupward_cols)
    part_down = contract_rows(hidden_cols, cotangent_all)
    grad_query, grad_latent, grad_out, grad_gate, grad_up, grad_down = (
        lax.psum_scatter(
            part_query.astype(jnp.bfloat16), "fsdp", scatter_dimension=0, tiled=True
        ).astype(jnp.float32),
        lax.psum_scatter(
            part_latent.astype(jnp.bfloat16), "fsdp", scatter_dimension=0, tiled=True
        ).astype(jnp.float32),
        lax.psum_scatter(
            part_out.astype(jnp.bfloat16), "fsdp", scatter_dimension=1, tiled=True
        ).astype(jnp.float32),
        lax.psum_scatter(
            part_gate.astype(jnp.bfloat16), "fsdp", scatter_dimension=0, tiled=True
        ).astype(jnp.float32),
        lax.psum_scatter(
            part_up.astype(jnp.bfloat16), "fsdp", scatter_dimension=0, tiled=True
        ).astype(jnp.float32),
        lax.psum_scatter(
            part_down.astype(jnp.bfloat16), "fsdp", scatter_dimension=1, tiled=True
        ).astype(jnp.float32),
    )
    small_sent = (
        lax.psum_scatter(grad_attn_gain, ("fsdp", "seq"), scatter_dimension=0, tiled=True),
        lax.psum_scatter(grad_key_up, ("fsdp", "seq"), scatter_dimension=1, tiled=True),
        lax.psum_scatter(grad_value_up, ("fsdp", "seq"), scatter_dimension=1, tiled=True),
        lax.psum_scatter(grad_mlp_gain, ("fsdp", "seq"), scatter_dimension=0, tiled=True),
    )
    return (
        output,
        tokens_grad,
        small_sent[0],
        grad_query,
        grad_latent,
        small_sent[1],
        small_sent[2],
        grad_out,
        small_sent[3],
        grad_gate,
        grad_up,
        grad_down,
    )


BF = jnp.bfloat16
F32 = jnp.float32
NEG = -1e30
SCALE = 0.125
RING = (0, 2, 4, 6, 7, 5, 3, 1)
MIB = 2**20

FS, ZS, Y0, Y1, ZH0, ZH1, ZL, ROW0 = 8, 12, 16, 17, 18, 19, 20, 21


def dot_nn(left, right):
    return lax.dot_general(left, right, (((1,), (0,)), ((), ())), preferred_element_type=F32)


def fold(total):
    return lax.rsqrt(jnp.mean(total * total, axis=-1, keepdims=True) + epsilon)


def at(index, size):
    return pl.ds(pl.multiple_of(index * size, size), size)


class Lazy:
    def __init__(self, ref, copy):
        self.ref, self.copy, self.shape = ref, copy, ref.shape

    def __getitem__(self, index):
        if self.copy is not None:
            self.copy.wait()
            self.copy = None
        return self.ref[index]


class Late:
    def __init__(self, ref, out, sem):
        self.ref, self.out, self.sem, self.shape, self.copy = ref, out, sem, ref.shape, None

    def __getitem__(self, index):
        return self.ref[index]

    def __setitem__(self, index, value):
        self.ref[index] = value

    def flush(self):
        self.copy = pltpu.make_async_copy(self.ref, self.out, self.sem)
        self.copy.start()


def call(kernel, n_smem, outs, scratch=(), limit=16, flops=1, far_in=(), far_out=()):
    far_in, far_out = tuple(far_in), tuple(far_out)
    n_out, n_far = len(outs), len(far_in) + len(far_out)

    def run(*args, deps=()):
        n_in = len(args) - n_smem

        def body(*refs):
            smem, ins, results = refs[:n_smem], list(refs[n_smem : n_smem + n_in]), list(refs[n_smem + n_in + len(deps) : n_smem + n_in + len(deps) + n_out])
            rest = refs[n_smem + n_in + len(deps) + n_out :]
            sems = rest[-1]
            far, own = rest[len(scratch) : len(scratch) + n_far], rest[: len(scratch)]
            for k, i in enumerate(far_in):
                copy = pltpu.make_async_copy(ins[i], far[k], sems.at[k])
                copy.start()
                ins[i] = Lazy(far[k], copy)
            late = []
            for k, i in enumerate(far_out):
                results[i] = Late(far[len(far_in) + k], results[i], sems.at[len(far_in) + k])
                late.append(results[i])
            kernel(*smem, *ins, *results, *own)
            for i in far_in:
                if ins[i].copy is not None:
                    ins[i].copy.wait()
            for v in late:
                if v.copy is None:
                    v.flush()
            for v in late:
                v.copy.wait()

        spec = lambda i, far: pl.BlockSpec(memory_space=pl.ANY if i in far else pltpu.VMEM)
        shapes = [pltpu.VMEM(shape, dtype) for shape, dtype in scratch]
        shapes += [pltpu.VMEM(args[n_smem + i].shape, args[n_smem + i].dtype) for i in far_in]
        shapes += [pltpu.VMEM(*outs[i]) for i in far_out]
        return pl.pallas_call(
            body,
            in_specs=[pl.BlockSpec(memory_space=pltpu.SMEM)] * n_smem + [spec(i, far_in) for i in range(n_in)] + [pl.BlockSpec(memory_space=pl.ANY)] * len(deps),
            out_specs=[spec(i, far_out) for i in range(n_out)],
            out_shape=[jax.ShapeDtypeStruct(shape, dtype) for shape, dtype in outs],
            scratch_shapes=shapes + [pltpu.SemaphoreType.DMA((max(1, n_far),))],
            compiler_params=pltpu.CompilerParams(vmem_limit_bytes=limit * MIB),
            cost_estimate=pl.CostEstimate(flops=flops, bytes_accessed=0, transcendentals=0),
        )(*args, *deps)

    return run


def attend_kernel(idx, lens, *refs):
    tok, wl, wb = refs[0:8], refs[8:12], refs[12:18]
    mixed_ref, probs_ref, out_ref, qs_ref, q_ref, na_ref, lat_ref, wq_ref, wk_ref, wv_ref, wlt_ref, bias_ref = refs[18:30]
    rows, d = tok[0].shape
    keys = 8 * rows
    part = wl[0].shape[0]
    width = GQ * rows
    for k in range(4):
        here = at(idx[FS + k], part)
        wlt_ref[:, here] = wl[k][...].T
        if k < 2:
            wq_ref[here, :] = wb[k][:, 0:QW]
            wk_ref[:, here] = wb[k][:, QW : QW + LAT_HEAD]
            wv_ref[:, here] = wb[k][:, QW + LAT_HEAD : QW + 2 * LAT_HEAD]
        else:
            first, second = wb[2 * k - 2], wb[2 * k - 1]
            cut = first.shape[1]
            wq_ref[here, 0:cut] = first[...]
            wq_ref[here, cut:QW] = second[:, 0 : QW - cut]
            wk_ref[:, here] = second[:, QW - cut : QW - cut + LAT_HEAD]
            wv_ref[:, here] = second[:, QW - cut + LAT_HEAD : QW - cut + 2 * LAT_HEAD]
    for i in range(8):
        values = tok[i][...].astype(F32)
        normed = (values * fold(values)).astype(BF)
        na_ref[at(idx[i], rows), :] = normed
        if i == 0:
            q_ref[...] = dot_nn(normed, wq_ref[...]).astype(BF)
    lat_ref[...] = contract_cols(na_ref[...], wlt_ref[...]).astype(BF)
    for ref in (wq_ref, wk_ref, wv_ref, wlt_ref, q_ref, na_ref, lat_ref):
        ref.flush()
    place = lax.broadcasted_iota(jnp.int32, (rows, keys), 1)
    own = idx[ROW0] + lax.broadcasted_iota(jnp.int32, (rows, keys), 0)
    first = jnp.zeros((rows, keys), jnp.int32)
    edge = 0
    for i in range(lens.shape[1] - 1):
        edge = edge + lens[0, i]
        first = jnp.where(own >= edge, edge, first)
    bias = jnp.where((place >= first) & (place <= own), 0.0, NEG)
    bias_ref[0:rows, :] = bias
    bias_ref[rows : 2 * rows, :] = bias
    low = lax.broadcasted_iota(jnp.int32, (rows, 2 * HD), 1) < HD
    for p in range(HEADS // 2):
        cols = slice(p * 2 * HD, (p + 1) * 2 * HD)
        q = q_ref[:, cols]
        none = jnp.zeros_like(q)
        for j, own_q in enumerate((jnp.where(low, q, none), jnp.where(low, none, q))):
            qs_ref[(2 * p + j) * rows : (2 * p + j + 1) * rows, :] = (contract_cols(own_q, wk_ref[:, cols]) * SCALE).astype(BF)
    for g in range(GROUPS):
        lat = lat_ref[:, g * LAT_HEAD : (g + 1) * LAT_HEAD]
        for r in range(0, width, 2 * rows):
            band = slice(g * width + r, g * width + r + 2 * rows)
            scores = contract_cols(qs_ref[band, :], lat) + bias_ref[...]
            mass = jnp.exp(scores - jnp.max(scores, axis=-1, keepdims=True))
            probs_ref[band, :] = (mass * (1.0 / jnp.sum(mass, axis=-1, keepdims=True))).astype(BF)
        band = slice(g * width, (g + 1) * width)
        out_ref[band, :] = dot_nn(probs_ref[band, :], lat).astype(BF)
    for ref in (probs_ref, qs_ref, out_ref):
        ref.flush()
    for p in range(HEADS // 2):
        cols = slice(p * 2 * HD, (p + 1) * 2 * HD)
        a, b = (dot_nn(out_ref[(2 * p + j) * rows : (2 * p + j + 1) * rows, :], wv_ref[:, cols]) for j in range(2))
        mixed_ref[:, cols] = jnp.where(low, a, b).astype(BF)


def attend(idx, lens, blocks, w_lats, w_bigs, deps=()):
    rows, d = blocks[0].shape
    keys, n_lat = 8 * rows, GROUPS * LAT_HEAD
    outs = [(rows, QW), (HEADS * rows, keys), (HEADS * rows, LAT_HEAD), (HEADS * rows, LAT_HEAD), (rows, QW)]
    outs += [(keys, d), (keys, n_lat), (d, QW), (LAT_HEAD, QW), (LAT_HEAD, QW), (n_lat, d)]
    macs = 2 * HEADS * rows * keys * LAT_HEAD + keys * d * n_lat
    return call(
        attend_kernel, 2, [(v, BF) for v in outs], [((2 * rows, keys), F32)], limit=60,
        far_in=range(18), far_out=range(1, 11),
    )(
        idx, lens, *blocks, *w_lats, *w_bigs, deps=deps
    )


def quarters(idx, parts):
    own, near, far, diag, other, last = parts
    half = far.shape[0]
    yield own, at(idx[FS], 2 * half)
    yield near, at(idx[FS + 1], 2 * half)
    yield far, at(idx[FS + 2] * 2 + idx[Y0], half)
    yield diag, at(idx[FS + 3] * 2 + idx[Y0], half)
    yield other, at(idx[FS + 2] * 2 + idx[Y1], half)
    yield last, at(idx[FS + 3] * 2 + idx[Y1], half)


def project_kernel(idx, mixed, tok, *refs):
    parts, (cot, cot_up, cot_far, gu_c, resid_ref, normed_ref, pack_ref, corner_ref) = refs[:4], refs[4:]
    total = tok[...].astype(F32)
    for k, w in enumerate(parts):
        total = total + dot_nn(mixed[:, at(idx[FS + k], w.shape[0])], w[...])
    resid_ref[...] = total
    normed = (total * fold(total)).astype(BF)
    normed_ref[...] = normed
    rows = normed.shape[0]
    corner_ref[0:rows, :] = normed
    corner_ref[rows:, :] = cot[...]
    pack_ref[0:rows, :] = normed
    pack_ref[rows : 2 * rows, :] = cot_up[...]
    pack_ref[2 * rows : 3 * rows, :] = cot_far[...]
    pack_ref[3 * rows :, 0 : gu_c.shape[1]] = gu_c[...]
    pack_ref[3 * rows :, gu_c.shape[1] :] = jnp.zeros((rows, pack_ref.shape[1] - gu_c.shape[1]), BF)


def columns_kernel(idx, gate_ref, up_ref, gain_ref, own_ref, near_ref, far_ref, other_ref, all_ref):
    gain = gain_ref[...].astype(F32)
    n, rows, two = all_ref.shape
    cols = gate_ref.shape[1] // n
    gap = jnp.zeros((rows, two // 2 - cols), BF)
    for j in range(n):
        for part, ref in enumerate((gate_ref, up_ref)):
            block = (ref[:, j * cols : (j + 1) * cols].astype(F32) * gain).astype(BF)
            all_ref[j, :, part * (two // 2) : (part + 1) * (two // 2)] = jnp.concatenate([block, gap], axis=1)
    band = at(idx[Y0], rows // 2)
    own_ref[...] = all_ref[2 * idx[FS] + idx[ZL]]
    near_ref[...] = all_ref[2 * idx[FS + 1] + idx[ZL]]
    far_ref[...] = all_ref[2 * idx[FS + 2] + idx[ZL], band, :]
    other_ref[...] = all_ref[2 * idx[FS + 3] + idx[ZL], band, :]


def assemble_kernel(idx, *refs):
    parts, (down, gu_ref, dn_ref) = refs[:6], refs[6:]
    n = gu_ref.shape[1]
    for i, (w, where) in enumerate(quarters(idx, parts)):
        gu_ref[where, :] = w[-parts[2].shape[0] :, :n] if i == 3 else w[...]
    n = down.shape[0] // 2
    dn_ref[0:n, :] = down[at(idx[ZL], n), :]
    dn_ref[n:, :] = jnp.zeros((dn_ref.shape[0] - n, dn_ref.shape[1]), BF)


def rows_of(ref, where, rows):
    return ref[where : where + rows, :]


def unit_kernel(places, n0, n1, c0, c1, w_gu, w_dn, hid_ref, both_ref, dkeep, dsend, okeep, osend):
    rows = dkeep.shape[0]
    wide = w_dn.shape[0]
    n0, n1, c0, c1 = (rows_of(ref, p, rows) for ref, p in zip((n0, n1, c0, c1), places))
    both = dot_nn(jnp.concatenate([n0, n1], 0), w_gu[...])
    gate, upward = both[:, :wide], both[:, wide:]
    dhid = contract_cols(jnp.concatenate([c0, c1], 0), w_dn[...]).astype(BF).astype(F32)
    sig = jax.nn.sigmoid(gate)
    act = gate * sig
    hid = (act * upward).astype(BF)
    hid_ref[...] = hid
    both_ref[:, :wide] = (dhid * upward * sig * (1.0 + gate * (1.0 - sig))).astype(BF)
    both_ref[:, wide:] = (dhid * act).astype(BF)
    dn = contract_cols(both_ref[...], w_gu[...])
    dkeep[...] = dn[:rows]
    dsend[...] = dn[rows:].astype(BF)
    out = dot_nn(hid, w_dn[...])
    okeep[...] = out[:rows]
    osend[...] = out[rows:].astype(BF)


def relative_columns(idx, shard):
    return [at(2 * idx[yy] + idx[zz], shard) for yy in (Y1, Y0) for zz in (ZH1, ZH0)]


def grow_kernel(places, idx, hid, both, n0, n1, c0, c1, *refs):
    down_ref, gu_ref = refs[-2:]
    shard = n0.shape[1] // 4
    rows = hid.shape[0] // 2
    for j, cols in enumerate(relative_columns(idx, shard)):
        here = slice(j * shard, (j + 1) * shard)
        v0, v1, t0, t1 = (ref[p : p + rows, cols] for ref, p in zip((n0, n1, c0, c1), places))
        down = contract_rows(hid[...], jnp.concatenate([t0, t1], 0))
        gu = contract_rows(both[...], jnp.concatenate([v0, v1], 0))
        if len(refs) == 4:
            down, gu = down + refs[0][:, here], gu + refs[1][:, here]
        down_ref[:, here] = down
        gu_ref[:, here] = gu


def last_kernel(ff8, places, idx, hid, both, n0, n1, c0, c1, down_ref, gu_ref, send1, keep1, send2, keep2):
    shard = n0.shape[1] // 4
    rows = hid.shape[0] // 2
    wide = (ff8 + 127) // 128 * 128
    for j, cols in enumerate(relative_columns(idx, shard)):
        here = slice(j * shard, (j + 1) * shard)
        there = slice(j % 2 * shard, (j % 2 + 1) * shard)
        v0, v1, t0, t1 = (ref[p : p + rows, cols] for ref, p in zip((n0, n1, c0, c1), places))
        down = down_ref[:, here] + contract_rows(hid[...], jnp.concatenate([t0, t1], 0))
        gu = gu_ref[:, here] + contract_rows(both[...], jnp.concatenate([v0, v1], 0))
        one, two = (send1, send2) if j < 2 else (keep1, keep2)
        one[0:ff8, there] = down[0:ff8].astype(BF)
        one[ff8:, there] = gu[0:ff8].astype(BF)
        two[:, there] = gu[wide : wide + ff8].astype(BF)


def middle_kernel(idx, dkeep, near, far, up, diag, resid_ref, cot, *refs):
    parts, (dresid_ref, dattn_ref, dmixed_ref, sum_ref) = refs[:4], refs[4:]
    e = dkeep[...]
    for v in (near, far, up, diag):
        e = e + v[...].astype(F32)
    resid = resid_ref[...]
    rms = fold(resid)
    n = resid * rms
    en = e * n
    dresid = cot[...].astype(F32) + rms * (e - n * jnp.mean(en, axis=-1, keepdims=True))
    dresid_ref[...] = dresid
    dattn = dresid.astype(BF)
    dattn_ref[...] = dattn
    sum_ref[...] = jnp.broadcast_to(jnp.sum(en, axis=0, keepdims=True), sum_ref.shape)
    for k, w in enumerate(parts):
        dmixed_ref[:, at(idx[FS + k], w.shape[0])] = contract_cols(dattn, w[...]).astype(BF)


def outer_out_kernel(idx, mixed, dattn, send, keep):
    rows = mixed.shape[0]
    shard = send.shape[2]
    for out, ks in ((send, (1, 3)), (keep, (0, 2))):
        for i, k in enumerate(ks):
            right = dattn[:, at(idx[FS + k], shard)]
            for j, yy in enumerate((Y1, Y0)):
                for kz in range(4):
                    left = mixed[:, at(2 * idx[ZS + kz] + idx[yy], rows)]
                    out[i, (4 * j + kz) * rows : (4 * j + kz + 1) * rows, :] = contract_rows(left, right).astype(BF)


def attend_back_kernel(idx, dm_ref, q_ref, lat_ref, wk_ref, wv_ref, probs_ref, out_ref, qs_ref, dlat_ref, send, keep, dq_ref, up_ref, ds_ref, do_ref, dqs_ref):
    rows = dm_ref.shape[0]
    width = GQ * rows
    half = HD // 2
    low = lax.broadcasted_iota(jnp.int32, (rows, 2 * HD), 1) < HD
    for p in range(HEADS // 2):
        cols = slice(p * 2 * HD, (p + 1) * 2 * HD)
        dm = dm_ref[:, cols]
        none = jnp.zeros_like(dm)
        for j, own in enumerate((jnp.where(low, dm, none), jnp.where(low, none, dm))):
            do_ref[(2 * p + j) * rows : (2 * p + j + 1) * rows, :] = contract_cols(own, wv_ref[:, cols]).astype(BF)
    for g in range(GROUPS):
        lat = lat_ref[:, g * LAT_HEAD : (g + 1) * LAT_HEAD]
        for r in range(0, width, 2 * rows):
            band = slice(g * width + r, g * width + r + 2 * rows)
            do = do_ref[band, :]
            delta = jnp.sum(do.astype(F32) * out_ref[band, :].astype(F32), axis=-1, keepdims=True)
            ds_ref[band, :] = (probs_ref[band, :].astype(F32) * (contract_cols(do, lat) - delta)).astype(BF)
        band = slice(g * width, (g + 1) * width)
        dlat_ref[:, g * LAT_HEAD : (g + 1) * LAT_HEAD] = (
            contract_rows(ds_ref[band, :], qs_ref[band, :]) + contract_rows(probs_ref[band, :], do_ref[band, :])
        ).astype(BF)
        dqs_ref[band, :] = (dot_nn(ds_ref[band, :], lat) * SCALE).astype(BF)
    for p in range(HEADS // 2):
        cols = slice(p * 2 * HD, (p + 1) * 2 * HD)
        bands = [slice((2 * p + j) * rows, (2 * p + j + 1) * rows) for j in range(2)]
        a, b = (dot_nn(dqs_ref[band, :], wk_ref[:, cols]) for band in bands)
        dq_ref[:, cols] = jnp.where(low, a, b).astype(BF)
        f, s = divmod(4 * p, 8)
        for j, band in enumerate(bands):
            gk = contract_rows(q_ref[:, cols], dqs_ref[band, :]).astype(BF)
            gv = contract_rows(dm_ref[:, cols], out_ref[band, :]).astype(BF)
            for i in range(2):
                piece = slice((2 * j + i) * half, (2 * j + i + 1) * half)
                up_ref[f, s + 2 * j + i, 0:half, :] = gk[piece, :]
                up_ref[f, s + 2 * j + i, half:HD, :] = gv[piece, :]
    for k in range(4):
        for out, yy in ((send, Y1), (keep, Y0)):
            block = 2 * idx[ZS + k] + idx[yy]
            n = dlat_ref.shape[1]
            out[k * rows : (k + 1) * rows, 0:n] = dlat_ref[at(block, rows), :]
            out[k * rows : (k + 1) * rows, n:] = dq_ref[:, at(block, 2 * HD)]


def bundle_kernel(idx, dlat, na, wlt, dq, wq, ups, sum_ref, e_ref, send, keep, part_ref, sums_ref):
    rows = dq.shape[0]
    e = contract_cols(dq[...], wq[...])
    e_ref[...] = e
    total = jnp.sum(na[at(idx[ROW0] // rows, rows), :].astype(F32) * e, axis=0, keepdims=True)
    for g in range(GROUPS):
        band = slice(g * LAT_HEAD, (g + 1) * LAT_HEAD)
        part = contract_rows(dlat[:, band], na[...])
        part_ref[band, :] = part.astype(BF)
        total = total + jnp.sum(part * wlt[band, :].astype(F32), axis=0, keepdims=True)
    line = lax.broadcasted_iota(jnp.int32, (16, total.shape[1]), 0)
    sums_ref[...] = jnp.where(line == 0, total, jnp.where(line == 1, sum_ref[0:1, :], 0.0)).astype(BF)
    shard = send.shape[3]
    n_lat = part_ref.shape[0] // 8
    for out, ks in ((send, (1, 3)), (keep, (0, 2))):
        for i, k in enumerate(ks):
            cols = at(idx[FS + k], shard)
            for j, yy in enumerate((Y1, Y0)):
                for kz in range(4):
                    s = 2 * idx[ZS + kz] + idx[yy]
                    out[i, 4 * j + kz, 0:HD, :] = ups[idx[FS + k], s]
                    out[i, 4 * j + kz, HD : HD + n_lat, :] = part_ref[at(s, n_lat), cols]
                    out[i, 4 * j + kz, HD + n_lat :, :] = sums_ref[:, cols]


def outer_query_kernel(idx, na, p0, p1, p2, p3, send, keep, total_ref):
    rows = p0.shape[0]
    wide = 2 * HD
    total = None
    for k, piece in enumerate((p0, p1, p2, p3)):
        first = piece.shape[1] - 2 * wide
        for j, yy in enumerate((Y0, Y1)):
            right = piece[:, first + j * wide : first + (j + 1) * wide]
            term = contract_rows(na[at(2 * idx[ZS + k] + idx[yy], rows), :], right)
            total = term if total is None else total + term
    total_ref[...] = total.astype(BF)
    shard = send.shape[1]
    for out, ks in ((send, (1, 3)), (keep, (0, 2))):
        for i, k in enumerate(ks):
            out[i, :, :] = total_ref[at(idx[FS + k], shard), :]


def tokens_kernel(p0, p1, p2, p3, e_ref, wlt, tok, dresid, out_ref):
    n = wlt.shape[0]
    dlat = wide_sum(p0[:, 0:n], p1[:, 0:n]) + wide_sum(p2[:, 0:n], p3[:, 0:n])
    e = e_ref[...] + dot_nn(dlat.astype(BF), wlt[...])
    values = tok[...].astype(F32)
    rms = fold(values)
    n = values * rms
    out_ref[...] = (dresid[...] + rms * (e - n * jnp.mean(e * n, axis=-1, keepdims=True))).astype(BF)


def wide_sum(left, right):
    return left.astype(F32) + right.astype(F32)


def pass_kernel(*refs):
    n = len(refs) // 2
    for src, dst in zip(refs[:n], refs[n:]):
        dst[...] = src[...]


def through(values, deps):
    return call(pass_kernel, 0, [(v.shape, v.dtype) for v in values])(*values, deps=deps)


def pairs_kernel(*refs):
    n = len(refs) // 3
    for i in range(n):
        refs[2 * n + i][...] = wide_sum(refs[2 * i][...], refs[2 * i + 1][...]).astype(BF)


def add_pairs(pairs, deps=()):
    return call(pairs_kernel, 0, [(a.shape, BF) for a, _ in pairs])(*[v for pair in pairs for v in pair], deps=deps)


def halves_kernel(*refs):
    n = len(refs) // 4
    for i in range(n):
        total = wide_sum(refs[2 * i][...], refs[2 * i + 1][...]).astype(BF)
        first, second = refs[2 * n + 2 * i : 2 * n + 2 * i + 2]
        cut = first.shape[1]
        first[...] = total[:, :cut]
        second[...] = total[:, cut:]


def two_kernel(keep, there, own, far):
    own[...] = wide_sum(keep[0], there[0]).astype(BF)
    far[...] = wide_sum(keep[1], there[1]).astype(BF)


def eleventh_kernel(up_keep, up_there, go_keep, go_there, up_a, go_own, cross):
    n, shard = up_a.shape
    total = wide_sum(up_keep[...], up_there[...]).astype(BF)
    up_a[...] = total[:, shard:]
    cross[0:n, :] = total[:, :shard]
    go_own[...] = wide_sum(go_keep[0], go_there[0]).astype(BF)
    cross[n:, :] = wide_sum(go_keep[1], go_there[1]).astype(BF)


def exchange_kernel(keep, there, go_own, cross, b_keep, b_there, p0, p1, p2, p3, go_all, b_own, b_far, up_b):
    two_kernel(b_keep, b_there, b_own, b_far)
    rows, wide = p0.shape
    n = wide - 4 * HD
    for k, out in enumerate((p0, p1, p2, p3)):
        band = slice(k * rows, (k + 1) * rows)
        out[:, 0:n] = wide_sum(keep[band, 0:n], there[band, 0:n]).astype(BF)
        out[:, n : n + 2 * HD] = keep[band, n:]
        out[:, n + 2 * HD :] = there[band, n:]
    n = up_b.shape[0]
    up_b[...] = cross[0:n, :]
    go_all[...] = wide_sum(go_own[...], cross[n:, :]).astype(BF)


def later_kernel(b_own, b_far, go_all, send, keep):
    half, tall = b_own.shape[0] // 2, b_own.shape[1]
    n = go_all.shape[0] // 2
    for out, h in ((send, 0), (keep, 1)):
        for i in range(half):
            out[i * tall : (i + 1) * tall, :] = wide_sum(b_own[h * half + i], b_far[h * half + i]).astype(BF)
        out[half * tall :, :] = go_all[h * n : (h + 1) * n, :]


def quarters_kernel(rows, keep, there, q_keep, q_there, *outs):
    two_kernel(q_keep, q_there, outs[4], outs[5])
    tall = outs[0].shape[0] - rows
    for k in range(4):
        for lo, n, into in ((k * tall, tall, 0), (4 * tall + k * rows, rows, tall)):
            outs[k][into : into + n, :] = wide_sum(keep[lo : lo + n, :], there[lo : lo + n, :]).astype(BF)


def stack_kernel(*refs):
    out = refs[-1]
    rows = refs[0].shape[0]
    for i, ref in enumerate(refs[:-1]):
        out[i * rows : (i + 1) * rows, :] = ref[...]


def outputs_kernel(k0, k1, k2, k3, there, own, *outs):
    rows = own.shape[0]
    own[...] = wide_sum(k0[...], there[0:rows, :])
    for i, (keep, out) in enumerate(zip((k1, k2, k3), outs)):
        out[...] = wide_sum(keep[...], there[(i + 1) * rows : (i + 2) * rows, :]).astype(BF)


def swap(value, axis):
    return lax.ppermute(value, axis, [(0, 1), (1, 0)])


def hop(value, k):
    return lax.ppermute(value, "z", [(i, i ^ k) for i in range(4)])


def corner(value):
    return lax.ppermute(value, ("x", "z"), [(i, i ^ 5) for i in range(8)])


def plus(left, right):
    return left.astype(F32) + right.astype(F32)


def fast_body(tokens, attn_gain, w_query, w_latent, w_key_up, w_value_up, w_out, mlp_gain, w_gate, w_up, w_down, lengths, cotangent):
    x, c, z, y = (lax.axis_index(a) for a in ("x", "c", "z", "y"))
    f, s, zl, zh = 2 * x + c, 2 * z + y, lax.rem(z, 2), z // 2
    rows, d = tokens.shape
    shard = d // 4
    half = shard // 2
    ff8 = w_gate.shape[1] // 8
    wide = (ff8 + 127) // 128 * 128
    n_lat = GROUPS * LAT_HEAD
    keys = 8 * rows

    cw = [(RING[i], RING[(i + 1) % 8]) for i in range(8)]
    ccw = [(b, a) for a, b in cw]
    place = jnp.where(y == 0, z, 7 - z)

    def owner(p):
        p = lax.rem(p + 8, 8)
        return jnp.where(p < 4, 2 * p, 15 - 2 * p)

    def ring(value, pairs):
        return lax.ppermute(value, ("z", "y"), pairs)

    def fold_into(gain, weight):
        return (weight.astype(F32) * gain).astype(BF)

    owners = [s, owner(place - 1), owner(place + 1), owner(place - 2), owner(place + 2), owner(place - 3), owner(place + 3), owner(place - 4)]
    idx = jnp.stack(owners + [f, f ^ 1, f ^ 2, f ^ 3, z, z ^ 1, z ^ 2, z ^ 3, y, y ^ 1, zh, zh ^ 1, zl, s * rows]).astype(jnp.int32)
    gain_a = attn_gain.astype(F32)[:, None]
    gain_m = mlp_gain.astype(F32)[:, None]

    a1, b1 = ring(tokens, cw), ring(tokens, ccw)
    wl_own = fold_into(gain_a, w_latent)
    wl_far, wl_near = swap(wl_own, "x"), swap(wl_own, "c")
    cut = QW * 3 // 4
    a1, b1 = through((a1, b1), (wl_far,))
    a2, b2 = ring(a1, cw), ring(b1, ccw)
    wl_diag = swap(wl_far, "c")
    wb_own = jnp.concatenate([fold_into(gain_a, w_query), w_key_up, w_value_up], axis=1)
    wb_own, wb_a, wb_b = through((wb_own, wb_own[:, :cut], wb_own[:, cut:]), (a1,))
    wb_near, wb_far = swap(wb_own, "c"), [swap(wb_a, "x")]
    gu_shapes = [((shard, 2 * wide), BF)] * 2 + [((half, 2 * wide), BF)] * 2
    gu_own, gu_near, gu_far, gu_other = call(columns_kernel, 1, gu_shapes, [((8, shard, 2 * wide), BF)], limit=16)(
        idx, w_gate, w_up, mlp_gain[:, None], deps=(a1,)
    )
    gu_near = swap(gu_near, "c")
    a2, b2 = through((a2, b2), (wb_far[0], gu_own))
    a3, b3 = ring(a2, cw), ring(b2, ccw)
    wb_far.append(swap(through((wb_b,), (a2,))[0], "x"))
    a3, wo_own = through((a3, w_out), (b3, wb_far[1]))
    a4 = ring(a3, cw)
    wo_far, wo_near = swap(wo_own, "x"), swap(wo_own, "c")
    wb_diag = [swap(v, "c") for v in wb_far]

    a4, gu_far, gu_other, cot = through((a4, gu_far, gu_other, cotangent), (wo_far,))
    wo_diag = swap(wo_far, "c")
    gu_far, gu_other = swap(gu_far, "x"), swap(gu_other, "x")
    cot_far, cot_up, cot_near = swap(cot, "x"), hop(cot, 1), swap(cot, "c")
    mixed, probs, outs, qs, queries, na_all, lat_all, w_q, w_key, w_value, w_lat_t = attend(
        idx, lengths, (tokens, a1, b1, a2, b2, a3, b3, a4), (wl_own, wl_near, wl_far, wl_diag), (wb_own, wb_near, *wb_far, *wb_diag)
    )
    w_os = (w_out, wo_near, wo_far, wo_diag)
    resid, normed, pack, corner_rows = call(
        project_kernel, 1, [((rows, d), F32), ((rows, d), BF), ((4 * rows, d), BF), ((2 * rows, d), BF)]
    )(idx, mixed, tokens, *w_os, cot, cot_up, cot_far, gu_other, deps=(gu_far,))

    pack = swap(pack, "c")
    nm_far, nm_up, diag_rows = swap(normed, "x"), hop(normed, 1), corner(corner_rows)
    gu_y, gu_yc = through((gu_far, gu_other), (normed,))
    gu_y = swap(gu_y, "y")
    gu_yc = lax.ppermute(gu_yc, ("c", "y"), [(i, i ^ 3) for i in range(4)])
    nm_up2, nm_far2, diag_rows2 = swap(nm_up, "c"), swap(nm_far, "c"), swap(diag_rows, "c")
    w_gu, w_dn = call(assemble_kernel, 1, [((d, 2 * wide), BF), ((wide, d), BF)])(
        idx, gu_own, gu_near, gu_far, pack, gu_y, gu_yc, w_down, deps=(nm_far, nm_up, diag_rows)
    )

    def unit(places, *args, deps=()):
        shapes = [((2 * rows, wide), BF), ((2 * rows, 2 * wide), BF), ((rows, d), F32), ((rows, d), BF), ((rows, d), F32), ((rows, d), BF)]
        return call(functools.partial(unit_kernel, places), 0, shapes)(*args, w_gu, w_dn, deps=deps)

    def grow(places, *args, deps=()):
        return call(functools.partial(grow_kernel, places), 1, [((wide, d), F32), ((2 * wide, d), F32)], limit=12)(idx, *args, deps=deps)

    at_own, at_up, at_far, at_diag = (0, 0, 0, 0), (0, 0, 0, rows), (0, 0, 0, 2 * rows), (0, 0, rows, rows)
    own_rows, up_rows, far_rows = (normed, pack, cot, cot_near), (nm_up, nm_up2, cot_up, pack), (nm_far, nm_far2, cot_far, pack)
    diag_rows = (diag_rows, diag_rows2, diag_rows, diag_rows2)
    own = unit(at_own, *own_rows)
    sums = grow(at_own, *own[:2], *own_rows)
    up = unit(at_up, *up_rows, deps=(sums[0],))
    far = unit(at_far, *far_rows, deps=(up[0],))
    diag = unit(at_diag, *diag_rows, deps=(far[0],))
    d_near2, d_up2, d_far2, d_diag2 = (swap(v[3], "c") for v in (own, up, far, diag))
    early = add_pairs([(up[2], d_up2), (far[2], d_far2), (diag[2], d_diag2)], deps=(d_near2,))
    d_up, d_far, d_diag = hop(early[0], 1), swap(early[1], "x"), corner(early[2])
    sums = grow(at_up, *up[:2], *up_rows, *sums, deps=early)
    sums = grow(at_far, *far[:2], *far_rows, *sums)
    shapes = [((2 * ff8, 2 * shard), BF)] * 2 + [((ff8, 2 * shard), BF)] * 2
    y1_send, y1_keep, y2_send, y2_keep = call(functools.partial(last_kernel, ff8, at_diag), 1, shapes)(idx, *diag[:2], *diag_rows, *sums)
    y1_there = swap(y1_send, "y")
    dresid, dattn, dmixed, v_m = call(middle_kernel, 1, [((rows, d), F32), ((rows, d), BF), ((rows, QW), BF), ((8, d), F32)])(
        idx, own[2], d_near2, d_far, d_up, d_diag, resid, cotangent, *w_os, deps=(y1_there,)
    )

    def home(value, flip, m):
        pairs = []
        for i in range(32):
            xx, cc, zz, yy = i // 16, i // 8 % 2, i // 2 % 4, i % 2
            pairs.append((i, ((yy * 2 + (zz // 2 ^ m)) * 4 + 2 * (xx ^ flip) + cc) * 2 + zz % 2))
        return lax.ppermute(value, ("x", "c", "z", "y"), pairs)

    go_send, go_keep = call(outer_out_kernel, 1, [((2, QW, shard), BF)] * 2)(idx, mixed, dattn)
    go_there = swap(go_send, "c")
    f1_b, f1_a = call(halves_kernel, 0, [((2 * ff8, shard), BF)] * 2)(y1_keep, y1_there, deps=(go_send,))
    f1_a, f1_b = home(f1_a, 0, 0), swap(f1_b, "x")
    y2_there = swap(through((y2_send,), (go_send,))[0], "y")
    dlat, p_send, p_keep, dq, ups = call(
        attend_back_kernel,
        1,
        [((keys, n_lat), BF)] + [((4 * rows, n_lat + 2 * HD), BF)] * 2 + [((rows, QW), BF), ((4, 8, HD, LAT_HEAD), BF)],
        [((HEADS * rows, keys), BF), ((HEADS * rows, LAT_HEAD), BF), ((HEADS * rows, LAT_HEAD), BF)],
        limit=40,
        far_in=range(1, 8),
    )(idx, dmixed, queries, lat_all, w_key, w_value, probs, outs, qs, deps=(y1_there, go_send))
    tall = HD + n_lat // 8 + 16
    e_q, b_send, b_keep = call(
        bundle_kernel,
        1,
        [((rows, d), F32), ((2, 8, tall, shard), BF), ((2, 8, tall, shard), BF)],
        [((n_lat, d), BF), ((16, d), BF)],
        limit=24,
        far_in=(1, 2, 4),
    )(idx, dlat, na_all, w_lat_t, dq, w_q, ups, v_m)
    f2_a, go_own, cross = call(eleventh_kernel, 0, [((ff8, shard), BF), ((QW, shard), BF), ((ff8 + QW, shard), BF)])(
        y2_keep, y2_there, go_keep, go_there, deps=(b_send, f1_a)
    )
    f1_b, b_send, p_send = through((f1_b, b_send, p_send), (cross,))
    p_there = swap(p_send, "y")
    f2_a, f1_b2 = home(f2_a, 0, 0), home(f1_b, 1, 1)
    cross, b_there = swap(cross, "x"), swap(b_send, "c")
    shapes = [((rows, n_lat + 4 * HD), BF)] * 4 + [((QW, shard), BF)] + [((8, tall, shard), BF)] * 2 + [((ff8, shard), BF)]
    p0, p1, p2, p3, go_all, b_own, b_sum, f2_b = call(exchange_kernel, 0, shapes)(
        p_keep, p_there, go_own, cross, b_keep, b_there, deps=(f2_a, f1_b2)
    )
    pieces = (p0, hop(p1, 1), hop(p2, 2), hop(p3, 3))
    b_far = swap(b_sum, "x")
    o_there = swap(call(stack_kernel, 0, [((4 * rows, d), BF)])(*[v[5] for v in (own, up, far, diag)], deps=(b_sum,))[0], "c")
    flat = ((4 * (tall + rows), shard), BF)
    yz_send, yz_keep = call(later_kernel, 0, [flat] * 2)(b_own, b_far, go_all, deps=pieces[1:])
    gq_send, gq_keep = call(outer_query_kernel, 1, [((2, shard, 2 * HD), BF)] * 2, [((d, 2 * HD), BF)], far_in=(0,))(idx, na_all, *pieces, deps=(yz_send,))
    o_own, o_up, o_far, o_diag = call(outputs_kernel, 0, [((rows, d), F32)] + [((rows, d), BF)] * 3)(
        *[v[4] for v in (own, up, far, diag)], o_there, deps=(yz_send,)
    )
    f2_b2 = home(through((f2_b,), (yz_send,))[0], 1, 1)
    yz_there, gq_there = swap(yz_send, "y"), swap(gq_send, "c")
    o_up, o_far, o_diag = hop(o_up, 1), swap(o_far, "x"), corner(o_diag)
    tokens_grad = call(tokens_kernel, 0, [((rows, d), BF)])(*pieces, e_q, w_lat_t, tokens, dresid, deps=(o_own,))[0]
    shapes = [((tall + rows, shard), BF)] * 4 + [((shard, 2 * HD), BF)] * 2
    z0, z1, z2, z3, gq_own, gq_sum = call(functools.partial(quarters_kernel, rows), 0, shapes)(
        yz_keep, yz_there, gq_keep, gq_there, deps=(tokens_grad, o_up, o_far, o_diag)
    )
    last = z0.astype(F32) + hop(z1, 1) + hop(z2, 2) + hop(z3, 3)
    gq_far = swap(gq_sum, "x")

    grad_query = plus(gq_own, gq_far) * gain_a
    output = (resid + o_own + o_up + o_far + o_diag).astype(BF)
    grad_down = plus(f1_a[:ff8], f1_b2[:ff8])
    grad_gate = plus(f1_a[ff8:], f1_b2[ff8:]).T * gain_m
    grad_up = plus(f2_a, f2_b2).T * gain_m
    grad_out = last[tall:]
    eighth = HD // 2
    n_small = n_lat // 8
    grad_key_up = last[:eighth].T
    grad_value_up = last[eighth:HD].T
    grad_latent = last[HD : HD + n_small].T * gain_a
    own_gain = shard // 8
    pair = lax.dynamic_slice(last, (HD + n_small, s * own_gain), (2, own_gain))
    grad_attn_gain = pair[0] / lax.dynamic_slice_in_dim(gain_a[:, 0], s * own_gain, own_gain)
    grad_mlp_gain = pair[1] / lax.dynamic_slice_in_dim(gain_m[:, 0], s * own_gain, own_gain)
    return (
        output,
        tokens_grad,
        grad_attn_gain,
        grad_query,
        grad_latent,
        grad_key_up,
        grad_value_up,
        grad_out,
        grad_mlp_gain,
        grad_gate,
        grad_up,
        grad_down,
    )


def fast_solution(mesh):
    mesh = Mesh(mesh.devices.reshape(2, 2, 4, 2), ("x", "c", "z", "y"))
    f, s = ("x", "c"), ("z", "y")
    a = f + s
    in_specs = (P(a, None), P(f), P(f, None), P(f, None), P(None, f), P(None, f), P(f, None), P(f), P(f, None), P(f, None), P(f, None), P(f, None), P(a, None))
    out_specs = (P(a, None), P(a, None), P(a), P(f, s), P(f, s), P(None, a), P(None, a), P(s, f), P(a), P(f, s), P(f, s), P(s, f))
    return jax.shard_map(fast_body, mesh=mesh, in_specs=in_specs, out_specs=out_specs, check_vma=False)


def solution(mesh):
    if mesh.shape["fsdp"] == 4 and mesh.shape["seq"] == 8:
        return fast_solution(mesh)
    in_specs = (
        P(("fsdp", "seq"), None),
        P("fsdp"),
        P("fsdp", None),
        P("fsdp", None),
        P(None, "fsdp"),
        P(None, "fsdp"),
        P("fsdp", None),
        P("fsdp"),
        P("fsdp", None),
        P("fsdp", None),
        P("fsdp", None),
        P("fsdp", None),
        P(("fsdp", "seq"), None),
    )
    out_specs = (
        P(("fsdp", "seq"), None),
        P(("fsdp", "seq"), None),
        P(("fsdp", "seq")),
        P("fsdp", "seq"),
        P("fsdp", "seq"),
        P(None, ("fsdp", "seq")),
        P(None, ("fsdp", "seq")),
        P("seq", "fsdp"),
        P(("fsdp", "seq")),
        P("fsdp", "seq"),
        P("fsdp", "seq"),
        P("seq", "fsdp"),
    )
    return jax.shard_map(body, mesh=mesh, in_specs=in_specs, out_specs=out_specs, check_vma=False)
```

```python
import functools

import jax
import jax.numpy as jnp
from jax import lax
from jax.experimental import pallas as pl
from jax.experimental.pallas import tpu as pltpu
from jax.sharding import Mesh
from jax.sharding import PartitionSpec as P

HEADS = 16
HD = 64
GROUPS = 2
LAT_HEAD = 256
KEYBLK = 1024
QW = 1024
GQ = 8


epsilon = 1e-06


def normalize(values, gain):
    return values * lax.rsqrt(jnp.mean(values * values, axis=-1, keepdims=True) + epsilon) * gain


def doc_numbers(lengths_row, count):
    bounds = jnp.cumsum(lengths_row)
    places = jnp.arange(count, dtype=jnp.int32)
    return jnp.sum((places[:, None] >= bounds[None, :-1]).astype(jnp.int32), axis=1)


def contract_rows(left, right):
    return lax.dot_general(
        left, right, (((0,), (0,)), ((), ())), preferred_element_type=jnp.float32
    )


def contract_cols(left, right):
    return lax.dot_general(
        left, right, (((1,), (1,)), ((), ())), preferred_element_type=jnp.float32
    )


def split_parts(values):
    upper = values.astype(jnp.bfloat16)
    lower = (values - upper.astype(jnp.float32)).astype(jnp.bfloat16)
    return (upper, lower)


def gated_unit(gate_pre, upward):
    return jax.nn.silu(gate_pre) * upward


def body(
    tokens,
    attn_gain,
    w_query,
    w_latent,
    w_key_up,
    w_value_up,
    w_out,
    mlp_gain,
    w_gate,
    w_up,
    w_down,
    lengths,
    cotangent,
):
    attn_gain, w_query, w_latent, w_key_up, w_value_up, w_out, mlp_gain, w_gate, w_up, w_down = (
        lax.all_gather(attn_gain, "fsdp", axis=0, tiled=True),
        lax.all_gather(w_query, "fsdp", axis=0, tiled=True),
        lax.all_gather(w_latent, "fsdp", axis=0, tiled=True),
        lax.all_gather(w_key_up, "fsdp", axis=1, tiled=True),
        lax.all_gather(w_value_up, "fsdp", axis=1, tiled=True),
        lax.all_gather(w_out, "fsdp", axis=0, tiled=True),
        lax.all_gather(mlp_gain, "fsdp", axis=0, tiled=True),
        lax.all_gather(w_gate, "fsdp", axis=0, tiled=True),
        lax.all_gather(w_up, "fsdp", axis=0, tiled=True),
        lax.all_gather(w_down, "fsdp", axis=0, tiled=True),
    )
    row_count = tokens.shape[0]
    seq_rank = lax.axis_index("seq")
    stream_len = row_count * lax.axis_size("seq")
    head_width = GQ * HD
    doc_ids = doc_numbers(lengths[0], stream_len)
    row_start = seq_rank * row_count
    own_docs = lax.dynamic_slice_in_dim(doc_ids, row_start, row_count)
    own_places = row_start + jnp.arange(row_count, dtype=jnp.int32)
    block_count = (row_start + row_count - 1) // KEYBLK + 1
    tokens_f = tokens.astype(jnp.float32)
    gain_a = attn_gain.astype(jnp.float32)
    gain_m = mlp_gain.astype(jnp.float32)
    normed = normalize(tokens_f, gain_a).astype(jnp.bfloat16)
    queries = jnp.dot(normed, w_query, preferred_element_type=jnp.float32).astype(jnp.bfloat16)
    latent = jnp.dot(normed, w_latent, preferred_element_type=jnp.float32).astype(jnp.bfloat16)
    gathered = lax.all_gather(latent, "seq", axis=0, tiled=True)
    query_heads = queries.reshape(row_count, HEADS, HD)

    def key_block(source, block_idx, group_idx, with_values):
        latent_part = lax.dynamic_slice(
            source, (block_idx * KEYBLK, group_idx * LAT_HEAD), (KEYBLK, LAT_HEAD)
        )
        low_col = group_idx * head_width
        key_rows = (
            jnp.dot(
                latent_part,
                w_key_up[:, low_col : low_col + head_width],
                preferred_element_type=jnp.float32,
            )
            .astype(jnp.bfloat16)
            .reshape(KEYBLK, GQ, HD)
        )
        value_rows = None
        if with_values:
            value_rows = (
                jnp.dot(
                    latent_part,
                    w_value_up[:, low_col : low_col + head_width],
                    preferred_element_type=jnp.float32,
                )
                .astype(jnp.bfloat16)
                .reshape(KEYBLK, GQ, HD)
            )
        key_docs = lax.dynamic_slice_in_dim(doc_ids, block_idx * KEYBLK, KEYBLK)
        key_places = block_idx * KEYBLK + jnp.arange(KEYBLK, dtype=jnp.int32)
        allowed = (own_docs[:, None] == key_docs[None, :]) & (
            own_places[:, None] >= key_places[None, :]
        )
        return (latent_part, key_rows, value_rows, allowed)

    def block_scores(group_idx, key_rows):
        group_query = query_heads[:, group_idx * GQ : (group_idx + 1) * GQ]
        return (
            jnp.einsum("qhd,khd->hqk", group_query, key_rows, preferred_element_type=jnp.float32)
            * 0.125
        )

    def first_pass(block_idx, carried):
        row_max, row_total = carried
        max_list = []
        total_list = []
        for group_idx in range(GROUPS):
            _, key_rows, _, allowed = key_block(gathered, block_idx, group_idx, False)
            masked = jnp.where(allowed[None], block_scores(group_idx, key_rows), -1e30)
            old_max = row_max[group_idx * GQ : (group_idx + 1) * GQ]
            new_max = jnp.maximum(old_max, jnp.max(masked, axis=-1))
            row_mass = jnp.sum(
                jnp.where(allowed[None], jnp.exp(masked - new_max[:, :, None]), 0.0), axis=-1
            )
            max_list.append(new_max)
            total_list.append(
                row_total[group_idx * GQ : (group_idx + 1) * GQ] * jnp.exp(old_max - new_max)
                + row_mass
            )
        return (jnp.concatenate(max_list, axis=0), jnp.concatenate(total_list, axis=0))

    start_max = jnp.full((HEADS, row_count), -1e30, jnp.float32)
    start_total = jnp.zeros((HEADS, row_count), jnp.float32)
    row_max, row_total = lax.fori_loop(0, block_count, first_pass, (start_max, start_total))
    logsum = row_max + jnp.log(row_total)

    def block_probs(group_idx, key_rows, allowed):
        group_logsum = logsum[group_idx * GQ : (group_idx + 1) * GQ]
        return jnp.where(
            allowed[None],
            jnp.exp(block_scores(group_idx, key_rows) - group_logsum[:, :, None]),
            0.0,
        )

    def second_pass(block_idx, carried):
        rounded_sum, exact_sum = carried
        rounded_list = []
        exact_list = []
        for group_idx in range(GROUPS):
            _, key_rows, value_rows, allowed = key_block(gathered, block_idx, group_idx, True)
            attn_probs = block_probs(group_idx, key_rows, allowed)
            probs_upper, probs_lower = split_parts(attn_probs)
            rounded_part = jnp.einsum(
                "hqk,khd->qhd", probs_upper, value_rows, preferred_element_type=jnp.float32
            )
            rounded_list.append(rounded_part)
            exact_list.append(
                rounded_part
                + jnp.einsum(
                    "hqk,khd->qhd", probs_lower, value_rows, preferred_element_type=jnp.float32
                )
            )
        return (
            rounded_sum + jnp.concatenate(rounded_list, axis=1),
            exact_sum + jnp.concatenate(exact_list, axis=1),
        )

    head_zeros = jnp.zeros((row_count, HEADS, HD), jnp.float32)
    rounded_sum, exact_sum = lax.fori_loop(0, block_count, second_pass, (head_zeros, head_zeros))
    mixed = rounded_sum.reshape(row_count, QW).astype(jnp.bfloat16)
    resid = tokens_f + jnp.dot(mixed, w_out, preferred_element_type=jnp.float32)
    normed_m = normalize(resid, gain_m).astype(jnp.bfloat16)
    gate_pre = jnp.dot(normed_m, w_gate, preferred_element_type=jnp.float32)
    upward = jnp.dot(normed_m, w_up, preferred_element_type=jnp.float32)
    hidden = gated_unit(gate_pre, upward).astype(jnp.bfloat16)
    output = (resid + jnp.dot(hidden, w_down, preferred_element_type=jnp.float32)).astype(
        jnp.bfloat16
    )
    dhidden = contract_cols(cotangent, w_down).astype(jnp.bfloat16)
    _, pull_unit = jax.vjp(gated_unit, gate_pre, upward)
    dgate, dupward = pull_unit(dhidden.astype(jnp.float32))
    dgate = dgate.astype(jnp.bfloat16)
    dupward = dupward.astype(jnp.bfloat16)
    dnormed_m = contract_cols(dgate, w_gate) + contract_cols(dupward, w_up)
    _, pull_norm_m = jax.vjp(normalize, resid, gain_m)
    dresid_norm, grad_mlp_gain = pull_norm_m(dnormed_m)
    dresid = cotangent.astype(jnp.float32) + dresid_norm
    dattn = dresid.astype(jnp.bfloat16)
    dmixed = contract_cols(dattn, w_out).astype(jnp.bfloat16)
    grad_heads = dmixed.reshape(row_count, HEADS, HD)
    row_delta = jnp.einsum("qhd,qhd->hq", grad_heads.astype(jnp.float32), exact_sum)
    source = gathered

    def backward_pass(block_idx, carried):
        dqueries, dlatent, grad_ku, grad_vu = carried
        query_list = []
        fresh_latent = []
        for group_idx in range(GROUPS):
            latent_part, key_rows, value_rows, allowed = key_block(
                source, block_idx, group_idx, True
            )
            low_col = group_idx * head_width
            group_query = query_heads[:, group_idx * GQ : (group_idx + 1) * GQ]
            group_grad = grad_heads[:, group_idx * GQ : (group_idx + 1) * GQ]
            attn_probs = block_probs(group_idx, key_rows, allowed)
            prob_grad = jnp.einsum(
                "qhd,khd->hqk", group_grad, value_rows, preferred_element_type=jnp.float32
            )
            group_delta = row_delta[group_idx * GQ : (group_idx + 1) * GQ]
            score_grad = (attn_probs * (prob_grad - group_delta[:, :, None])).astype(jnp.bfloat16)
            query_list.append(
                jnp.einsum("hqk,khd->qhd", score_grad, key_rows, preferred_element_type=jnp.float32)
                * 0.125
            )
            key_grad = (
                jnp.einsum(
                    "hqk,qhd->khd", score_grad, group_query, preferred_element_type=jnp.float32
                )
                * 0.125
            ).reshape(KEYBLK, head_width)
            value_grad = jnp.einsum(
                "hqk,qhd->khd",
                attn_probs.astype(jnp.bfloat16),
                group_grad,
                preferred_element_type=jnp.float32,
            ).reshape(KEYBLK, head_width)
            key_upper, key_lower = split_parts(key_grad)
            value_upper, value_lower = split_parts(value_grad)
            key_weight = w_key_up[:, low_col : low_col + head_width]
            value_weight = w_value_up[:, low_col : low_col + head_width]
            latent_grad = (
                contract_cols(key_upper, key_weight)
                + contract_cols(key_lower, key_weight)
                + contract_cols(value_upper, value_weight)
                + contract_cols(value_lower, value_weight)
            )
            fresh_latent.append(
                lax.dynamic_update_slice_in_dim(
                    dlatent[group_idx], latent_grad, block_idx * KEYBLK, 0
                )
            )
            grad_ku = grad_ku.at[:, low_col : low_col + head_width].add(
                contract_rows(latent_part, key_upper) + contract_rows(latent_part, key_lower)
            )
            grad_vu = grad_vu.at[:, low_col : low_col + head_width].add(
                contract_rows(latent_part, value_upper) + contract_rows(latent_part, value_lower)
            )
        return (
            dqueries + jnp.concatenate(query_list, axis=1),
            tuple(fresh_latent),
            grad_ku,
            grad_vu,
        )

    latent_zeros = tuple(
        (jnp.zeros((stream_len, LAT_HEAD), jnp.float32) for group_idx in range(GROUPS))
    )
    weight_zeros = jnp.zeros((LAT_HEAD, QW), jnp.float32)
    dqueries, dlatent, grad_key_up, grad_value_up = lax.fori_loop(
        0, block_count, backward_pass, (head_zeros, latent_zeros, weight_zeros, weight_zeros)
    )
    dqueries = dqueries.reshape(row_count, QW).astype(jnp.bfloat16)
    shares = (
        lax.psum_scatter(dlatent[0], "seq", scatter_dimension=0, tiled=True),
        lax.psum_scatter(dlatent[1], "seq", scatter_dimension=0, tiled=True),
    )
    dlatent_own = jnp.concatenate(shares, axis=1).astype(jnp.bfloat16)
    dnormed = contract_cols(dqueries, w_query) + contract_cols(dlatent_own, w_latent)
    _, pull_norm_a = jax.vjp(normalize, tokens_f, gain_a)
    dtokens_norm, grad_attn_gain = pull_norm_a(dnormed)
    tokens_grad = (dresid + dtokens_norm).astype(jnp.bfloat16)
    normed_all, normed_m_all, cotangent_all, dattn_all = (
        lax.all_gather(normed, "seq", axis=0, tiled=True),
        lax.all_gather(normed_m, "seq", axis=0, tiled=True),
        lax.all_gather(cotangent, "seq", axis=0, tiled=True),
        lax.all_gather(dattn, "seq", axis=0, tiled=True),
    )
    hidden_cols, dgate_cols, dupward_cols, mixed_cols, dquery_cols, dlatent_cols = (
        lax.all_to_all(hidden, "seq", split_axis=1, concat_axis=0, tiled=True),
        lax.all_to_all(dgate, "seq", split_axis=1, concat_axis=0, tiled=True),
        lax.all_to_all(dupward, "seq", split_axis=1, concat_axis=0, tiled=True),
        lax.all_to_all(mixed, "seq", split_axis=1, concat_axis=0, tiled=True),
        lax.all_to_all(dqueries, "seq", split_axis=1, concat_axis=0, tiled=True),
        lax.all_to_all(dlatent_own, "seq", split_axis=1, concat_axis=0, tiled=True),
    )
    part_query = contract_rows(normed_all, dquery_cols)
    part_latent = contract_rows(normed_all, dlatent_cols)
    part_out = contract_rows(mixed_cols, dattn_all)
    part_gate = contract_rows(normed_m_all, dgate_cols)
    part_up = contract_rows(normed_m_all, dupward_cols)
    part_down = contract_rows(hidden_cols, cotangent_all)
    grad_query, grad_latent, grad_out, grad_gate, grad_up, grad_down = (
        lax.psum_scatter(
            part_query.astype(jnp.bfloat16), "fsdp", scatter_dimension=0, tiled=True
        ).astype(jnp.float32),
        lax.psum_scatter(
            part_latent.astype(jnp.bfloat16), "fsdp", scatter_dimension=0, tiled=True
        ).astype(jnp.float32),
        lax.psum_scatter(
            part_out.astype(jnp.bfloat16), "fsdp", scatter_dimension=1, tiled=True
        ).astype(jnp.float32),
        lax.psum_scatter(
            part_gate.astype(jnp.bfloat16), "fsdp", scatter_dimension=0, tiled=True
        ).astype(jnp.float32),
        lax.psum_scatter(
            part_up.astype(jnp.bfloat16), "fsdp", scatter_dimension=0, tiled=True
        ).astype(jnp.float32),
        lax.psum_scatter(
            part_down.astype(jnp.bfloat16), "fsdp", scatter_dimension=1, tiled=True
        ).astype(jnp.float32),
    )
    small_sent = (
        lax.psum_scatter(grad_attn_gain, ("fsdp", "seq"), scatter_dimension=0, tiled=True),
        lax.psum_scatter(grad_key_up, ("fsdp", "seq"), scatter_dimension=1, tiled=True),
        lax.psum_scatter(grad_value_up, ("fsdp", "seq"), scatter_dimension=1, tiled=True),
        lax.psum_scatter(grad_mlp_gain, ("fsdp", "seq"), scatter_dimension=0, tiled=True),
    )
    return (
        output,
        tokens_grad,
        small_sent[0],
        grad_query,
        grad_latent,
        small_sent[1],
        small_sent[2],
        grad_out,
        small_sent[3],
        grad_gate,
        grad_up,
        grad_down,
    )


BF = jnp.bfloat16
F32 = jnp.float32
NEG = -1e30
SCALE = 0.125
RING = (0, 2, 4, 6, 7, 5, 3, 1)
MIB = 2**20

FS, ZS, Y0, Y1, ZH0, ZH1, ZL, ROW0, BLOCK, X0, X1 = 8, 12, 16, 17, 18, 19, 20, 21, 22, 23, 24


def dot_nn(left, right):
    return lax.dot_general(left, right, (((1,), (0,)), ((), ())), preferred_element_type=F32)


def fold(total):
    return lax.rsqrt(jnp.mean(total * total, axis=-1, keepdims=True) + epsilon)


def at(index, size):
    return pl.ds(pl.multiple_of(index * size, size), size)


class Lazy:
    def __init__(self, ref, copy):
        self.ref, self.copy, self.shape = ref, copy, ref.shape

    def __getitem__(self, index):
        if self.copy is not None:
            self.copy.wait()
            self.copy = None
        return self.ref[index]


class Late:
    def __init__(self, ref, out, sem):
        self.ref, self.out, self.sem, self.shape, self.copy = ref, out, sem, ref.shape, None

    def __getitem__(self, index):
        return self.ref[index]

    def __setitem__(self, index, value):
        self.ref[index] = value

    def flush(self):
        self.copy = pltpu.make_async_copy(self.ref, self.out, self.sem)
        self.copy.start()


def call(kernel, n_smem, outs, scratch=(), limit=16, flops=1, far_in=(), far_out=()):
    far_in, far_out = tuple(far_in), tuple(far_out)
    n_out, n_far = len(outs), len(far_in) + len(far_out)

    def run(*args, deps=()):
        n_in = len(args) - n_smem

        def body(*refs):
            smem, ins, results = refs[:n_smem], list(refs[n_smem : n_smem + n_in]), list(refs[n_smem + n_in + len(deps) : n_smem + n_in + len(deps) + n_out])
            rest = refs[n_smem + n_in + len(deps) + n_out :]
            sems = rest[-1]
            far, own = rest[len(scratch) : len(scratch) + n_far], rest[: len(scratch)]
            for k, i in enumerate(far_in):
                copy = pltpu.make_async_copy(ins[i], far[k], sems.at[k])
                copy.start()
                ins[i] = Lazy(far[k], copy)
            late = []
            for k, i in enumerate(far_out):
                results[i] = Late(far[len(far_in) + k], results[i], sems.at[len(far_in) + k])
                late.append(results[i])
            kernel(*smem, *ins, *results, *own)
            for i in far_in:
                if ins[i].copy is not None:
                    ins[i].copy.wait()
            for v in late:
                if v.copy is None:
                    v.flush()
            for v in late:
                v.copy.wait()

        spec = lambda i, far: pl.BlockSpec(memory_space=pl.ANY if i in far else pltpu.VMEM)
        shapes = [pltpu.VMEM(shape, dtype) for shape, dtype in scratch]
        shapes += [pltpu.VMEM(args[n_smem + i].shape, args[n_smem + i].dtype) for i in far_in]
        shapes += [pltpu.VMEM(*outs[i]) for i in far_out]
        return pl.pallas_call(
            body,
            in_specs=[pl.BlockSpec(memory_space=pltpu.SMEM)] * n_smem + [spec(i, far_in) for i in range(n_in)] + [pl.BlockSpec(memory_space=pl.ANY)] * len(deps),
            out_specs=[spec(i, far_out) for i in range(n_out)],
            out_shape=[jax.ShapeDtypeStruct(shape, dtype) for shape, dtype in outs],
            scratch_shapes=shapes + [pltpu.SemaphoreType.DMA((max(1, n_far),))],
            compiler_params=pltpu.CompilerParams(vmem_limit_bytes=limit * MIB),
            cost_estimate=pl.CostEstimate(flops=flops, bytes_accessed=0, transcendentals=0),
        )(*args, *deps)

    return run


def attend_kernel(idx, lens, *refs):
    tok, wl, wb = refs[0:8], refs[8:12], refs[12:18]
    mixed_ref, probs_ref, out_ref, qs_ref, q_ref, na_ref, lat_ref, wq_ref, wk_ref, wv_ref, wlt_ref, bias_ref = refs[18:30]
    rows, d = tok[0].shape
    keys = 8 * rows
    part = wl[0].shape[0]
    width = GQ * rows
    for k in range(4):
        here = at(idx[FS + k], part)
        wlt_ref[:, here] = wl[k][...].T
        if k < 2:
            wq_ref[here, :] = wb[k][:, 0:QW]
            wk_ref[:, here] = wb[k][:, QW : QW + LAT_HEAD]
            wv_ref[:, here] = wb[k][:, QW + LAT_HEAD : QW + 2 * LAT_HEAD]
        else:
            first, second = wb[2 * k - 2], wb[2 * k - 1]
            cut = first.shape[1]
            wq_ref[here, 0:cut] = first[...]
            wq_ref[here, cut:QW] = second[:, 0 : QW - cut]
            wk_ref[:, here] = second[:, QW - cut : QW - cut + LAT_HEAD]
            wv_ref[:, here] = second[:, QW - cut + LAT_HEAD : QW - cut + 2 * LAT_HEAD]
    for i in range(8):
        values = tok[i][...].astype(F32)
        normed = (values * fold(values)).astype(BF)
        na_ref[at(idx[i], rows), :] = normed
        if i == 0:
            q_ref[...] = dot_nn(normed, wq_ref[...]).astype(BF)
    lat_ref[...] = contract_cols(na_ref[...], wlt_ref[...]).astype(BF)
    for ref in (wq_ref, wk_ref, wv_ref, wlt_ref, q_ref, na_ref, lat_ref):
        ref.flush()
    place = lax.broadcasted_iota(jnp.int32, (rows, keys), 1)
    own = idx[ROW0] + lax.broadcasted_iota(jnp.int32, (rows, keys), 0)
    first = jnp.zeros((rows, keys), jnp.int32)
    edge = 0
    for i in range(lens.shape[1] - 1):
        edge = edge + lens[0, i]
        first = jnp.where(own >= edge, edge, first)
    bias = jnp.where((place >= first) & (place <= own), 0.0, NEG)
    bias_ref[0:rows, :] = bias
    bias_ref[rows : 2 * rows, :] = bias
    low = lax.broadcasted_iota(jnp.int32, (rows, 2 * HD), 1) < HD
    for p in range(HEADS // 2):
        cols = slice(p * 2 * HD, (p + 1) * 2 * HD)
        q = q_ref[:, cols]
        none = jnp.zeros_like(q)
        for j, own_q in enumerate((jnp.where(low, q, none), jnp.where(low, none, q))):
            qs_ref[(2 * p + j) * rows : (2 * p + j + 1) * rows, :] = (contract_cols(own_q, wk_ref[:, cols]) * SCALE).astype(BF)
    for g in range(GROUPS):
        lat = lat_ref[:, g * LAT_HEAD : (g + 1) * LAT_HEAD]
        for r in range(0, width, 2 * rows):
            band = slice(g * width + r, g * width + r + 2 * rows)
            scores = contract_cols(qs_ref[band, :], lat) + bias_ref[...]
            mass = jnp.exp(scores - jnp.max(scores, axis=-1, keepdims=True))
            probs_ref[band, :] = (mass * (1.0 / jnp.sum(mass, axis=-1, keepdims=True))).astype(BF)
        band = slice(g * width, (g + 1) * width)
        out_ref[band, :] = dot_nn(probs_ref[band, :], lat).astype(BF)
    for ref in (probs_ref, qs_ref, out_ref):
        ref.flush()
    for p in range(HEADS // 2):
        cols = slice(p * 2 * HD, (p + 1) * 2 * HD)
        a, b = (dot_nn(out_ref[(2 * p + j) * rows : (2 * p + j + 1) * rows, :], wv_ref[:, cols]) for j in range(2))
        mixed_ref[:, cols] = jnp.where(low, a, b).astype(BF)


def attend(idx, lens, blocks, w_lats, w_bigs, deps=()):
    rows, d = blocks[0].shape
    keys, n_lat = 8 * rows, GROUPS * LAT_HEAD
    outs = [(rows, QW), (HEADS * rows, keys), (HEADS * rows, LAT_HEAD), (HEADS * rows, LAT_HEAD), (rows, QW)]
    outs += [(keys, d), (keys, n_lat), (d, QW), (LAT_HEAD, QW), (LAT_HEAD, QW), (n_lat, d)]
    macs = 2 * HEADS * rows * keys * LAT_HEAD + keys * d * n_lat
    return call(
        attend_kernel, 2, [(v, BF) for v in outs], [((2 * rows, keys), F32)], limit=60,
        far_in=range(18), far_out=range(1, 11),
    )(
        idx, lens, *blocks, *w_lats, *w_bigs, deps=deps
    )


def project_kernel(idx, mixed, tok, *refs):
    parts, (cot_up, cot_far, cot_diag, gu_c, resid_ref, normed_ref, pack_ref) = refs[:4], refs[4:]
    total = tok[...].astype(F32)
    for k, w in enumerate(parts):
        total = total + dot_nn(mixed[:, at(idx[FS + k], w.shape[0])], w[...])
    resid_ref[...] = total
    normed = (total * fold(total)).astype(BF)
    normed_ref[...] = normed
    rows = normed.shape[0]
    pack_ref[0:rows, :] = normed
    for i, ref in enumerate((cot_up, cot_far, cot_diag)):
        pack_ref[(i + 1) * rows : (i + 2) * rows, :] = ref[...]
    n = gu_c.shape[0] // 2
    pack_ref[4 * rows :, 0 : gu_c.shape[1]] = gu_c[n:, :]
    pack_ref[4 * rows :, gu_c.shape[1] :] = jnp.zeros((n, pack_ref.shape[1] - gu_c.shape[1]), BF)


def columns_kernel(idx, gate_ref, up_ref, gain_ref, own_ref, near_ref, pair_ref, all_ref):
    gain = gain_ref[...].astype(F32)
    n, rows, two = all_ref.shape
    cols = gate_ref.shape[1] // n
    gap = jnp.zeros((rows, two // 2 - cols), BF)
    for j in range(n):
        for part, ref in enumerate((gate_ref, up_ref)):
            block = (ref[:, j * cols : (j + 1) * cols].astype(F32) * gain).astype(BF)
            all_ref[j, :, part * (two // 2) : (part + 1) * (two // 2)] = jnp.concatenate([block, gap], axis=1)
    own_ref[...] = all_ref[idx[BLOCK]]
    near_ref[...] = all_ref[idx[BLOCK] ^ 4]
    pair_ref[0:rows, :] = own_ref[...]
    pair_ref[rows:, :] = near_ref[...]


def assemble_kernel(idx, own, near, far, pack, down, gu_ref, dn_ref):
    part, n = own.shape
    for k, w in enumerate((own[...], near[...], far[0:part, :], pack[-part:, 0:n])):
        gu_ref[at(idx[FS + k], part), :] = w
    n = down.shape[0]
    dn_ref[0:n, :] = down[...]
    dn_ref[n:, :] = jnp.zeros((dn_ref.shape[0] - n, dn_ref.shape[1]), BF)


def rows_of(ref, where, rows):
    return ref[where : where + rows, :]


def unit_kernel(places, n0, n1, c0, c1, w_gu, w_dn, hid_ref, both_ref, dkeep, okeep, send):
    rows = dkeep.shape[0]
    wide = w_dn.shape[0]
    n0, n1, c0, c1 = (rows_of(ref, p, rows) for ref, p in zip((n0, n1, c0, c1), places))
    both = dot_nn(jnp.concatenate([n0, n1], 0), w_gu[...])
    gate, upward = both[:, :wide], both[:, wide:]
    dhid = contract_cols(jnp.concatenate([c0, c1], 0), w_dn[...]).astype(BF).astype(F32)
    sig = jax.nn.sigmoid(gate)
    act = gate * sig
    hid = (act * upward).astype(BF)
    hid_ref[...] = hid
    both_ref[:, :wide] = (dhid * upward * sig * (1.0 + gate * (1.0 - sig))).astype(BF)
    both_ref[:, wide:] = (dhid * act).astype(BF)
    dn = contract_cols(both_ref[...], w_gu[...])
    dkeep[...] = dn[:rows]
    send[0:rows, :] = dn[rows:].astype(BF)
    out = dot_nn(hid, w_dn[...])
    okeep[...] = out[:rows]
    send[rows:, :] = out[rows:].astype(BF)


def relative_columns(idx, shard):
    return [at(2 * idx[xx] + idx[zz], shard) for xx in (X1, X0) for zz in (ZH1, ZH0)]


def grow_kernel(places, idx, hid, both, n0, n1, c0, c1, *refs):
    down_ref, gu_ref = refs[-2:]
    shard = n0.shape[1] // 4
    rows = hid.shape[0] // 2
    for j, cols in enumerate(relative_columns(idx, shard)):
        here = slice(j * shard, (j + 1) * shard)
        v0, v1, t0, t1 = (ref[p : p + rows, cols] for ref, p in zip((n0, n1, c0, c1), places))
        down = contract_rows(hid[...], jnp.concatenate([t0, t1], 0))
        gu = contract_rows(both[...], jnp.concatenate([v0, v1], 0))
        if len(refs) == 4:
            down, gu = down + refs[0][:, here], gu + refs[1][:, here]
        down_ref[:, here] = down
        gu_ref[:, here] = gu


def last_kernel(ff8, places, idx, hid, both, n0, n1, c0, c1, down_ref, gu_ref, send1, keep1, send2, keep2):
    shard = n0.shape[1] // 4
    rows = hid.shape[0] // 2
    wide = (ff8 + 127) // 128 * 128
    for j, cols in enumerate(relative_columns(idx, shard)):
        here = slice(j * shard, (j + 1) * shard)
        there = slice(j % 2 * shard, (j % 2 + 1) * shard)
        v0, v1, t0, t1 = (ref[p : p + rows, cols] for ref, p in zip((n0, n1, c0, c1), places))
        down = down_ref[:, here] + contract_rows(hid[...], jnp.concatenate([t0, t1], 0))
        gu = gu_ref[:, here] + contract_rows(both[...], jnp.concatenate([v0, v1], 0))
        one, two = (send1, send2) if j < 2 else (keep1, keep2)
        one[0:ff8, there] = down[0:ff8].astype(BF)
        one[ff8:, there] = gu[0:ff8].astype(BF)
        two[:, there] = gu[wide : wide + ff8].astype(BF)


def middle_kernel(idx, e_own, far, up, diag, resid_ref, cot, *refs):
    parts, (dresid_ref, dattn_ref, dmixed_ref, sum_ref) = refs[:4], refs[4:]
    e = e_own[...]
    for v in (far, up, diag):
        e = e + v[...].astype(F32)
    resid = resid_ref[...]
    rms = fold(resid)
    n = resid * rms
    en = e * n
    dresid = cot[...].astype(F32) + rms * (e - n * jnp.mean(en, axis=-1, keepdims=True))
    dresid_ref[...] = dresid
    dattn = dresid.astype(BF)
    dattn_ref[...] = dattn
    sum_ref[...] = jnp.broadcast_to(jnp.sum(en, axis=0, keepdims=True), sum_ref.shape)
    for k, w in enumerate(parts):
        dmixed_ref[:, at(idx[FS + k], w.shape[0])] = contract_cols(dattn, w[...]).astype(BF)


def outer_out_kernel(idx, mixed, dattn, send, keep):
    rows = mixed.shape[0]
    shard = send.shape[2]
    for out, ks in ((send, (1, 3)), (keep, (0, 2))):
        for i, k in enumerate(ks):
            right = dattn[:, at(idx[FS + k], shard)]
            for j, yy in enumerate((Y1, Y0)):
                for kz in range(4):
                    left = mixed[:, at(2 * idx[ZS + kz] + idx[yy], rows)]
                    out[i, (4 * j + kz) * rows : (4 * j + kz + 1) * rows, :] = contract_rows(left, right).astype(BF)


def attend_back_kernel(idx, dm_ref, q_ref, lat_ref, wk_ref, wv_ref, probs_ref, out_ref, qs_ref, dlat_ref, send, keep, dq_ref, up_ref, ds_ref, do_ref, dqs_ref):
    rows = dm_ref.shape[0]
    width = GQ * rows
    half = HD // 2
    low = lax.broadcasted_iota(jnp.int32, (rows, 2 * HD), 1) < HD
    for p in range(HEADS // 2):
        cols = slice(p * 2 * HD, (p + 1) * 2 * HD)
        dm = dm_ref[:, cols]
        none = jnp.zeros_like(dm)
        for j, own in enumerate((jnp.where(low, dm, none), jnp.where(low, none, dm))):
            do_ref[(2 * p + j) * rows : (2 * p + j + 1) * rows, :] = contract_cols(own, wv_ref[:, cols]).astype(BF)
    for g in range(GROUPS):
        lat = lat_ref[:, g * LAT_HEAD : (g + 1) * LAT_HEAD]
        for r in range(0, width, 2 * rows):
            band = slice(g * width + r, g * width + r + 2 * rows)
            do = do_ref[band, :]
            delta = jnp.sum(do.astype(F32) * out_ref[band, :].astype(F32), axis=-1, keepdims=True)
            ds_ref[band, :] = (probs_ref[band, :].astype(F32) * (contract_cols(do, lat) - delta)).astype(BF)
        band = slice(g * width, (g + 1) * width)
        dlat_ref[:, g * LAT_HEAD : (g + 1) * LAT_HEAD] = (
            contract_rows(ds_ref[band, :], qs_ref[band, :]) + contract_rows(probs_ref[band, :], do_ref[band, :])
        ).astype(BF)
        dqs_ref[band, :] = (dot_nn(ds_ref[band, :], lat) * SCALE).astype(BF)
    for p in range(HEADS // 2):
        cols = slice(p * 2 * HD, (p + 1) * 2 * HD)
        bands = [slice((2 * p + j) * rows, (2 * p + j + 1) * rows) for j in range(2)]
        a, b = (dot_nn(dqs_ref[band, :], wk_ref[:, cols]) for band in bands)
        dq_ref[:, cols] = jnp.where(low, a, b).astype(BF)
        f, s = divmod(4 * p, 8)
        for j, band in enumerate(bands):
            gk = contract_rows(q_ref[:, cols], dqs_ref[band, :]).astype(BF)
            gv = contract_rows(dm_ref[:, cols], out_ref[band, :]).astype(BF)
            for i in range(2):
                piece = slice((2 * j + i) * half, (2 * j + i + 1) * half)
                up_ref[f, s + 2 * j + i, 0:half, :] = gk[piece, :]
                up_ref[f, s + 2 * j + i, half:HD, :] = gv[piece, :]
    for k in range(4):
        for out, yy in ((send, Y1), (keep, Y0)):
            block = 2 * idx[ZS + k] + idx[yy]
            n = dlat_ref.shape[1]
            out[k * rows : (k + 1) * rows, 0:n] = dlat_ref[at(block, rows), :]
            out[k * rows : (k + 1) * rows, n:] = dq_ref[:, at(block, 2 * HD)]


def bundle_kernel(idx, dlat, na, wlt, dq, wq, ups, sum_ref, e_ref, send, keep, part_ref, sums_ref):
    rows = dq.shape[0]
    e = contract_cols(dq[...], wq[...])
    e_ref[...] = e
    total = jnp.sum(na[at(idx[ROW0] // rows, rows), :].astype(F32) * e, axis=0, keepdims=True)
    for g in range(GROUPS):
        band = slice(g * LAT_HEAD, (g + 1) * LAT_HEAD)
        part = contract_rows(dlat[:, band], na[...])
        part_ref[band, :] = part.astype(BF)
        total = total + jnp.sum(part * wlt[band, :].astype(F32), axis=0, keepdims=True)
    line = lax.broadcasted_iota(jnp.int32, (16, total.shape[1]), 0)
    sums_ref[...] = jnp.where(line == 0, total, jnp.where(line == 1, sum_ref[0:1, :], 0.0)).astype(BF)
    shard = send.shape[3]
    n_lat = part_ref.shape[0] // 8
    for out, ks in ((send, (1, 3)), (keep, (0, 2))):
        for i, k in enumerate(ks):
            cols = at(idx[FS + k], shard)
            for j, yy in enumerate((Y1, Y0)):
                for kz in range(4):
                    s = 2 * idx[ZS + kz] + idx[yy]
                    out[i, 4 * j + kz, 0:HD, :] = ups[idx[FS + k], s]
                    out[i, 4 * j + kz, HD : HD + n_lat, :] = part_ref[at(s, n_lat), cols]
                    out[i, 4 * j + kz, HD + n_lat :, :] = sums_ref[:, cols]


def outer_query_kernel(idx, na, p0, p1, p2, p3, own, near, far, diag, total_ref):
    rows = p0.shape[0]
    wide = 2 * HD
    total = None
    for k, piece in enumerate((p0, p1, p2, p3)):
        first = p0.shape[1] - 2 * wide
        for j, yy in enumerate((Y0, Y1)):
            right = piece[:, first + j * wide : first + (j + 1) * wide]
            term = contract_rows(na[at(2 * idx[ZS + k] + idx[yy], rows), :], right)
            total = term if total is None else total + term
    total_ref[...] = total.astype(BF)
    for k, out in enumerate((own, near, far, diag)):
        out[...] = total_ref[at(idx[FS + k], out.shape[0]), :]


def tokens_kernel(p0, p1, p2, p3, e_ref, wlt, tok, dresid, out_ref):
    n = wlt.shape[0]
    dlat = wide_sum(p0[:, 0:n], p1[:, 0:n]) + wide_sum(p2[:, 0:n], p3[:, 0:n])
    e = e_ref[...] + dot_nn(dlat.astype(BF), wlt[...])
    values = tok[...].astype(F32)
    rms = fold(values)
    n = values * rms
    out_ref[...] = (dresid[...] + rms * (e - n * jnp.mean(e * n, axis=-1, keepdims=True))).astype(BF)


def wide_sum(left, right):
    return left.astype(F32) + right.astype(F32)


def pass_kernel(*refs):
    pass


def half_kernel(both, second):
    second[...] = both[second.shape[0] :, :]


def through(values, deps):
    n = len(values)
    return pl.pallas_call(
        pass_kernel,
        in_specs=[pl.BlockSpec(memory_space=pl.ANY)] * (n + len(deps)),
        out_specs=[pl.BlockSpec(memory_space=pl.ANY)] * n,
        out_shape=[jax.ShapeDtypeStruct(v.shape, v.dtype) for v in values],
        input_output_aliases={i: i for i in range(n)},
        compiler_params=pltpu.CompilerParams(vmem_limit_bytes=MIB),
    )(*values, *deps)


def rows_kernel(*refs):
    keeps, theres, (e0, e1, e2, e3, o0, o_up, o_x) = refs[0:8], refs[8:12], refs[12:19]
    rows = e0.shape[0]
    for i, e in enumerate((e0, e1, e2, e3)):
        e[...] = wide_sum(keeps[i][...], theres[i][0:rows, :]).astype(e.dtype)
    sums = [wide_sum(keeps[4 + i][...], theres[i][rows:, :]) for i in range(4)]
    o0[...] = sums[0]
    o_up[...] = sums[1]
    o_x[0:rows, :] = sums[2].astype(BF)
    o_x[rows:, :] = sums[3].astype(BF)


def halves_kernel(*refs):
    n = len(refs) // 4
    for i in range(n):
        total = wide_sum(refs[2 * i][...], refs[2 * i + 1][...]).astype(BF)
        first, second = refs[2 * n + 2 * i : 2 * n + 2 * i + 2]
        cut = first.shape[1]
        first[...] = total[:, :cut]
        second[...] = total[:, cut:]


def two_kernel(keep, there, own, far):
    own[...] = wide_sum(keep[0], there[0]).astype(BF)
    far[...] = wide_sum(keep[1], there[1]).astype(BF)


def eleventh_kernel(up_keep, up_there, go_keep, go_there, up_b, up_a, go_own, go_far):
    halves_kernel(up_keep, up_there, up_b, up_a)
    go_own[...] = wide_sum(go_keep[0], go_there[0]).astype(BF)
    go_far[...] = wide_sum(go_keep[1], go_there[1]).astype(BF)


def exchange_kernel(keep, there, go_own, go_far, b_keep, b_there, o_up, o_x, p0, p1, p2, p3, b_x, b_xy, y_send, y_keep):
    rows, wide = p0.shape
    n = wide - 4 * HD
    for k, out in enumerate((p0, p1, p2, p3)):
        band = slice(k * rows, (k + 1) * rows)
        out[:, 0:n] = wide_sum(keep[band, 0:n], there[band, 0:n]).astype(BF)
        out[:, n : n + 2 * HD] = keep[band, n:]
        out[:, n + 2 * HD : wide] = there[band, n:]
    p1[:, wide:] = wide_sum(o_up[...], o_x[rows:, :]).astype(BF)
    tall = b_keep.shape[2]
    for j in range(8):
        band = slice(j % 4 * tall, (j % 4 + 1) * tall)
        (y_send, y_keep)[j // 4][band, :] = wide_sum(b_keep[0, j], b_there[0, j]).astype(BF)
        (b_xy, b_x)[j // 4][band, :] = wide_sum(b_keep[1, j], b_there[1, j]).astype(BF)
    half = go_own.shape[0] // 2
    for i, out in enumerate((y_send, y_keep)):
        band = slice(i * half, (i + 1) * half)
        out[4 * tall :, :] = wide_sum(go_own[band, :], go_far[band, :]).astype(BF)


def quarters_kernel(rows, keep, y_there, x_there, xy_there, z0, z1, z2, z3):
    tall = z0.shape[0] - rows
    for k, out in enumerate((z0, z1, z2, z3)):
        band = slice(k * tall, (k + 1) * tall)
        out[0:tall, :] = (wide_sum(keep[band, :], y_there[band, :]) + wide_sum(x_there[band, :], xy_there[band, :])).astype(BF)
        band = slice(4 * tall + k * rows, 4 * tall + (k + 1) * rows)
        out[tall:, :] = wide_sum(keep[band, :], y_there[band, :]).astype(BF)


def swap(value, axis):
    return lax.ppermute(value, axis, [(0, 1), (1, 0)])


def hop(value, k):
    return lax.ppermute(value, "z", [(i, i ^ k) for i in range(4)])


def corner(value):
    return lax.ppermute(value, ("z", "y"), [(i, i ^ 3) for i in range(8)])


def plus(left, right):
    return left.astype(F32) + right.astype(F32)


def fast_body(tokens, attn_gain, w_query, w_latent, w_key_up, w_value_up, w_out, mlp_gain, w_gate, w_up, w_down, lengths, cotangent):
    x, c, z, y = (lax.axis_index(a) for a in ("x", "c", "z", "y"))
    f, s, zl, zh = 2 * x + c, 2 * z + y, lax.rem(z, 2), z // 2
    rows, d = tokens.shape
    shard = d // 4
    half = shard // 2
    ff8 = w_gate.shape[1] // 8
    wide = (ff8 + 127) // 128 * 128
    n_lat = GROUPS * LAT_HEAD
    keys = 8 * rows

    cw = [(RING[i], RING[(i + 1) % 8]) for i in range(8)]
    ccw = [(b, a) for a, b in cw]
    place = jnp.where(y == 0, z, 7 - z)

    def owner(p):
        p = lax.rem(p + 8, 8)
        return jnp.where(p < 4, 2 * p, 15 - 2 * p)

    def ring(value, pairs):
        return lax.ppermute(value, ("z", "y"), pairs)

    def fold_into(gain, weight):
        return (weight.astype(F32) * gain).astype(BF)

    owners = [s, owner(place - 1), owner(place + 1), owner(place - 2), owner(place + 2), owner(place - 3), owner(place + 3), owner(place - 4)]
    idx = jnp.stack(owners + [f, f ^ 1, f ^ 2, f ^ 3, z, z ^ 1, z ^ 2, z ^ 3, y, y ^ 1, zh, zh ^ 1, zl, s * rows, 4 * c + 2 * zl + y, x, x ^ 1]).astype(jnp.int32)
    gain_a = attn_gain.astype(F32)[:, None]
    gain_m = mlp_gain.astype(F32)[:, None]

    a1, b1 = ring(tokens, cw), ring(tokens, ccw)
    wl_own = fold_into(gain_a, w_latent)
    wl_far, wl_near = swap(wl_own, "x"), swap(wl_own, "c")
    cut = QW * 3 // 4
    a1, b1 = through((a1, b1), (wl_far,))
    a2, b2 = ring(a1, cw), ring(b1, ccw)
    wl_diag = swap(wl_far, "c")
    wb_own = jnp.concatenate([fold_into(gain_a, w_query), w_key_up, w_value_up], axis=1)
    wb_own, wb_a, wb_b = through((wb_own, wb_own[:, :cut], wb_own[:, cut:]), (a1,))
    wb_near, wb_far = swap(wb_own, "c"), [swap(wb_a, "x")]
    gu_own, gu_near, gu_far = call(columns_kernel, 1, [((shard, 2 * wide), BF)] * 2 + [((2 * shard, 2 * wide), BF)], [((8, shard, 2 * wide), BF)], limit=16)(
        idx, w_gate, w_up, mlp_gain[:, None], deps=(a1,)
    )
    gu_near = swap(gu_near, "c")
    a2, b2 = through((a2, b2), (wb_far[0], gu_own))
    a3, b3 = ring(a2, cw), ring(b2, ccw)
    wo_own = through((w_out,), (a2,))[0]
    wo_far, wo_near = swap(wo_own, "x"), swap(wo_own, "c")
    a3, wb_b = through((a3, wb_b), (b3, wo_far, gu_near))
    a4 = ring(a3, cw)
    wb_far.append(swap(wb_b, "x"))
    wb_diag, wo_diag = [swap(v, "c") for v in wb_far], swap(wo_far, "c")

    a4, gu_far, cot, down_rows = through((a4, gu_far, cotangent, lax.dynamic_slice_in_dim(w_down, y * ff8, ff8, 0)), (wb_far[1], wo_diag))
    gu_far = swap(gu_far, "x")
    pairs = []
    for i in range(16):
        xx, cc, zz = i // 8, i // 4 % 2, i % 4
        pairs.append(((2 * cc + zz % 2) * 4 + zz - zz % 2 + xx, i))
    down_rows = lax.ppermute(down_rows, ("x", "c", "z"), pairs)
    cot_far, cot_up, cot_near, cot_diag = swap(cot, "y"), hop(cot, 1), swap(cot, "c"), corner(cot)
    mixed, probs, outs, qs, queries, na_all, lat_all, w_q, w_key, w_value, w_lat_t = attend(
        idx, lengths, (tokens, a1, b1, a2, b2, a3, b3, a4), (wl_own, wl_near, wl_far, wl_diag), (wb_own, wb_near, *wb_far, *wb_diag)
    )
    w_os = (w_out, wo_near, wo_far, wo_diag)
    resid, normed, pack = call(project_kernel, 1, [((rows, d), F32), ((rows, d), BF), ((4 * rows + shard, d), BF)])(
        idx, mixed, tokens, *w_os, cot_up, cot_far, cot_diag, gu_far, deps=(down_rows,)
    )

    pack = swap(pack, "c")
    nm_far, nm_up, nm_diag = swap(normed, "y"), hop(normed, 1), corner(normed)
    nm_up2, nm_far2, nm_diag2 = swap(nm_up, "c"), swap(nm_far, "c"), swap(nm_diag, "c")
    w_gu, w_dn = call(assemble_kernel, 1, [((d, 2 * wide), BF), ((wide, d), BF)])(
        idx, gu_own, gu_near, gu_far, pack, down_rows, deps=(nm_far, nm_up, nm_diag)
    )

    def unit(places, *args, deps=()):
        shapes = [((2 * rows, wide), BF), ((2 * rows, 2 * wide), BF), ((rows, d), F32), ((rows, d), F32), ((2 * rows, d), BF)]
        return call(functools.partial(unit_kernel, places), 0, shapes)(*args, w_gu, w_dn, deps=deps)

    def grow(places, *args, deps=()):
        return call(functools.partial(grow_kernel, places), 1, [((wide, d), F32), ((2 * wide, d), F32)], limit=12)(idx, *args, deps=deps)

    at_own, at_up, at_far, at_diag = (0, 0, 0, 0), (0, 0, 0, rows), (0, 0, 0, 2 * rows), (0, 0, 0, 3 * rows)
    own_rows, up_rows, far_rows = (normed, pack, cot, cot_near), (nm_up, nm_up2, cot_up, pack), (nm_far, nm_far2, cot_far, pack)
    diag_rows = (nm_diag, nm_diag2, cot_diag, pack)
    own = unit(at_own, *own_rows)
    sums = grow(at_own, *own[:2], *own_rows)
    up = unit(at_up, *up_rows, deps=(sums[0],))
    far = unit(at_far, *far_rows, deps=(up[0],))
    diag = unit(at_diag, *diag_rows, deps=(far[0],))
    near2, up2, far2, diag2 = (swap(v[4], "c") for v in (own, up, far, diag))
    units = (own, up, far, diag)
    shapes = [((rows, d), F32)] + [((rows, d), BF)] * 3 + [((rows, d), F32)] * 2 + [((2 * rows, d), BF)]
    e_own, *early, o_own, o_up, o_x = call(rows_kernel, 0, shapes)(*[v[2] for v in units], *[v[3] for v in units], near2, up2, far2, diag2)
    d_up, d_far, d_diag = hop(early[0], 1), swap(early[1], "y"), corner(early[2])
    sums = grow(at_up, *up[:2], *up_rows, *sums, deps=early)
    sums = grow(at_far, *far[:2], *far_rows, *sums)
    shapes = [((2 * ff8, 2 * shard), BF)] * 2 + [((ff8, 2 * shard), BF)] * 2
    y1_send, y1_keep, y2_send, y2_keep = call(functools.partial(last_kernel, ff8, at_diag), 1, shapes)(idx, *diag[:2], *diag_rows, *sums)
    y1_there = swap(y1_send, "x")
    dresid, dattn, dmixed, v_m = call(middle_kernel, 1, [((rows, d), F32), ((rows, d), BF), ((rows, QW), BF), ((8, d), F32)])(
        idx, e_own, d_far, d_up, d_diag, resid, cotangent, *w_os, deps=(y1_there,)
    )

    def home(value, m):
        pairs = []
        for i in range(8):
            cc, hh, ll = i // 4, i // 2 % 2, i % 2
            pairs.append((i, (hh ^ m) * 4 + 2 * cc + ll))
        return lax.ppermute(value, ("c", "z"), pairs)

    go_send, go_keep = call(outer_out_kernel, 1, [((2, QW, shard), BF)] * 2)(idx, mixed, dattn)
    go_there = swap(go_send, "c")
    f1_b, f1_a = call(halves_kernel, 0, [((2 * ff8, shard), BF)] * 2)(y1_keep, y1_there, deps=(go_send,))
    f1_a, f1_b = home(f1_a, 0), home(f1_b, 1)
    o_x = swap(through((o_x,), (go_send,))[0], "y")
    y2_there = swap(through((y2_send,), (go_send,))[0], "x")
    dlat, p_send, p_keep, dq, ups = call(
        attend_back_kernel,
        1,
        [((keys, n_lat), BF)] + [((4 * rows, n_lat + 2 * HD), BF)] * 2 + [((rows, QW), BF), ((4, 8, HD, LAT_HEAD), BF)],
        [((HEADS * rows, keys), BF), ((HEADS * rows, LAT_HEAD), BF), ((HEADS * rows, LAT_HEAD), BF)],
        limit=40,
        far_in=range(1, 8),
    )(idx, dmixed, queries, lat_all, w_key, w_value, probs, outs, qs, deps=(y1_there, go_send))
    tall = HD + n_lat // 8 + 16
    e_q, b_send, b_keep = call(
        bundle_kernel,
        1,
        [((rows, d), F32), ((2, 8, tall, shard), BF), ((2, 8, tall, shard), BF)],
        [((n_lat, d), BF), ((16, d), BF)],
        limit=24,
        far_in=(1, 2, 4),
    )(idx, dlat, na_all, w_lat_t, dq, w_q, ups, v_m)
    f2_b, f2_a, go_own, go_far = call(eleventh_kernel, 0, [((ff8, shard), BF)] * 2 + [((QW, shard), BF)] * 2)(
        y2_keep, y2_there, go_keep, go_there, deps=(b_send, f1_a, f1_b, o_x)
    )
    b_send, p_send = through((b_send, p_send), (go_far,))
    p_there = swap(p_send, "y")
    f2_a, f2_b = home(f2_a, 0), home(f2_b, 1)
    go_far, b_there = swap(go_far, "x"), swap(b_send, "c")
    flat = ((4 * tall, shard), BF)
    tower = ((4 * tall + QW // 2, shard), BF)
    n_p = n_lat + 4 * HD
    shapes = [((rows, n), BF) for n in (n_p, n_p + d, n_p, n_p)] + [flat, flat, tower, tower]
    p0, p1, p2, p3, b_x, b_xy, y_send, y_keep = call(exchange_kernel, 0, shapes)(
        p_keep, p_there, go_own, go_far, b_keep, b_there, o_up, o_x, deps=(f2_a, f2_b)
    )
    pieces = (p0, hop(p1, 1), hop(p2, 2), hop(p3, 3))
    b_x, y_there = swap(b_x, "x"), swap(y_send, "y")
    b_xy = lax.ppermute(b_xy, ("x", "y"), [(i, i ^ 3) for i in range(4)])
    z0, z1, z2, z3 = call(functools.partial(quarters_kernel, rows), 0, [((tall + rows, shard), BF)] * 4)(
        y_keep, y_there, b_x, b_xy, deps=pieces[1:]
    )
    last = z0.astype(F32) + hop(z1, 1) + hop(z2, 2) + hop(z3, 3)
    gq, gq_near, gq_far, gq_diag = call(outer_query_kernel, 1, [((shard, 2 * HD), BF)] * 4, [((d, 2 * HD), BF)], far_in=(0,))(
        idx, na_all, *pieces, deps=(z0,)
    )
    gq_near, gq_far, gq_diag = swap(gq_near, "c"), swap(gq_far, "x"), lax.ppermute(gq_diag, ("x", "c"), [(i, i ^ 3) for i in range(4)])
    tokens_grad = call(tokens_kernel, 0, [((rows, d), BF)])(*pieces, e_q, w_lat_t, tokens, dresid, deps=(gq,))[0]
    grad_query = (plus(gq, gq_near) + plus(gq_far, gq_diag)) * gain_a
    output = (resid + o_own + o_x[:rows] + pieces[1][:, n_p:]).astype(BF)
    grad_down = plus(f1_a[:ff8], f1_b[:ff8])
    grad_gate = plus(f1_a[ff8:], f1_b[ff8:]).T * gain_m
    grad_up = plus(f2_a, f2_b).T * gain_m
    grad_out = last[tall:]
    eighth = HD // 2
    n_small = n_lat // 8
    grad_key_up = last[:eighth].T
    grad_value_up = last[eighth:HD].T
    grad_latent = last[HD : HD + n_small].T * gain_a
    own_gain = shard // 8
    pair = lax.dynamic_slice(last, (HD + n_small, s * own_gain), (2, own_gain))
    grad_attn_gain = pair[0] / lax.dynamic_slice_in_dim(gain_a[:, 0], s * own_gain, own_gain)
    grad_mlp_gain = pair[1] / lax.dynamic_slice_in_dim(gain_m[:, 0], s * own_gain, own_gain)
    return (
        output,
        tokens_grad,
        grad_attn_gain,
        grad_query,
        grad_latent,
        grad_key_up,
        grad_value_up,
        grad_out,
        grad_mlp_gain,
        grad_gate,
        grad_up,
        grad_down,
    )


def fast_solution(mesh):
    mesh = Mesh(mesh.devices.reshape(2, 2, 4, 2), ("x", "c", "z", "y"))
    f, s = ("x", "c"), ("z", "y")
    a = f + s
    in_specs = (P(a, None), P(f), P(f, None), P(f, None), P(None, f), P(None, f), P(f, None), P(f), P(f, None), P(f, None), P(f, None), P(f, None), P(a, None))
    out_specs = (P(a, None), P(a, None), P(a), P(f, s), P(f, s), P(None, a), P(None, a), P(s, f), P(a), P(f, s), P(f, s), P(s, f))
    return jax.shard_map(fast_body, mesh=mesh, in_specs=in_specs, out_specs=out_specs, check_vma=False)


def solution(mesh):
    if mesh.shape["fsdp"] == 4 and mesh.shape["seq"] == 8:
        return fast_solution(mesh)
    in_specs = (
        P(("fsdp", "seq"), None),
        P("fsdp"),
        P("fsdp", None),
        P("fsdp", None),
        P(None, "fsdp"),
        P(None, "fsdp"),
        P("fsdp", None),
        P("fsdp"),
        P("fsdp", None),
        P("fsdp", None),
        P("fsdp", None),
        P("fsdp", None),
        P(("fsdp", "seq"), None),
    )
    out_specs = (
        P(("fsdp", "seq"), None),
        P(("fsdp", "seq"), None),
        P(("fsdp", "seq")),
        P("fsdp", "seq"),
        P("fsdp", "seq"),
        P(None, ("fsdp", "seq")),
        P(None, ("fsdp", "seq")),
        P("seq", "fsdp"),
        P(("fsdp", "seq")),
        P("fsdp", "seq"),
        P("fsdp", "seq"),
        P("seq", "fsdp"),
    )
    return jax.shard_map(body, mesh=mesh, in_specs=in_specs, out_specs=out_specs, check_vma=False)
```

```python
import functools

import jax
import jax.numpy as jnp
from jax import lax
from jax.experimental import pallas as pl
from jax.experimental.pallas import tpu as pltpu
from jax.sharding import Mesh
from jax.sharding import PartitionSpec as P

HEADS = 16
HD = 64
GROUPS = 2
LAT_HEAD = 256
KEYBLK = 1024
QW = 1024
GQ = 8


epsilon = 1e-06


def normalize(values, gain):
    return values * lax.rsqrt(jnp.mean(values * values, axis=-1, keepdims=True) + epsilon) * gain


def doc_numbers(lengths_row, count):
    bounds = jnp.cumsum(lengths_row)
    places = jnp.arange(count, dtype=jnp.int32)
    return jnp.sum((places[:, None] >= bounds[None, :-1]).astype(jnp.int32), axis=1)


def contract_rows(left, right):
    return lax.dot_general(
        left, right, (((0,), (0,)), ((), ())), preferred_element_type=jnp.float32
    )


def contract_cols(left, right):
    return lax.dot_general(
        left, right, (((1,), (1,)), ((), ())), preferred_element_type=jnp.float32
    )


def split_parts(values):
    upper = values.astype(jnp.bfloat16)
    lower = (values - upper.astype(jnp.float32)).astype(jnp.bfloat16)
    return (upper, lower)


def gated_unit(gate_pre, upward):
    return jax.nn.silu(gate_pre) * upward


def body(
    tokens,
    attn_gain,
    w_query,
    w_latent,
    w_key_up,
    w_value_up,
    w_out,
    mlp_gain,
    w_gate,
    w_up,
    w_down,
    lengths,
    cotangent,
):
    attn_gain, w_query, w_latent, w_key_up, w_value_up, w_out, mlp_gain, w_gate, w_up, w_down = (
        lax.all_gather(attn_gain, "fsdp", axis=0, tiled=True),
        lax.all_gather(w_query, "fsdp", axis=0, tiled=True),
        lax.all_gather(w_latent, "fsdp", axis=0, tiled=True),
        lax.all_gather(w_key_up, "fsdp", axis=1, tiled=True),
        lax.all_gather(w_value_up, "fsdp", axis=1, tiled=True),
        lax.all_gather(w_out, "fsdp", axis=0, tiled=True),
        lax.all_gather(mlp_gain, "fsdp", axis=0, tiled=True),
        lax.all_gather(w_gate, "fsdp", axis=0, tiled=True),
        lax.all_gather(w_up, "fsdp", axis=0, tiled=True),
        lax.all_gather(w_down, "fsdp", axis=0, tiled=True),
    )
    row_count = tokens.shape[0]
    seq_rank = lax.axis_index("seq")
    stream_len = row_count * lax.axis_size("seq")
    head_width = GQ * HD
    doc_ids = doc_numbers(lengths[0], stream_len)
    row_start = seq_rank * row_count
    own_docs = lax.dynamic_slice_in_dim(doc_ids, row_start, row_count)
    own_places = row_start + jnp.arange(row_count, dtype=jnp.int32)
    block_count = (row_start + row_count - 1) // KEYBLK + 1
    tokens_f = tokens.astype(jnp.float32)
    gain_a = attn_gain.astype(jnp.float32)
    gain_m = mlp_gain.astype(jnp.float32)
    normed = normalize(tokens_f, gain_a).astype(jnp.bfloat16)
    queries = jnp.dot(normed, w_query, preferred_element_type=jnp.float32).astype(jnp.bfloat16)
    latent = jnp.dot(normed, w_latent, preferred_element_type=jnp.float32).astype(jnp.bfloat16)
    gathered = lax.all_gather(latent, "seq", axis=0, tiled=True)
    query_heads = queries.reshape(row_count, HEADS, HD)

    def key_block(source, block_idx, group_idx, with_values):
        latent_part = lax.dynamic_slice(
            source, (block_idx * KEYBLK, group_idx * LAT_HEAD), (KEYBLK, LAT_HEAD)
        )
        low_col = group_idx * head_width
        key_rows = (
            jnp.dot(
                latent_part,
                w_key_up[:, low_col : low_col + head_width],
                preferred_element_type=jnp.float32,
            )
            .astype(jnp.bfloat16)
            .reshape(KEYBLK, GQ, HD)
        )
        value_rows = None
        if with_values:
            value_rows = (
                jnp.dot(
                    latent_part,
                    w_value_up[:, low_col : low_col + head_width],
                    preferred_element_type=jnp.float32,
                )
                .astype(jnp.bfloat16)
                .reshape(KEYBLK, GQ, HD)
            )
        key_docs = lax.dynamic_slice_in_dim(doc_ids, block_idx * KEYBLK, KEYBLK)
        key_places = block_idx * KEYBLK + jnp.arange(KEYBLK, dtype=jnp.int32)
        allowed = (own_docs[:, None] == key_docs[None, :]) & (
            own_places[:, None] >= key_places[None, :]
        )
        return (latent_part, key_rows, value_rows, allowed)

    def block_scores(group_idx, key_rows):
        group_query = query_heads[:, group_idx * GQ : (group_idx + 1) * GQ]
        return (
            jnp.einsum("qhd,khd->hqk", group_query, key_rows, preferred_element_type=jnp.float32)
            * 0.125
        )

    def first_pass(block_idx, carried):
        row_max, row_total = carried
        max_list = []
        total_list = []
        for group_idx in range(GROUPS):
            _, key_rows, _, allowed = key_block(gathered, block_idx, group_idx, False)
            masked = jnp.where(allowed[None], block_scores(group_idx, key_rows), -1e30)
            old_max = row_max[group_idx * GQ : (group_idx + 1) * GQ]
            new_max = jnp.maximum(old_max, jnp.max(masked, axis=-1))
            row_mass = jnp.sum(
                jnp.where(allowed[None], jnp.exp(masked - new_max[:, :, None]), 0.0), axis=-1
            )
            max_list.append(new_max)
            total_list.append(
                row_total[group_idx * GQ : (group_idx + 1) * GQ] * jnp.exp(old_max - new_max)
                + row_mass
            )
        return (jnp.concatenate(max_list, axis=0), jnp.concatenate(total_list, axis=0))

    start_max = jnp.full((HEADS, row_count), -1e30, jnp.float32)
    start_total = jnp.zeros((HEADS, row_count), jnp.float32)
    row_max, row_total = lax.fori_loop(0, block_count, first_pass, (start_max, start_total))
    logsum = row_max + jnp.log(row_total)

    def block_probs(group_idx, key_rows, allowed):
        group_logsum = logsum[group_idx * GQ : (group_idx + 1) * GQ]
        return jnp.where(
            allowed[None],
            jnp.exp(block_scores(group_idx, key_rows) - group_logsum[:, :, None]),
            0.0,
        )

    def second_pass(block_idx, carried):
        rounded_sum, exact_sum = carried
        rounded_list = []
        exact_list = []
        for group_idx in range(GROUPS):
            _, key_rows, value_rows, allowed = key_block(gathered, block_idx, group_idx, True)
            attn_probs = block_probs(group_idx, key_rows, allowed)
            probs_upper, probs_lower = split_parts(attn_probs)
            rounded_part = jnp.einsum(
                "hqk,khd->qhd", probs_upper, value_rows, preferred_element_type=jnp.float32
            )
            rounded_list.append(rounded_part)
            exact_list.append(
                rounded_part
                + jnp.einsum(
                    "hqk,khd->qhd", probs_lower, value_rows, preferred_element_type=jnp.float32
                )
            )
        return (
            rounded_sum + jnp.concatenate(rounded_list, axis=1),
            exact_sum + jnp.concatenate(exact_list, axis=1),
        )

    head_zeros = jnp.zeros((row_count, HEADS, HD), jnp.float32)
    rounded_sum, exact_sum = lax.fori_loop(0, block_count, second_pass, (head_zeros, head_zeros))
    mixed = rounded_sum.reshape(row_count, QW).astype(jnp.bfloat16)
    resid = tokens_f + jnp.dot(mixed, w_out, preferred_element_type=jnp.float32)
    normed_m = normalize(resid, gain_m).astype(jnp.bfloat16)
    gate_pre = jnp.dot(normed_m, w_gate, preferred_element_type=jnp.float32)
    upward = jnp.dot(normed_m, w_up, preferred_element_type=jnp.float32)
    hidden = gated_unit(gate_pre, upward).astype(jnp.bfloat16)
    output = (resid + jnp.dot(hidden, w_down, preferred_element_type=jnp.float32)).astype(
        jnp.bfloat16
    )
    dhidden = contract_cols(cotangent, w_down).astype(jnp.bfloat16)
    _, pull_unit = jax.vjp(gated_unit, gate_pre, upward)
    dgate, dupward = pull_unit(dhidden.astype(jnp.float32))
    dgate = dgate.astype(jnp.bfloat16)
    dupward = dupward.astype(jnp.bfloat16)
    dnormed_m = contract_cols(dgate, w_gate) + contract_cols(dupward, w_up)
    _, pull_norm_m = jax.vjp(normalize, resid, gain_m)
    dresid_norm, grad_mlp_gain = pull_norm_m(dnormed_m)
    dresid = cotangent.astype(jnp.float32) + dresid_norm
    dattn = dresid.astype(jnp.bfloat16)
    dmixed = contract_cols(dattn, w_out).astype(jnp.bfloat16)
    grad_heads = dmixed.reshape(row_count, HEADS, HD)
    row_delta = jnp.einsum("qhd,qhd->hq", grad_heads.astype(jnp.float32), exact_sum)
    source = gathered

    def backward_pass(block_idx, carried):
        dqueries, dlatent, grad_ku, grad_vu = carried
        query_list = []
        fresh_latent = []
        for group_idx in range(GROUPS):
            latent_part, key_rows, value_rows, allowed = key_block(
                source, block_idx, group_idx, True
            )
            low_col = group_idx * head_width
            group_query = query_heads[:, group_idx * GQ : (group_idx + 1) * GQ]
            group_grad = grad_heads[:, group_idx * GQ : (group_idx + 1) * GQ]
            attn_probs = block_probs(group_idx, key_rows, allowed)
            prob_grad = jnp.einsum(
                "qhd,khd->hqk", group_grad, value_rows, preferred_element_type=jnp.float32
            )
            group_delta = row_delta[group_idx * GQ : (group_idx + 1) * GQ]
            score_grad = (attn_probs * (prob_grad - group_delta[:, :, None])).astype(jnp.bfloat16)
            query_list.append(
                jnp.einsum("hqk,khd->qhd", score_grad, key_rows, preferred_element_type=jnp.float32)
                * 0.125
            )
            key_grad = (
                jnp.einsum(
                    "hqk,qhd->khd", score_grad, group_query, preferred_element_type=jnp.float32
                )
                * 0.125
            ).reshape(KEYBLK, head_width)
            value_grad = jnp.einsum(
                "hqk,qhd->khd",
                attn_probs.astype(jnp.bfloat16),
                group_grad,
                preferred_element_type=jnp.float32,
            ).reshape(KEYBLK, head_width)
            key_upper, key_lower = split_parts(key_grad)
            value_upper, value_lower = split_parts(value_grad)
            key_weight = w_key_up[:, low_col : low_col + head_width]
            value_weight = w_value_up[:, low_col : low_col + head_width]
            latent_grad = (
                contract_cols(key_upper, key_weight)
                + contract_cols(key_lower, key_weight)
                + contract_cols(value_upper, value_weight)
                + contract_cols(value_lower, value_weight)
            )
            fresh_latent.append(
                lax.dynamic_update_slice_in_dim(
                    dlatent[group_idx], latent_grad, block_idx * KEYBLK, 0
                )
            )
            grad_ku = grad_ku.at[:, low_col : low_col + head_width].add(
                contract_rows(latent_part, key_upper) + contract_rows(latent_part, key_lower)
            )
            grad_vu = grad_vu.at[:, low_col : low_col + head_width].add(
                contract_rows(latent_part, value_upper) + contract_rows(latent_part, value_lower)
            )
        return (
            dqueries + jnp.concatenate(query_list, axis=1),
            tuple(fresh_latent),
            grad_ku,
            grad_vu,
        )

    latent_zeros = tuple(
        (jnp.zeros((stream_len, LAT_HEAD), jnp.float32) for group_idx in range(GROUPS))
    )
    weight_zeros = jnp.zeros((LAT_HEAD, QW), jnp.float32)
    dqueries, dlatent, grad_key_up, grad_value_up = lax.fori_loop(
        0, block_count, backward_pass, (head_zeros, latent_zeros, weight_zeros, weight_zeros)
    )
    dqueries = dqueries.reshape(row_count, QW).astype(jnp.bfloat16)
    shares = (
        lax.psum_scatter(dlatent[0], "seq", scatter_dimension=0, tiled=True),
        lax.psum_scatter(dlatent[1], "seq", scatter_dimension=0, tiled=True),
    )
    dlatent_own = jnp.concatenate(shares, axis=1).astype(jnp.bfloat16)
    dnormed = contract_cols(dqueries, w_query) + contract_cols(dlatent_own, w_latent)
    _, pull_norm_a = jax.vjp(normalize, tokens_f, gain_a)
    dtokens_norm, grad_attn_gain = pull_norm_a(dnormed)
    tokens_grad = (dresid + dtokens_norm).astype(jnp.bfloat16)
    normed_all, normed_m_all, cotangent_all, dattn_all = (
        lax.all_gather(normed, "seq", axis=0, tiled=True),
        lax.all_gather(normed_m, "seq", axis=0, tiled=True),
        lax.all_gather(cotangent, "seq", axis=0, tiled=True),
        lax.all_gather(dattn, "seq", axis=0, tiled=True),
    )
    hidden_cols, dgate_cols, dupward_cols, mixed_cols, dquery_cols, dlatent_cols = (
        lax.all_to_all(hidden, "seq", split_axis=1, concat_axis=0, tiled=True),
        lax.all_to_all(dgate, "seq", split_axis=1, concat_axis=0, tiled=True),
        lax.all_to_all(dupward, "seq", split_axis=1, concat_axis=0, tiled=True),
        lax.all_to_all(mixed, "seq", split_axis=1, concat_axis=0, tiled=True),
        lax.all_to_all(dqueries, "seq", split_axis=1, concat_axis=0, tiled=True),
        lax.all_to_all(dlatent_own, "seq", split_axis=1, concat_axis=0, tiled=True),
    )
    part_query = contract_rows(normed_all, dquery_cols)
    part_latent = contract_rows(normed_all, dlatent_cols)
    part_out = contract_rows(mixed_cols, dattn_all)
    part_gate = contract_rows(normed_m_all, dgate_cols)
    part_up = contract_rows(normed_m_all, dupward_cols)
    part_down = contract_rows(hidden_cols, cotangent_all)
    grad_query, grad_latent, grad_out, grad_gate, grad_up, grad_down = (
        lax.psum_scatter(
            part_query.astype(jnp.bfloat16), "fsdp", scatter_dimension=0, tiled=True
        ).astype(jnp.float32),
        lax.psum_scatter(
            part_latent.astype(jnp.bfloat16), "fsdp", scatter_dimension=0, tiled=True
        ).astype(jnp.float32),
        lax.psum_scatter(
            part_out.astype(jnp.bfloat16), "fsdp", scatter_dimension=1, tiled=True
        ).astype(jnp.float32),
        lax.psum_scatter(
            part_gate.astype(jnp.bfloat16), "fsdp", scatter_dimension=0, tiled=True
        ).astype(jnp.float32),
        lax.psum_scatter(
            part_up.astype(jnp.bfloat16), "fsdp", scatter_dimension=0, tiled=True
        ).astype(jnp.float32),
        lax.psum_scatter(
            part_down.astype(jnp.bfloat16), "fsdp", scatter_dimension=1, tiled=True
        ).astype(jnp.float32),
    )
    small_sent = (
        lax.psum_scatter(grad_attn_gain, ("fsdp", "seq"), scatter_dimension=0, tiled=True),
        lax.psum_scatter(grad_key_up, ("fsdp", "seq"), scatter_dimension=1, tiled=True),
        lax.psum_scatter(grad_value_up, ("fsdp", "seq"), scatter_dimension=1, tiled=True),
        lax.psum_scatter(grad_mlp_gain, ("fsdp", "seq"), scatter_dimension=0, tiled=True),
    )
    return (
        output,
        tokens_grad,
        small_sent[0],
        grad_query,
        grad_latent,
        small_sent[1],
        small_sent[2],
        grad_out,
        small_sent[3],
        grad_gate,
        grad_up,
        grad_down,
    )


BF = jnp.bfloat16
F32 = jnp.float32
NEG = -1e30
SCALE = 0.125
RING = (0, 2, 4, 6, 7, 5, 3, 1)
MIB = 2**20

FS, ZS, Y0, Y1, ZH0, ZH1, ZL, ROW0, BLOCK, X0, X1, DOWN = 8, 12, 16, 17, 18, 19, 20, 21, 22, 23, 24, 25


def dot_nn(left, right):
    return lax.dot_general(left, right, (((1,), (0,)), ((), ())), preferred_element_type=F32)


def fold(total):
    return lax.rsqrt(jnp.mean(total * total, axis=-1, keepdims=True) + epsilon)


def at(index, size):
    return pl.ds(pl.multiple_of(index * size, size), size)


class Lazy:
    def __init__(self, ref, copy):
        self.ref, self.copy, self.shape = ref, copy, ref.shape

    def __getitem__(self, index):
        if self.copy is not None:
            self.copy.wait()
            self.copy = None
        return self.ref[index]


class Late:
    def __init__(self, ref, out, sems, parts):
        self.ref, self.out, self.sems, self.parts, self.shape, self.copies = ref, out, sems, parts, ref.shape, []

    def __getitem__(self, index):
        return self.ref[index]

    def __setitem__(self, index, value):
        self.ref[index] = value

    def flush(self):
        n = self.shape[0] // self.parts
        band = pl.ds(len(self.copies) * n, n)
        copy = pltpu.make_async_copy(self.ref.at[band], self.out.at[band], self.sems[len(self.copies)])
        copy.start()
        self.copies.append(copy)


def call(kernel, n_smem, outs, scratch=(), limit=16, flops=1, far_in=(), far_out=(), parts=1, split=()):
    far_in, far_out = tuple(far_in), tuple(far_out)
    n_out, n_far, n_sems = len(outs), len(far_in) + len(far_out), len(far_in) + parts * len(far_out)

    def run(*args, deps=()):
        n_in = len(args) - n_smem

        def body(*refs):
            smem, ins, results = refs[:n_smem], list(refs[n_smem : n_smem + n_in]), list(refs[n_smem + n_in + len(deps) : n_smem + n_in + len(deps) + n_out])
            rest = refs[n_smem + n_in + len(deps) + n_out :]
            sems = rest[-1]
            far, own = rest[len(scratch) : len(scratch) + n_far], rest[: len(scratch)]
            for k, i in enumerate(far_in):
                copy = pltpu.make_async_copy(ins[i], far[k], sems.at[k])
                copy.start()
                ins[i] = Lazy(far[k], copy)
            late = []
            for k, i in enumerate(far_out):
                own_sems = [sems.at[len(far_in) + parts * k + p] for p in range(parts)]
                results[i] = Late(far[len(far_in) + k], results[i], own_sems, parts if i in split else 1)
                late.append(results[i])
            kernel(*smem, *ins, *results, *own)
            for i in far_in:
                if ins[i].copy is not None:
                    ins[i].copy.wait()
            for v in late:
                while len(v.copies) < v.parts:
                    v.flush()
            for v in late:
                for copy in v.copies:
                    copy.wait()

        spec = lambda i, far: pl.BlockSpec(memory_space=pl.ANY if i in far else pltpu.VMEM)
        shapes = [pltpu.VMEM(shape, dtype) for shape, dtype in scratch]
        shapes += [pltpu.VMEM(args[n_smem + i].shape, args[n_smem + i].dtype) for i in far_in]
        shapes += [pltpu.VMEM(*outs[i]) for i in far_out]
        return pl.pallas_call(
            body,
            in_specs=[pl.BlockSpec(memory_space=pltpu.SMEM)] * n_smem + [spec(i, far_in) for i in range(n_in)] + [pl.BlockSpec(memory_space=pl.ANY)] * len(deps),
            out_specs=[spec(i, far_out) for i in range(n_out)],
            out_shape=[jax.ShapeDtypeStruct(shape, dtype) for shape, dtype in outs],
            scratch_shapes=shapes + [pltpu.SemaphoreType.DMA((max(1, n_sems),))],
            compiler_params=pltpu.CompilerParams(vmem_limit_bytes=limit * MIB),
            cost_estimate=pl.CostEstimate(flops=flops, bytes_accessed=0, transcendentals=0),
        )(*args, *deps)

    return run


def attend_kernel(idx, lens, *refs):
    tok, wl, wb = refs[0:8], refs[8:12], refs[12:18]
    mixed_ref, probs_ref, out_ref, qs_ref, q_ref, na_ref, lat_ref, wq_ref, wk_ref, wv_ref, wlt_ref, bias_ref = refs[18:30]
    rows, d = tok[0].shape
    keys = 8 * rows
    part = wl[0].shape[0]
    width = GQ * rows
    for i in range(8):
        values = tok[i][...].astype(F32)
        na_ref[at(idx[i], rows), :] = (values * fold(values)).astype(BF)
    na_ref.flush()
    for k in range(4):
        wlt_ref[:, at(idx[FS + k], part)] = wl[k][...].T
    wlt_ref.flush()
    lat_ref[...] = contract_cols(na_ref[...], wlt_ref[...]).astype(BF)
    lat_ref.flush()
    for k in range(4):
        here = at(idx[FS + k], part)
        if k < 2:
            wq_ref[here, :] = wb[k][:, 0:QW]
            wk_ref[:, here] = wb[k][:, QW : QW + LAT_HEAD]
            wv_ref[:, here] = wb[k][:, QW + LAT_HEAD : QW + 2 * LAT_HEAD]
        else:
            first, second = wb[2 * k - 2], wb[2 * k - 1]
            cut = first.shape[1]
            wq_ref[here, 0:cut] = first[...]
            wq_ref[here, cut:QW] = second[:, 0 : QW - cut]
            wk_ref[:, here] = second[:, QW - cut : QW - cut + LAT_HEAD]
            wv_ref[:, here] = second[:, QW - cut + LAT_HEAD : QW - cut + 2 * LAT_HEAD]
    q_ref[...] = dot_nn(na_ref[at(idx[0], rows), :], wq_ref[...]).astype(BF)
    for ref in (wq_ref, wk_ref, wv_ref, q_ref):
        ref.flush()
    place = lax.broadcasted_iota(jnp.int32, (rows, keys), 1)
    own = idx[ROW0] + lax.broadcasted_iota(jnp.int32, (rows, keys), 0)
    first = jnp.zeros((rows, keys), jnp.int32)
    edge = 0
    for i in range(lens.shape[1] - 1):
        edge = edge + lens[0, i]
        first = jnp.where(own >= edge, edge, first)
    bias = jnp.where((place >= first) & (place <= own), 0.0, NEG)
    bias_ref[0:rows, :] = bias
    bias_ref[rows : 2 * rows, :] = bias
    low = lax.broadcasted_iota(jnp.int32, (rows, 2 * HD), 1) < HD
    for p in range(HEADS // 2):
        cols = slice(p * 2 * HD, (p + 1) * 2 * HD)
        q = q_ref[:, cols]
        none = jnp.zeros_like(q)
        for j, own_q in enumerate((jnp.where(low, q, none), jnp.where(low, none, q))):
            qs_ref[(2 * p + j) * rows : (2 * p + j + 1) * rows, :] = (contract_cols(own_q, wk_ref[:, cols]) * SCALE).astype(BF)
    for g in range(GROUPS):
        lat = lat_ref[:, g * LAT_HEAD : (g + 1) * LAT_HEAD]
        for r in range(0, width, 2 * rows):
            band = slice(g * width + r, g * width + r + 2 * rows)
            scores = contract_cols(qs_ref[band, :], lat) + bias_ref[...]
            mass = jnp.exp(scores - jnp.max(scores, axis=-1, keepdims=True))
            probs_ref[band, :] = (mass * (1.0 / jnp.sum(mass, axis=-1, keepdims=True))).astype(BF)
        band = slice(g * width, (g + 1) * width)
        out_ref[band, :] = dot_nn(probs_ref[band, :], lat).astype(BF)
        for ref in (probs_ref, qs_ref, out_ref):
            ref.flush()
    for p in range(HEADS // 2):
        cols = slice(p * 2 * HD, (p + 1) * 2 * HD)
        a, b = (dot_nn(out_ref[(2 * p + j) * rows : (2 * p + j + 1) * rows, :], wv_ref[:, cols]) for j in range(2))
        mixed_ref[:, cols] = jnp.where(low, a, b).astype(BF)


def attend(idx, lens, blocks, w_lats, w_bigs, deps=()):
    rows, d = blocks[0].shape
    keys, n_lat = 8 * rows, GROUPS * LAT_HEAD
    outs = [(rows, QW), (HEADS * rows, keys), (HEADS * rows, LAT_HEAD), (HEADS * rows, LAT_HEAD), (rows, QW)]
    outs += [(keys, d), (keys, n_lat), (d, QW), (LAT_HEAD, QW), (LAT_HEAD, QW), (n_lat, d)]
    macs = 2 * HEADS * rows * keys * LAT_HEAD + keys * d * n_lat
    return call(
        attend_kernel, 2, [(v, BF) for v in outs], [((2 * rows, keys), F32)], limit=60,
        far_in=range(18), far_out=range(1, 11), parts=GROUPS, split=(1, 2, 3),
    )(
        idx, lens, *blocks, *w_lats, *w_bigs, deps=deps
    )


def project_kernel(idx, mixed, tok, *refs):
    parts, (cot_up, cot_far, cot_diag, cot, gu_c, down, resid_ref, normed_ref, pack_ref) = refs[:4], refs[4:]
    total = tok[...].astype(F32)
    for k, w in enumerate(parts):
        total = total + dot_nn(mixed[:, at(idx[FS + k], w.shape[0])], w[...])
    resid_ref[...] = total
    normed = (total * fold(total)).astype(BF)
    normed_ref[...] = normed
    rows = normed.shape[0]
    pack_ref[0:rows, :] = normed
    for i, ref in enumerate((cot_up, cot_far, cot_diag, cot)):
        pack_ref[(i + 1) * rows : (i + 2) * rows, :] = ref[...]
    n = gu_c.shape[0] // 2
    first = 5 * rows
    pack_ref[first : first + n, 0 : gu_c.shape[1]] = gu_c[n:, :]
    pack_ref[first : first + n, gu_c.shape[1] :] = jnp.zeros((n, pack_ref.shape[1] - gu_c.shape[1]), BF)
    pack_ref[first + n :, :] = down[...]


def columns_kernel(idx, gate_ref, up_ref, gain_ref, own_ref, near_ref, pair_ref, all_ref):
    gain = gain_ref[...].astype(F32)
    n, rows, two = all_ref.shape
    cols = gate_ref.shape[1] // n
    gap = jnp.zeros((rows, two // 2 - cols), BF)
    for j in range(n):
        for part, ref in enumerate((gate_ref, up_ref)):
            block = (ref[:, j * cols : (j + 1) * cols].astype(F32) * gain).astype(BF)
            all_ref[j, :, part * (two // 2) : (part + 1) * (two // 2)] = jnp.concatenate([block, gap], axis=1)
    own_ref[...] = all_ref[idx[BLOCK]]
    near_ref[...] = all_ref[idx[BLOCK] ^ 4]
    pair_ref[0:rows, :] = own_ref[...]
    pair_ref[rows:, :] = near_ref[...]


def assemble_kernel(idx, own, near, far, pack, down_x, down, gu_ref, dn_ref, near_ref):
    near_ref[...] = pack[0 : near_ref.shape[0], :]
    part, n = own.shape
    first = pack.shape[0] - down.shape[0]
    for k, w in enumerate((own[...], near[...], far[0:part, :], pack[first - part : first, 0:n])):
        gu_ref[at(idx[FS + k], part), :] = w
    n = down.shape[0]
    for i, ref in enumerate((down_x, pack, down)):

        @pl.when(idx[DOWN] == i)
        def _(ref=ref):
            dn_ref[0:n, :] = ref[-n:, :]

    dn_ref[n:, :] = jnp.zeros((dn_ref.shape[0] - n, dn_ref.shape[1]), BF)


def rows_of(ref, where, rows):
    return ref[where : where + rows, :]


def unit_kernel(places, n0, n1, c0, c1, w_gu, w_dn, hid_ref, both_ref, dkeep, okeep, send):
    rows = dkeep.shape[0]
    wide = w_dn.shape[0]
    n0, n1, c0, c1 = (rows_of(ref, p, rows) for ref, p in zip((n0, n1, c0, c1), places))
    both = dot_nn(jnp.concatenate([n0, n1], 0), w_gu[...])
    gate, upward = both[:, :wide], both[:, wide:]
    dhid = contract_cols(jnp.concatenate([c0, c1], 0), w_dn[...]).astype(BF).astype(F32)
    sig = jax.nn.sigmoid(gate)
    act = gate * sig
    hid = (act * upward).astype(BF)
    hid_ref[...] = hid
    both_ref[:, :wide] = (dhid * upward * sig * (1.0 + gate * (1.0 - sig))).astype(BF)
    both_ref[:, wide:] = (dhid * act).astype(BF)
    dn = contract_cols(both_ref[...], w_gu[...])
    dkeep[...] = dn[:rows]
    send[0:rows, :] = dn[rows:].astype(BF)
    out = dot_nn(hid, w_dn[...])
    okeep[...] = out[:rows]
    send[rows:, :] = out[rows:].astype(BF)


def relative_columns(idx, shard):
    return [at(2 * idx[xx] + idx[zz], shard) for xx in (X1, X0) for zz in (ZH1, ZH0)]


def outer_kernel(ff8, places, idx, *refs):
    hids, boths, blocks, (send1, keep1, send2, keep2) = refs[0:4], refs[4:8], refs[8:24], refs[24:28]
    rows = hids[0].shape[0] // 2
    shard = send1.shape[1] // 2
    wide = (ff8 + 127) // 128 * 128
    hid = jnp.concatenate([ref[...] for ref in hids], 0)
    both = jnp.concatenate([ref[...] for ref in boths], 0)
    for j, cols in enumerate(relative_columns(idx, shard)):
        there = slice(j % 2 * shard, (j % 2 + 1) * shard)
        values = [ref[p : p + rows, cols] for ref, p in zip(blocks, places)]
        normed = jnp.concatenate([v for i in range(4) for v in values[4 * i : 4 * i + 2]], 0)
        cot = jnp.concatenate([v for i in range(4) for v in values[4 * i + 2 : 4 * i + 4]], 0)
        down = contract_rows(hid, cot)
        gu = contract_rows(both, normed)
        one, two = (send1, send2) if j < 2 else (keep1, keep2)
        one[0:ff8, there] = down[0:ff8].astype(BF)
        one[ff8:, there] = gu[0:ff8].astype(BF)
        two[:, there] = gu[wide : wide + ff8].astype(BF)


def middle_kernel(idx, e_own, far, up, diag, resid_ref, cot, *refs):
    parts, (dresid_ref, dattn_ref, dmixed_ref, sum_ref) = refs[:4], refs[4:]
    e = e_own[...]
    for v in (far, up, diag):
        e = e + v[...].astype(F32)
    resid = resid_ref[...]
    rms = fold(resid)
    n = resid * rms
    en = e * n
    dresid = cot[...].astype(F32) + rms * (e - n * jnp.mean(en, axis=-1, keepdims=True))
    dresid_ref[...] = dresid
    dattn = dresid.astype(BF)
    dattn_ref[...] = dattn
    sum_ref[...] = jnp.broadcast_to(jnp.sum(en, axis=0, keepdims=True), sum_ref.shape)
    for k, w in enumerate(parts):
        dmixed_ref[:, at(idx[FS + k], w.shape[0])] = contract_cols(dattn, w[...]).astype(BF)


def outer_out_kernel(idx, mixed, dattn, send, keep):
    rows = mixed.shape[0]
    shard = send.shape[2]
    for out, ks in ((send, (1, 3)), (keep, (0, 2))):
        for i, k in enumerate(ks):
            right = dattn[:, at(idx[FS + k], shard)]
            for j, yy in enumerate((Y1, Y0)):
                for kz in range(4):
                    left = mixed[:, at(2 * idx[ZS + kz] + idx[yy], rows)]
                    out[i, (4 * j + kz) * rows : (4 * j + kz + 1) * rows, :] = contract_rows(left, right).astype(BF)


def attend_back_kernel(idx, dm_ref, q_ref, lat_ref, wk_ref, wv_ref, probs_ref, out_ref, qs_ref, dlat_ref, send, keep, dq_ref, up_ref, ds_ref, do_ref, dqs_ref):
    rows = dm_ref.shape[0]
    width = GQ * rows
    half = HD // 2
    low = lax.broadcasted_iota(jnp.int32, (rows, 2 * HD), 1) < HD
    for p in range(HEADS // 2):
        cols = slice(p * 2 * HD, (p + 1) * 2 * HD)
        dm = dm_ref[:, cols]
        none = jnp.zeros_like(dm)
        for j, own in enumerate((jnp.where(low, dm, none), jnp.where(low, none, dm))):
            do_ref[(2 * p + j) * rows : (2 * p + j + 1) * rows, :] = contract_cols(own, wv_ref[:, cols]).astype(BF)
    for g in range(GROUPS):
        lat = lat_ref[:, g * LAT_HEAD : (g + 1) * LAT_HEAD]
        for r in range(0, width, 2 * rows):
            band = slice(g * width + r, g * width + r + 2 * rows)
            do = do_ref[band, :]
            delta = jnp.sum(do.astype(F32) * out_ref[band, :].astype(F32), axis=-1, keepdims=True)
            ds_ref[band, :] = (probs_ref[band, :].astype(F32) * (contract_cols(do, lat) - delta)).astype(BF)
        band = slice(g * width, (g + 1) * width)
        dlat_ref[:, g * LAT_HEAD : (g + 1) * LAT_HEAD] = (
            contract_rows(ds_ref[band, :], qs_ref[band, :]) + contract_rows(probs_ref[band, :], do_ref[band, :])
        ).astype(BF)
        dqs_ref[band, :] = (dot_nn(ds_ref[band, :], lat) * SCALE).astype(BF)
    for p in range(HEADS // 2):
        cols = slice(p * 2 * HD, (p + 1) * 2 * HD)
        bands = [slice((2 * p + j) * rows, (2 * p + j + 1) * rows) for j in range(2)]
        a, b = (dot_nn(dqs_ref[band, :], wk_ref[:, cols]) for band in bands)
        dq_ref[:, cols] = jnp.where(low, a, b).astype(BF)
        f, s = divmod(4 * p, 8)
        for j, band in enumerate(bands):
            gk = contract_rows(q_ref[:, cols], dqs_ref[band, :]).astype(BF)
            gv = contract_rows(dm_ref[:, cols], out_ref[band, :]).astype(BF)
            for i in range(2):
                piece = slice((2 * j + i) * half, (2 * j + i + 1) * half)
                up_ref[f, s + 2 * j + i, 0:half, :] = gk[piece, :]
                up_ref[f, s + 2 * j + i, half:HD, :] = gv[piece, :]
    for k in range(4):
        for out, yy in ((send, Y1), (keep, Y0)):
            block = 2 * idx[ZS + k] + idx[yy]
            n = dlat_ref.shape[1]
            out[k * rows : (k + 1) * rows, 0:n] = dlat_ref[at(block, rows), :]
            out[k * rows : (k + 1) * rows, n:] = dq_ref[:, at(block, 2 * HD)]


def bundle_kernel(idx, dlat, na, wlt, dq, wq, ups, sum_ref, e_ref, send, keep, part_ref, sums_ref):
    rows = dq.shape[0]
    e = contract_cols(dq[...], wq[...])
    e_ref[...] = e
    total = jnp.sum(na[at(idx[ROW0] // rows, rows), :].astype(F32) * e, axis=0, keepdims=True)
    for g in range(GROUPS):
        band = slice(g * LAT_HEAD, (g + 1) * LAT_HEAD)
        part = contract_rows(dlat[:, band], na[...])
        part_ref[band, :] = part.astype(BF)
        total = total + jnp.sum(part * wlt[band, :].astype(F32), axis=0, keepdims=True)
    line = lax.broadcasted_iota(jnp.int32, (16, total.shape[1]), 0)
    sums_ref[...] = jnp.where(line == 0, total, jnp.where(line == 1, sum_ref[0:1, :], 0.0)).astype(BF)
    shard = send.shape[3]
    n_lat = part_ref.shape[0] // 8
    for out, ks in ((send, (1, 3)), (keep, (0, 2))):
        for i, k in enumerate(ks):
            cols = at(idx[FS + k], shard)
            for j, yy in enumerate((Y1, Y0)):
                for kz in range(4):
                    s = 2 * idx[ZS + kz] + idx[yy]
                    out[i, 4 * j + kz, 0:HD, :] = ups[idx[FS + k], s]
                    out[i, 4 * j + kz, HD : HD + n_lat, :] = part_ref[at(s, n_lat), cols]
                    out[i, 4 * j + kz, HD + n_lat :, :] = sums_ref[:, cols]


def outer_query_kernel(idx, na, p0, p1, p2, p3, f1, f2, own, near, far, diag, total_ref):
    rows = p0.shape[0]
    wide = 2 * HD
    total = None
    for k, piece in enumerate((p0, p1, p2, p3)):
        first = p0.shape[1] - 2 * wide
        for j, yy in enumerate((Y0, Y1)):
            right = piece[:, first + j * wide : first + (j + 1) * wide]
            term = contract_rows(na[at(2 * idx[ZS + k] + idx[yy], rows), :], right)
            total = term if total is None else total + term
    total_ref[...] = total.astype(BF)
    n = own.shape[0]
    for k, out in ((0, own), (2, far), (3, diag)):
        out[...] = total_ref[at(idx[FS + k], n), :]
    first = 0
    for ref in (f1, f2):
        near[first : first + ref.shape[0], :] = ref[:, 0 : near.shape[1]]
        first += ref.shape[0]
    for i in range(n // rows):
        near[first:, i * wide : (i + 1) * wide] = total_ref[at(idx[FS + 1] * (n // rows) + i, rows), :]


def tokens_kernel(p0, p1, p2, p3, e_ref, wlt, tok, dresid, out_ref):
    n = wlt.shape[0]
    dlat = wide_sum(p0[:, 0:n], p1[:, 0:n]) + wide_sum(p2[:, 0:n], p3[:, 0:n])
    e = e_ref[...] + dot_nn(dlat.astype(BF), wlt[...])
    values = tok[...].astype(F32)
    rms = fold(values)
    n = values * rms
    out_ref[...] = (dresid[...] + rms * (e - n * jnp.mean(e * n, axis=-1, keepdims=True))).astype(BF)


def wide_sum(left, right):
    return left.astype(F32) + right.astype(F32)


def pass_kernel(*refs):
    pass


def half_kernel(both, second):
    second[...] = both[second.shape[0] :, :]


def through(values, deps):
    n = len(values)
    return pl.pallas_call(
        pass_kernel,
        in_specs=[pl.BlockSpec(memory_space=pl.ANY)] * (n + len(deps)),
        out_specs=[pl.BlockSpec(memory_space=pl.ANY)] * n,
        out_shape=[jax.ShapeDtypeStruct(v.shape, v.dtype) for v in values],
        input_output_aliases={i: i for i in range(n)},
        compiler_params=pltpu.CompilerParams(vmem_limit_bytes=MIB),
    )(*values, *deps)


def rows_kernel(*refs):
    keeps, theres, (e0, e1, e2, e3, o0, o_up, o_x) = refs[0:8], refs[8:12], refs[12:19]
    rows = e0.shape[0]
    for i, e in enumerate((e0, e1, e2, e3)):
        e[...] = wide_sum(keeps[i][...], theres[i][0:rows, :]).astype(e.dtype)
    sums = [wide_sum(keeps[4 + i][...], theres[i][rows:, :]) for i in range(4)]
    o0[...] = sums[0]
    o_up[...] = sums[1]
    o_x[0:rows, :] = sums[2].astype(BF)
    o_x[rows:, :] = sums[3].astype(BF)


def sum_kernel(left, right, out):
    out[...] = wide_sum(left[...], right[...]).astype(BF)


def eleventh_kernel(up_keep, up_there, go_keep, go_there, o_up, o_x, up, go_own, go_far, o_send):
    o_send[...] = wide_sum(o_up[...], o_x[o_up.shape[0] :, :]).astype(BF)
    sum_kernel(up_keep, up_there, up)
    go_own[...] = wide_sum(go_keep[0], go_there[0]).astype(BF)
    go_far[...] = wide_sum(go_keep[1], go_there[1]).astype(BF)


def exchange_kernel(keep, there, go_own, go_far, b_keep, b_there, p0, p1, p2, p3, b_x, b_xy, y_send, y_keep):
    rows, wide = p0.shape
    n = wide - 4 * HD
    for k, out in enumerate((p0, p1, p2, p3)):
        band = slice(k * rows, (k + 1) * rows)
        out[:, 0:n] = wide_sum(keep[band, 0:n], there[band, 0:n]).astype(BF)
        out[:, n : n + 2 * HD] = keep[band, n:]
        out[:, n + 2 * HD : wide] = there[band, n:]
    tall = b_keep.shape[2]
    for j in range(8):
        band = slice(j % 4 * tall, (j % 4 + 1) * tall)
        (y_send, y_keep)[j // 4][band, :] = wide_sum(b_keep[0, j], b_there[0, j]).astype(BF)
        (b_xy, b_x)[j // 4][band, :] = wide_sum(b_keep[1, j], b_there[1, j]).astype(BF)
    half = go_own.shape[0] // 2
    for i, out in enumerate((y_send, y_keep)):
        band = slice(i * half, (i + 1) * half)
        out[4 * tall :, :] = wide_sum(go_own[band, :], go_far[band, :]).astype(BF)


def quarters_kernel(rows, keep, y_there, x_there, xy_there, z0, z1, z2, z3):
    tall = z0.shape[0] - rows
    for k, out in enumerate((z0, z1, z2, z3)):
        band = slice(k * tall, (k + 1) * tall)
        out[0:tall, :] = (wide_sum(keep[band, :], y_there[band, :]) + wide_sum(x_there[band, :], xy_there[band, :])).astype(BF)
        band = slice(4 * tall + k * rows, 4 * tall + (k + 1) * rows)
        out[tall:, :] = wide_sum(keep[band, :], y_there[band, :]).astype(BF)


def swap(value, axis):
    return lax.ppermute(value, axis, [(0, 1), (1, 0)])


def hop(value, k):
    return lax.ppermute(value, "z", [(i, i ^ k) for i in range(4)])


def corner(value):
    return lax.ppermute(value, ("z", "y"), [(i, i ^ 3) for i in range(8)])


def plus(left, right):
    return left.astype(F32) + right.astype(F32)


def fast_body(tokens, attn_gain, w_query, w_latent, w_key_up, w_value_up, w_out, mlp_gain, w_gate, w_up, w_down, lengths, cotangent):
    x, c, z, y = (lax.axis_index(a) for a in ("x", "c", "z", "y"))
    f, s, zl, zh = 2 * x + c, 2 * z + y, lax.rem(z, 2), z // 2
    rows, d = tokens.shape
    shard = d // 4
    half = shard // 2
    ff8 = w_gate.shape[1] // 8
    wide = (ff8 + 127) // 128 * 128
    n_lat = GROUPS * LAT_HEAD
    keys = 8 * rows

    cw = [(RING[i], RING[(i + 1) % 8]) for i in range(8)]
    ccw = [(b, a) for a, b in cw]
    place = jnp.where(y == 0, z, 7 - z)

    def owner(p):
        p = lax.rem(p + 8, 8)
        return jnp.where(p < 4, 2 * p, 15 - 2 * p)

    def ring(value, pairs):
        return lax.ppermute(value, ("z", "y"), pairs)

    def fold_into(gain, weight):
        return (weight.astype(F32) * gain).astype(BF)

    owners = [s, owner(place - 1), owner(place + 1), owner(place - 2), owner(place + 2), owner(place - 3), owner(place + 3), owner(place - 4)]
    idx = jnp.stack(owners + [f, f ^ 1, f ^ 2, f ^ 3, z, z ^ 1, z ^ 2, z ^ 3, y, y ^ 1, zh, zh ^ 1, zl, s * rows, 4 * c + 2 * zl + y, x, x ^ 1, jnp.where(x != c, 0, jnp.where(zl != c, 1, 2))]).astype(jnp.int32)
    gain_a = attn_gain.astype(F32)[:, None]
    gain_m = mlp_gain.astype(F32)[:, None]

    a1, b1 = ring(tokens, cw), ring(tokens, ccw)
    wl_own = fold_into(gain_a, w_latent)
    wl_far, wl_near = swap(wl_own, "x"), swap(wl_own, "c")
    cut = QW * 3 // 4
    a1, b1 = through((a1, b1), (wl_far,))
    a2, b2 = ring(a1, cw), ring(b1, ccw)
    wl_diag = swap(wl_far, "c")
    wb_own = jnp.concatenate([fold_into(gain_a, w_query), w_key_up, w_value_up], axis=1)
    wb_own, wb_a, wb_b = through((wb_own, wb_own[:, :cut], wb_own[:, cut:]), (a1,))
    wb_near, wb_far = swap(wb_own, "c"), [swap(wb_a, "x")]
    gu_own, gu_near, gu_far = call(columns_kernel, 1, [((shard, 2 * wide), BF)] * 2 + [((2 * shard, 2 * wide), BF)], [((8, shard, 2 * wide), BF)], limit=16)(
        idx, w_gate, w_up, mlp_gain[:, None], deps=(a1,)
    )
    gu_near = swap(gu_near, "c")
    a2, b2 = through((a2, b2), (wb_far[0], gu_own))
    a3, b3 = ring(a2, cw), ring(b2, ccw)
    wo_own = through((w_out,), (a2,))[0]
    wo_far, wo_near = swap(wo_own, "x"), swap(wo_own, "c")
    a3, wb_b = through((a3, wb_b), (b3, wo_far, gu_near))
    down = lax.dynamic_slice_in_dim(w_down, y * ff8, ff8, 0)
    a4 = ring(a3, cw)
    wb_far.append(swap(wb_b, "x"))
    wb_diag, wo_diag = [swap(v, "c") for v in wb_far], swap(wo_far, "c")

    a4, gu_far, cot = through((a4, gu_far, cotangent), (wb_far[1], wo_diag))
    gu_far = swap(gu_far, "x")
    cot_far, cot_up, cot_diag = swap(cot, "y"), hop(cot, 1), corner(cot)
    mixed, probs, outs, qs, queries, na_all, lat_all, w_q, w_key, w_value, w_lat_t = attend(
        idx, lengths, (tokens, a1, b1, a2, b2, a3, b3, a4), (wl_own, wl_near, wl_far, wl_diag), (wb_own, wb_near, *wb_far, *wb_diag)
    )
    w_os = (w_out, wo_near, wo_far, wo_diag)
    resid, normed, pack = call(project_kernel, 1, [((rows, d), F32), ((rows, d), BF), ((5 * rows + shard + ff8, d), BF)])(
        idx, mixed, tokens, *w_os, cot_up, cot_far, cot_diag, cot, gu_far, down
    )

    pack = swap(pack, "c")
    nm_far, nm_up, nm_diag = swap(normed, "y"), hop(normed, 1), corner(normed)
    down_x = through((down,), (normed,))[0]
    pairs = []
    for xx in range(2):
        for zz in range(4):
            pairs.append((((1 - xx) * 2 + zz % 2) * 4 + zz, (xx * 2 + 1 - xx) * 4 + zz))
    down_x = lax.ppermute(down_x, ("x", "c", "z"), pairs)
    w_gu, w_dn, near = call(assemble_kernel, 1, [((d, 2 * wide), BF), ((wide, d), BF), ((5 * rows, d), BF)])(
        idx, gu_own, gu_near, gu_far, pack, down_x, down
    )

    def unit(places, *args, deps=()):
        shapes = [((2 * rows, wide), BF), ((2 * rows, 2 * wide), BF), ((rows, d), F32), ((rows, d), F32), ((2 * rows, d), BF)]
        return call(functools.partial(unit_kernel, places), 0, shapes)(*args, w_gu, w_dn, deps=deps)

    at_own, at_up, at_far, at_diag = (0, 0, 0, 4 * rows), (0, 0, 0, rows), (0, 0, 0, 2 * rows), (0, 0, 0, 3 * rows)
    own_rows = (normed, near, cot, near)
    own = unit(at_own, *own_rows)
    nm_far = through((nm_far,), (w_dn,))[0]
    nm_far2 = swap(nm_far, "c")
    far_rows = (nm_far, nm_far2, cot_far, near)
    far = unit(at_far, *far_rows, deps=(own[0],))
    nm_up = through((nm_up,), (own[0],))[0]
    nm_up2 = swap(nm_up, "c")
    up_rows = (nm_up, nm_up2, cot_up, near)
    up = unit(at_up, *up_rows, deps=(far[0],))
    nm_diag = through((nm_diag,), (own[0],))[0]
    nm_diag2 = swap(nm_diag, "c")
    diag_rows = (nm_diag, nm_diag2, cot_diag, near)
    diag = unit(at_diag, *diag_rows, deps=(up[0],))
    near2, up2, far2, diag2 = (swap(v[4], "c") for v in (own, up, far, diag))
    units = (own, up, far, diag)
    shapes = [((rows, d), F32)] + [((rows, d), BF)] * 3 + [((rows, d), F32)] * 2 + [((2 * rows, d), BF)]
    e_own, *early, o_own, o_up, o_x = call(rows_kernel, 0, shapes)(*[v[2] for v in units], *[v[3] for v in units], near2, up2, far2, diag2)
    d_up, d_far, d_diag = hop(early[0], 1), swap(early[1], "y"), corner(early[2])
    shapes = [((2 * ff8, 2 * shard), BF)] * 2 + [((ff8, 2 * shard), BF)] * 2
    at_all, all_rows = at_own + at_up + at_far + at_diag, own_rows + up_rows + far_rows + diag_rows
    y1_send, y1_keep, y2_send, y2_keep = call(functools.partial(outer_kernel, ff8, at_all), 1, shapes, limit=24)(
        idx, *[v[0] for v in units], *[v[1] for v in units], *all_rows
    )
    y1_there = swap(y1_send, "x")
    dresid, dattn, dmixed, v_m = call(middle_kernel, 1, [((rows, d), F32), ((rows, d), BF), ((rows, QW), BF), ((8, d), F32)])(
        idx, e_own, d_far, d_up, d_diag, resid, cotangent, *w_os, deps=(y1_there,)
    )

    def home(value):
        pairs = []
        for i in range(8):
            cc, hh, ll = i // 4, i // 2 % 2, i % 2
            pairs.append((i, hh * 4 + 2 * cc + ll))
        return lax.ppermute(value, ("c", "z"), pairs)

    go_send, go_keep = call(outer_out_kernel, 1, [((2, QW, shard), BF)] * 2)(idx, mixed, dattn)
    go_there = swap(go_send, "c")
    f1 = home(call(sum_kernel, 0, [((2 * ff8, 2 * shard), BF)])(y1_keep, y1_there, deps=(go_send,))[0])
    o_x = swap(through((o_x,), (go_send,))[0], "y")
    y2_there = swap(through((y2_send,), (go_send,))[0], "x")
    dlat, p_send, p_keep, dq, ups = call(
        attend_back_kernel,
        1,
        [((keys, n_lat), BF)] + [((4 * rows, n_lat + 2 * HD), BF)] * 2 + [((rows, QW), BF), ((4, 8, HD, LAT_HEAD), BF)],
        [((HEADS * rows, keys), BF), ((HEADS * rows, LAT_HEAD), BF), ((HEADS * rows, LAT_HEAD), BF)],
        limit=40,
        far_in=range(1, 8),
    )(idx, dmixed, queries, lat_all, w_key, w_value, probs, outs, qs, deps=(y1_there, go_send))
    tall = HD + n_lat // 8 + 16
    e_q, b_send, b_keep = call(
        bundle_kernel,
        1,
        [((rows, d), F32), ((2, 8, tall, shard), BF), ((2, 8, tall, shard), BF)],
        [((n_lat, d), BF), ((16, d), BF)],
        limit=24,
        far_in=(1, 2, 4),
    )(idx, dlat, na_all, w_lat_t, dq, w_q, ups, v_m)
    f2, go_own, go_far, o_send = call(eleventh_kernel, 0, [((ff8, 2 * shard), BF)] + [((QW, shard), BF)] * 2 + [((rows, d), BF)])(
        y2_keep, y2_there, go_keep, go_there, o_up, o_x, deps=(b_send, f1)
    )
    b_send, p_send = through((b_send, p_send), (go_far,))
    p_there = swap(p_send, "y")
    f2, o_there = home(f2), hop(o_send, 1)
    go_far, b_there = swap(go_far, "x"), swap(b_send, "c")
    flat = ((4 * tall, shard), BF)
    tower = ((4 * tall + QW // 2, shard), BF)
    n_p = n_lat + 4 * HD
    shapes = [((rows, n_p), BF)] * 4 + [flat, flat, tower, tower]
    p0, p1, p2, p3, b_x, b_xy, y_send, y_keep = call(exchange_kernel, 0, shapes)(
        p_keep, p_there, go_own, go_far, b_keep, b_there, deps=(f2, o_there)
    )
    pieces = (p0, hop(p1, 1), hop(p2, 2), hop(p3, 3))
    b_x, y_there = swap(b_x, "x"), swap(y_send, "y")
    b_xy = lax.ppermute(b_xy, ("x", "y"), [(i, i ^ 3) for i in range(4)])
    z0, z1, z2, z3 = call(functools.partial(quarters_kernel, rows), 0, [((tall + rows, shard), BF)] * 4)(
        y_keep, y_there, b_x, b_xy, deps=pieces[1:]
    )
    last = z0.astype(F32) + hop(z1, 1) + hop(z2, 2) + hop(z3, 3)
    quarter = ((shard, 2 * HD), BF)
    gq, near, gq_far, gq_diag = call(
        outer_query_kernel, 1, [quarter, ((3 * ff8 + rows, shard), BF), quarter, quarter], [((d, 2 * HD), BF)], far_in=(0,)
    )(idx, na_all, *pieces, f1, f2, deps=(z0,))
    near, gq_far, gq_diag = swap(near, "c"), swap(gq_far, "x"), lax.ppermute(gq_diag, ("x", "c"), [(i, i ^ 3) for i in range(4)])
    tokens_grad = call(tokens_kernel, 0, [((rows, d), BF)])(*pieces, e_q, w_lat_t, tokens, dresid, deps=(gq,))[0]
    gq_near = jnp.concatenate([near[3 * ff8 :, i * 2 * HD : (i + 1) * 2 * HD] for i in range(shard // rows)], 0)
    grad_query = (plus(gq, gq_near) + plus(gq_far, gq_diag)) * gain_a
    output = (resid + o_own + o_x[:rows] + o_there).astype(BF)
    grad_down = plus(f1[:ff8, shard:], near[:ff8])
    grad_gate = plus(f1[ff8:, shard:], near[ff8 : 2 * ff8]).T * gain_m
    grad_up = plus(f2[:, shard:], near[2 * ff8 : 3 * ff8]).T * gain_m
    grad_out = last[tall:]
    eighth = HD // 2
    n_small = n_lat // 8
    grad_key_up = last[:eighth].T
    grad_value_up = last[eighth:HD].T
    grad_latent = last[HD : HD + n_small].T * gain_a
    own_gain = shard // 8
    pair = lax.dynamic_slice(last, (HD + n_small, s * own_gain), (2, own_gain))
    grad_attn_gain = pair[0] / lax.dynamic_slice_in_dim(gain_a[:, 0], s * own_gain, own_gain)
    grad_mlp_gain = pair[1] / lax.dynamic_slice_in_dim(gain_m[:, 0], s * own_gain, own_gain)
    return (
        output,
        tokens_grad,
        grad_attn_gain,
        grad_query,
        grad_latent,
        grad_key_up,
        grad_value_up,
        grad_out,
        grad_mlp_gain,
        grad_gate,
        grad_up,
        grad_down,
    )


def fast_solution(mesh):
    mesh = Mesh(mesh.devices.reshape(2, 2, 4, 2), ("x", "c", "z", "y"))
    f, s = ("x", "c"), ("z", "y")
    a = f + s
    in_specs = (P(a, None), P(f), P(f, None), P(f, None), P(None, f), P(None, f), P(f, None), P(f), P(f, None), P(f, None), P(f, None), P(f, None), P(a, None))
    out_specs = (P(a, None), P(a, None), P(a), P(f, s), P(f, s), P(None, a), P(None, a), P(s, f), P(a), P(f, s), P(f, s), P(s, f))
    return jax.shard_map(fast_body, mesh=mesh, in_specs=in_specs, out_specs=out_specs, check_vma=False)


def solution(mesh):
    if mesh.shape["fsdp"] == 4 and mesh.shape["seq"] == 8:
        return fast_solution(mesh)
    in_specs = (
        P(("fsdp", "seq"), None),
        P("fsdp"),
        P("fsdp", None),
        P("fsdp", None),
        P(None, "fsdp"),
        P(None, "fsdp"),
        P("fsdp", None),
        P("fsdp"),
        P("fsdp", None),
        P("fsdp", None),
        P("fsdp", None),
        P("fsdp", None),
        P(("fsdp", "seq"), None),
    )
    out_specs = (
        P(("fsdp", "seq"), None),
        P(("fsdp", "seq"), None),
        P(("fsdp", "seq")),
        P("fsdp", "seq"),
        P("fsdp", "seq"),
        P(None, ("fsdp", "seq")),
        P(None, ("fsdp", "seq")),
        P("seq", "fsdp"),
        P(("fsdp", "seq")),
        P("fsdp", "seq"),
        P("fsdp", "seq"),
        P("seq", "fsdp"),
    )
    return jax.shard_map(body, mesh=mesh, in_specs=in_specs, out_specs=out_specs, check_vma=False)
```

```python
import functools

import jax
import jax.numpy as jnp
from jax import lax
from jax.experimental import pallas as pl
from jax.experimental.pallas import tpu as pltpu
from jax.sharding import Mesh
from jax.sharding import PartitionSpec as P

HEADS = 16
HD = 64
GROUPS = 2
LAT_HEAD = 256
KEYBLK = 1024
QW = 1024
GQ = 8


epsilon = 1e-06


def normalize(values, gain):
    return values * lax.rsqrt(jnp.mean(values * values, axis=-1, keepdims=True) + epsilon) * gain


def doc_numbers(lengths_row, count):
    bounds = jnp.cumsum(lengths_row)
    places = jnp.arange(count, dtype=jnp.int32)
    return jnp.sum((places[:, None] >= bounds[None, :-1]).astype(jnp.int32), axis=1)


def contract_rows(left, right):
    return lax.dot_general(
        left, right, (((0,), (0,)), ((), ())), preferred_element_type=jnp.float32
    )


def contract_cols(left, right):
    return lax.dot_general(
        left, right, (((1,), (1,)), ((), ())), preferred_element_type=jnp.float32
    )


def split_parts(values):
    upper = values.astype(jnp.bfloat16)
    lower = (values - upper.astype(jnp.float32)).astype(jnp.bfloat16)
    return (upper, lower)


def gated_unit(gate_pre, upward):
    return jax.nn.silu(gate_pre) * upward


def body(
    tokens,
    attn_gain,
    w_query,
    w_latent,
    w_key_up,
    w_value_up,
    w_out,
    mlp_gain,
    w_gate,
    w_up,
    w_down,
    lengths,
    cotangent,
):
    attn_gain, w_query, w_latent, w_key_up, w_value_up, w_out, mlp_gain, w_gate, w_up, w_down = (
        lax.all_gather(attn_gain, "fsdp", axis=0, tiled=True),
        lax.all_gather(w_query, "fsdp", axis=0, tiled=True),
        lax.all_gather(w_latent, "fsdp", axis=0, tiled=True),
        lax.all_gather(w_key_up, "fsdp", axis=1, tiled=True),
        lax.all_gather(w_value_up, "fsdp", axis=1, tiled=True),
        lax.all_gather(w_out, "fsdp", axis=0, tiled=True),
        lax.all_gather(mlp_gain, "fsdp", axis=0, tiled=True),
        lax.all_gather(w_gate, "fsdp", axis=0, tiled=True),
        lax.all_gather(w_up, "fsdp", axis=0, tiled=True),
        lax.all_gather(w_down, "fsdp", axis=0, tiled=True),
    )
    row_count = tokens.shape[0]
    seq_rank = lax.axis_index("seq")
    stream_len = row_count * lax.axis_size("seq")
    head_width = GQ * HD
    doc_ids = doc_numbers(lengths[0], stream_len)
    row_start = seq_rank * row_count
    own_docs = lax.dynamic_slice_in_dim(doc_ids, row_start, row_count)
    own_places = row_start + jnp.arange(row_count, dtype=jnp.int32)
    block_count = (row_start + row_count - 1) // KEYBLK + 1
    tokens_f = tokens.astype(jnp.float32)
    gain_a = attn_gain.astype(jnp.float32)
    gain_m = mlp_gain.astype(jnp.float32)
    normed = normalize(tokens_f, gain_a).astype(jnp.bfloat16)
    queries = jnp.dot(normed, w_query, preferred_element_type=jnp.float32).astype(jnp.bfloat16)
    latent = jnp.dot(normed, w_latent, preferred_element_type=jnp.float32).astype(jnp.bfloat16)
    gathered = lax.all_gather(latent, "seq", axis=0, tiled=True)
    query_heads = queries.reshape(row_count, HEADS, HD)

    def key_block(source, block_idx, group_idx, with_values):
        latent_part = lax.dynamic_slice(
            source, (block_idx * KEYBLK, group_idx * LAT_HEAD), (KEYBLK, LAT_HEAD)
        )
        low_col = group_idx * head_width
        key_rows = (
            jnp.dot(
                latent_part,
                w_key_up[:, low_col : low_col + head_width],
                preferred_element_type=jnp.float32,
            )
            .astype(jnp.bfloat16)
            .reshape(KEYBLK, GQ, HD)
        )
        value_rows = None
        if with_values:
            value_rows = (
                jnp.dot(
                    latent_part,
                    w_value_up[:, low_col : low_col + head_width],
                    preferred_element_type=jnp.float32,
                )
                .astype(jnp.bfloat16)
                .reshape(KEYBLK, GQ, HD)
            )
        key_docs = lax.dynamic_slice_in_dim(doc_ids, block_idx * KEYBLK, KEYBLK)
        key_places = block_idx * KEYBLK + jnp.arange(KEYBLK, dtype=jnp.int32)
        allowed = (own_docs[:, None] == key_docs[None, :]) & (
            own_places[:, None] >= key_places[None, :]
        )
        return (latent_part, key_rows, value_rows, allowed)

    def block_scores(group_idx, key_rows):
        group_query = query_heads[:, group_idx * GQ : (group_idx + 1) * GQ]
        return (
            jnp.einsum("qhd,khd->hqk", group_query, key_rows, preferred_element_type=jnp.float32)
            * 0.125
        )

    def first_pass(block_idx, carried):
        row_max, row_total = carried
        max_list = []
        total_list = []
        for group_idx in range(GROUPS):
            _, key_rows, _, allowed = key_block(gathered, block_idx, group_idx, False)
            masked = jnp.where(allowed[None], block_scores(group_idx, key_rows), -1e30)
            old_max = row_max[group_idx * GQ : (group_idx + 1) * GQ]
            new_max = jnp.maximum(old_max, jnp.max(masked, axis=-1))
            row_mass = jnp.sum(
                jnp.where(allowed[None], jnp.exp(masked - new_max[:, :, None]), 0.0), axis=-1
            )
            max_list.append(new_max)
            total_list.append(
                row_total[group_idx * GQ : (group_idx + 1) * GQ] * jnp.exp(old_max - new_max)
                + row_mass
            )
        return (jnp.concatenate(max_list, axis=0), jnp.concatenate(total_list, axis=0))

    start_max = jnp.full((HEADS, row_count), -1e30, jnp.float32)
    start_total = jnp.zeros((HEADS, row_count), jnp.float32)
    row_max, row_total = lax.fori_loop(0, block_count, first_pass, (start_max, start_total))
    logsum = row_max + jnp.log(row_total)

    def block_probs(group_idx, key_rows, allowed):
        group_logsum = logsum[group_idx * GQ : (group_idx + 1) * GQ]
        return jnp.where(
            allowed[None],
            jnp.exp(block_scores(group_idx, key_rows) - group_logsum[:, :, None]),
            0.0,
        )

    def second_pass(block_idx, carried):
        rounded_sum, exact_sum = carried
        rounded_list = []
        exact_list = []
        for group_idx in range(GROUPS):
            _, key_rows, value_rows, allowed = key_block(gathered, block_idx, group_idx, True)
            attn_probs = block_probs(group_idx, key_rows, allowed)
            probs_upper, probs_lower = split_parts(attn_probs)
            rounded_part = jnp.einsum(
                "hqk,khd->qhd", probs_upper, value_rows, preferred_element_type=jnp.float32
            )
            rounded_list.append(rounded_part)
            exact_list.append(
                rounded_part
                + jnp.einsum(
                    "hqk,khd->qhd", probs_lower, value_rows, preferred_element_type=jnp.float32
                )
            )
        return (
            rounded_sum + jnp.concatenate(rounded_list, axis=1),
            exact_sum + jnp.concatenate(exact_list, axis=1),
        )

    head_zeros = jnp.zeros((row_count, HEADS, HD), jnp.float32)
    rounded_sum, exact_sum = lax.fori_loop(0, block_count, second_pass, (head_zeros, head_zeros))
    mixed = rounded_sum.reshape(row_count, QW).astype(jnp.bfloat16)
    resid = tokens_f + jnp.dot(mixed, w_out, preferred_element_type=jnp.float32)
    normed_m = normalize(resid, gain_m).astype(jnp.bfloat16)
    gate_pre = jnp.dot(normed_m, w_gate, preferred_element_type=jnp.float32)
    upward = jnp.dot(normed_m, w_up, preferred_element_type=jnp.float32)
    hidden = gated_unit(gate_pre, upward).astype(jnp.bfloat16)
    output = (resid + jnp.dot(hidden, w_down, preferred_element_type=jnp.float32)).astype(
        jnp.bfloat16
    )
    dhidden = contract_cols(cotangent, w_down).astype(jnp.bfloat16)
    _, pull_unit = jax.vjp(gated_unit, gate_pre, upward)
    dgate, dupward = pull_unit(dhidden.astype(jnp.float32))
    dgate = dgate.astype(jnp.bfloat16)
    dupward = dupward.astype(jnp.bfloat16)
    dnormed_m = contract_cols(dgate, w_gate) + contract_cols(dupward, w_up)
    _, pull_norm_m = jax.vjp(normalize, resid, gain_m)
    dresid_norm, grad_mlp_gain = pull_norm_m(dnormed_m)
    dresid = cotangent.astype(jnp.float32) + dresid_norm
    dattn = dresid.astype(jnp.bfloat16)
    dmixed = contract_cols(dattn, w_out).astype(jnp.bfloat16)
    grad_heads = dmixed.reshape(row_count, HEADS, HD)
    row_delta = jnp.einsum("qhd,qhd->hq", grad_heads.astype(jnp.float32), exact_sum)
    source = gathered

    def backward_pass(block_idx, carried):
        dqueries, dlatent, grad_ku, grad_vu = carried
        query_list = []
        fresh_latent = []
        for group_idx in range(GROUPS):
            latent_part, key_rows, value_rows, allowed = key_block(
                source, block_idx, group_idx, True
            )
            low_col = group_idx * head_width
            group_query = query_heads[:, group_idx * GQ : (group_idx + 1) * GQ]
            group_grad = grad_heads[:, group_idx * GQ : (group_idx + 1) * GQ]
            attn_probs = block_probs(group_idx, key_rows, allowed)
            prob_grad = jnp.einsum(
                "qhd,khd->hqk", group_grad, value_rows, preferred_element_type=jnp.float32
            )
            group_delta = row_delta[group_idx * GQ : (group_idx + 1) * GQ]
            score_grad = (attn_probs * (prob_grad - group_delta[:, :, None])).astype(jnp.bfloat16)
            query_list.append(
                jnp.einsum("hqk,khd->qhd", score_grad, key_rows, preferred_element_type=jnp.float32)
                * 0.125
            )
            key_grad = (
                jnp.einsum(
                    "hqk,qhd->khd", score_grad, group_query, preferred_element_type=jnp.float32
                )
                * 0.125
            ).reshape(KEYBLK, head_width)
            value_grad = jnp.einsum(
                "hqk,qhd->khd",
                attn_probs.astype(jnp.bfloat16),
                group_grad,
                preferred_element_type=jnp.float32,
            ).reshape(KEYBLK, head_width)
            key_upper, key_lower = split_parts(key_grad)
            value_upper, value_lower = split_parts(value_grad)
            key_weight = w_key_up[:, low_col : low_col + head_width]
            value_weight = w_value_up[:, low_col : low_col + head_width]
            latent_grad = (
                contract_cols(key_upper, key_weight)
                + contract_cols(key_lower, key_weight)
                + contract_cols(value_upper, value_weight)
                + contract_cols(value_lower, value_weight)
            )
            fresh_latent.append(
                lax.dynamic_update_slice_in_dim(
                    dlatent[group_idx], latent_grad, block_idx * KEYBLK, 0
                )
            )
            grad_ku = grad_ku.at[:, low_col : low_col + head_width].add(
                contract_rows(latent_part, key_upper) + contract_rows(latent_part, key_lower)
            )
            grad_vu = grad_vu.at[:, low_col : low_col + head_width].add(
                contract_rows(latent_part, value_upper) + contract_rows(latent_part, value_lower)
            )
        return (
            dqueries + jnp.concatenate(query_list, axis=1),
            tuple(fresh_latent),
            grad_ku,
            grad_vu,
        )

    latent_zeros = tuple(
        (jnp.zeros((stream_len, LAT_HEAD), jnp.float32) for group_idx in range(GROUPS))
    )
    weight_zeros = jnp.zeros((LAT_HEAD, QW), jnp.float32)
    dqueries, dlatent, grad_key_up, grad_value_up = lax.fori_loop(
        0, block_count, backward_pass, (head_zeros, latent_zeros, weight_zeros, weight_zeros)
    )
    dqueries = dqueries.reshape(row_count, QW).astype(jnp.bfloat16)
    shares = (
        lax.psum_scatter(dlatent[0], "seq", scatter_dimension=0, tiled=True),
        lax.psum_scatter(dlatent[1], "seq", scatter_dimension=0, tiled=True),
    )
    dlatent_own = jnp.concatenate(shares, axis=1).astype(jnp.bfloat16)
    dnormed = contract_cols(dqueries, w_query) + contract_cols(dlatent_own, w_latent)
    _, pull_norm_a = jax.vjp(normalize, tokens_f, gain_a)
    dtokens_norm, grad_attn_gain = pull_norm_a(dnormed)
    tokens_grad = (dresid + dtokens_norm).astype(jnp.bfloat16)
    normed_all, normed_m_all, cotangent_all, dattn_all = (
        lax.all_gather(normed, "seq", axis=0, tiled=True),
        lax.all_gather(normed_m, "seq", axis=0, tiled=True),
        lax.all_gather(cotangent, "seq", axis=0, tiled=True),
        lax.all_gather(dattn, "seq", axis=0, tiled=True),
    )
    hidden_cols, dgate_cols, dupward_cols, mixed_cols, dquery_cols, dlatent_cols = (
        lax.all_to_all(hidden, "seq", split_axis=1, concat_axis=0, tiled=True),
        lax.all_to_all(dgate, "seq", split_axis=1, concat_axis=0, tiled=True),
        lax.all_to_all(dupward, "seq", split_axis=1, concat_axis=0, tiled=True),
        lax.all_to_all(mixed, "seq", split_axis=1, concat_axis=0, tiled=True),
        lax.all_to_all(dqueries, "seq", split_axis=1, concat_axis=0, tiled=True),
        lax.all_to_all(dlatent_own, "seq", split_axis=1, concat_axis=0, tiled=True),
    )
    part_query = contract_rows(normed_all, dquery_cols)
    part_latent = contract_rows(normed_all, dlatent_cols)
    part_out = contract_rows(mixed_cols, dattn_all)
    part_gate = contract_rows(normed_m_all, dgate_cols)
    part_up = contract_rows(normed_m_all, dupward_cols)
    part_down = contract_rows(hidden_cols, cotangent_all)
    grad_query, grad_latent, grad_out, grad_gate, grad_up, grad_down = (
        lax.psum_scatter(
            part_query.astype(jnp.bfloat16), "fsdp", scatter_dimension=0, tiled=True
        ).astype(jnp.float32),
        lax.psum_scatter(
            part_latent.astype(jnp.bfloat16), "fsdp", scatter_dimension=0, tiled=True
        ).astype(jnp.float32),
        lax.psum_scatter(
            part_out.astype(jnp.bfloat16), "fsdp", scatter_dimension=1, tiled=True
        ).astype(jnp.float32),
        lax.psum_scatter(
            part_gate.astype(jnp.bfloat16), "fsdp", scatter_dimension=0, tiled=True
        ).astype(jnp.float32),
        lax.psum_scatter(
            part_up.astype(jnp.bfloat16), "fsdp", scatter_dimension=0, tiled=True
        ).astype(jnp.float32),
        lax.psum_scatter(
            part_down.astype(jnp.bfloat16), "fsdp", scatter_dimension=1, tiled=True
        ).astype(jnp.float32),
    )
    small_sent = (
        lax.psum_scatter(grad_attn_gain, ("fsdp", "seq"), scatter_dimension=0, tiled=True),
        lax.psum_scatter(grad_key_up, ("fsdp", "seq"), scatter_dimension=1, tiled=True),
        lax.psum_scatter(grad_value_up, ("fsdp", "seq"), scatter_dimension=1, tiled=True),
        lax.psum_scatter(grad_mlp_gain, ("fsdp", "seq"), scatter_dimension=0, tiled=True),
    )
    return (
        output,
        tokens_grad,
        small_sent[0],
        grad_query,
        grad_latent,
        small_sent[1],
        small_sent[2],
        grad_out,
        small_sent[3],
        grad_gate,
        grad_up,
        grad_down,
    )


BF = jnp.bfloat16
F32 = jnp.float32
NEG = -1e30
SCALE = 0.125
RING = (0, 2, 4, 6, 7, 5, 3, 1)
MIB = 2**20

FS, ZS, Y0, Y1, ZH0, ZH1, ZL, ROW0, BLOCK, X0, X1, DOWN = 8, 12, 16, 17, 18, 19, 20, 21, 22, 23, 24, 25


def dot_nn(left, right):
    return lax.dot_general(left, right, (((1,), (0,)), ((), ())), preferred_element_type=F32)


def fold(total):
    return lax.rsqrt(jnp.mean(total * total, axis=-1, keepdims=True) + epsilon)


def at(index, size):
    return pl.ds(pl.multiple_of(index * size, size), size)


class Lazy:
    def __init__(self, ref, copy):
        self.ref, self.copy, self.shape = ref, copy, ref.shape

    def __getitem__(self, index):
        if self.copy is not None:
            self.copy.wait()
            self.copy = None
        return self.ref[index]


class Late:
    def __init__(self, ref, out, sems, parts):
        self.ref, self.out, self.sems, self.parts, self.shape, self.copies = ref, out, sems, parts, ref.shape, []

    def __getitem__(self, index):
        return self.ref[index]

    def __setitem__(self, index, value):
        self.ref[index] = value

    def flush(self):
        n = self.shape[0] // self.parts
        band = pl.ds(len(self.copies) * n, n)
        copy = pltpu.make_async_copy(self.ref.at[band], self.out.at[band], self.sems[len(self.copies)])
        copy.start()
        self.copies.append(copy)


def call(kernel, n_smem, outs, scratch=(), limit=16, flops=1, far_in=(), far_out=(), parts=1, split=()):
    far_in, far_out = tuple(far_in), tuple(far_out)
    n_out, n_far, n_sems = len(outs), len(far_in) + len(far_out), len(far_in) + parts * len(far_out)

    def run(*args, deps=()):
        n_in = len(args) - n_smem

        def body(*refs):
            smem, ins, results = refs[:n_smem], list(refs[n_smem : n_smem + n_in]), list(refs[n_smem + n_in + len(deps) : n_smem + n_in + len(deps) + n_out])
            rest = refs[n_smem + n_in + len(deps) + n_out :]
            sems = rest[-1]
            far, own = rest[len(scratch) : len(scratch) + n_far], rest[: len(scratch)]
            for k, i in enumerate(far_in):
                copy = pltpu.make_async_copy(ins[i], far[k], sems.at[k])
                copy.start()
                ins[i] = Lazy(far[k], copy)
            late = []
            for k, i in enumerate(far_out):
                own_sems = [sems.at[len(far_in) + parts * k + p] for p in range(parts)]
                results[i] = Late(far[len(far_in) + k], results[i], own_sems, parts if i in split else 1)
                late.append(results[i])
            kernel(*smem, *ins, *results, *own)
            for i in far_in:
                if ins[i].copy is not None:
                    ins[i].copy.wait()
            for v in late:
                while len(v.copies) < v.parts:
                    v.flush()
            for v in late:
                for copy in v.copies:
                    copy.wait()

        spec = lambda i, far: pl.BlockSpec(memory_space=pl.ANY if i in far else pltpu.VMEM)
        shapes = [pltpu.VMEM(shape, dtype) for shape, dtype in scratch]
        shapes += [pltpu.VMEM(args[n_smem + i].shape, args[n_smem + i].dtype) for i in far_in]
        shapes += [pltpu.VMEM(*outs[i]) for i in far_out]
        return pl.pallas_call(
            body,
            in_specs=[pl.BlockSpec(memory_space=pltpu.SMEM)] * n_smem + [spec(i, far_in) for i in range(n_in)] + [pl.BlockSpec(memory_space=pl.ANY)] * len(deps),
            out_specs=[spec(i, far_out) for i in range(n_out)],
            out_shape=[jax.ShapeDtypeStruct(shape, dtype) for shape, dtype in outs],
            scratch_shapes=shapes + [pltpu.SemaphoreType.DMA((max(1, n_sems),))],
            compiler_params=pltpu.CompilerParams(vmem_limit_bytes=limit * MIB),
            cost_estimate=pl.CostEstimate(flops=flops, bytes_accessed=0, transcendentals=0),
        )(*args, *deps)

    return run


def attend_kernel(idx, lens, *refs):
    tok, wl, wb = refs[0:8], refs[8:12], refs[12:18]
    mixed_ref, probs_ref, out_ref, qs_ref, q_ref, na_ref, lat_ref, wq_ref, wk_ref, wv_ref, wlt_ref, bias_ref = refs[18:30]
    rows, d = tok[0].shape
    keys = 8 * rows
    part = wl[0].shape[0]
    width = GQ * rows
    for i in range(8):
        values = tok[i][...].astype(F32)
        na_ref[at(idx[i], rows), :] = (values * fold(values)).astype(BF)
    na_ref.flush()
    for k in range(4):
        wlt_ref[:, at(idx[FS + k], part)] = wl[k][...].T
    wlt_ref.flush()
    lat_ref[...] = contract_cols(na_ref[...], wlt_ref[...]).astype(BF)
    lat_ref.flush()
    for k in range(4):
        here = at(idx[FS + k], part)
        if k < 2:
            wq_ref[here, :] = wb[k][:, 0:QW]
            wk_ref[:, here] = wb[k][:, QW : QW + LAT_HEAD]
            wv_ref[:, here] = wb[k][:, QW + LAT_HEAD : QW + 2 * LAT_HEAD]
        else:
            first, second = wb[2 * k - 2], wb[2 * k - 1]
            cut = first.shape[1]
            wq_ref[here, 0:cut] = first[...]
            wq_ref[here, cut:QW] = second[:, 0 : QW - cut]
            wk_ref[:, here] = second[:, QW - cut : QW - cut + LAT_HEAD]
            wv_ref[:, here] = second[:, QW - cut + LAT_HEAD : QW - cut + 2 * LAT_HEAD]
    q_ref[...] = dot_nn(na_ref[at(idx[0], rows), :], wq_ref[...]).astype(BF)
    for ref in (wq_ref, wk_ref, wv_ref, q_ref):
        ref.flush()
    place = lax.broadcasted_iota(jnp.int32, (rows, keys), 1)
    own = idx[ROW0] + lax.broadcasted_iota(jnp.int32, (rows, keys), 0)
    first = jnp.zeros((rows, keys), jnp.int32)
    edge = 0
    for i in range(lens.shape[1] - 1):
        edge = edge + lens[0, i]
        first = jnp.where(own >= edge, edge, first)
    bias = jnp.where((place >= first) & (place <= own), 0.0, NEG)
    bias_ref[0:rows, :] = bias
    bias_ref[rows : 2 * rows, :] = bias
    low = lax.broadcasted_iota(jnp.int32, (rows, 2 * HD), 1) < HD
    for p in range(HEADS // 2):
        cols = slice(p * 2 * HD, (p + 1) * 2 * HD)
        q = q_ref[:, cols]
        none = jnp.zeros_like(q)
        for j, own_q in enumerate((jnp.where(low, q, none), jnp.where(low, none, q))):
            qs_ref[(2 * p + j) * rows : (2 * p + j + 1) * rows, :] = (contract_cols(own_q, wk_ref[:, cols]) * SCALE).astype(BF)
    for g in range(GROUPS):
        lat = lat_ref[:, g * LAT_HEAD : (g + 1) * LAT_HEAD]
        for r in range(0, width, 2 * rows):
            band = slice(g * width + r, g * width + r + 2 * rows)
            scores = contract_cols(qs_ref[band, :], lat) + bias_ref[...]
            mass = jnp.exp(scores - jnp.max(scores, axis=-1, keepdims=True))
            probs_ref[band, :] = (mass * (1.0 / jnp.sum(mass, axis=-1, keepdims=True))).astype(BF)
        band = slice(g * width, (g + 1) * width)
        out_ref[band, :] = dot_nn(probs_ref[band, :], lat).astype(BF)
        for ref in (probs_ref, qs_ref, out_ref):
            ref.flush()
    for p in range(HEADS // 2):
        cols = slice(p * 2 * HD, (p + 1) * 2 * HD)
        a, b = (dot_nn(out_ref[(2 * p + j) * rows : (2 * p + j + 1) * rows, :], wv_ref[:, cols]) for j in range(2))
        mixed_ref[:, cols] = jnp.where(low, a, b).astype(BF)


def attend(idx, lens, blocks, w_lats, w_bigs, deps=()):
    rows, d = blocks[0].shape
    keys, n_lat = 8 * rows, GROUPS * LAT_HEAD
    outs = [(rows, QW), (HEADS * rows, keys), (HEADS * rows, LAT_HEAD), (HEADS * rows, LAT_HEAD), (rows, QW)]
    outs += [(keys, d), (keys, n_lat), (d, QW), (LAT_HEAD, QW), (LAT_HEAD, QW), (n_lat, d)]
    macs = 2 * HEADS * rows * keys * LAT_HEAD + keys * d * n_lat
    return call(
        attend_kernel, 2, [(v, BF) for v in outs], [((2 * rows, keys), F32)], limit=60,
        far_in=range(18), far_out=range(1, 11), parts=GROUPS, split=(1, 2, 3),
    )(
        idx, lens, *blocks, *w_lats, *w_bigs, deps=deps
    )


def project_kernel(idx, mixed, tok, *refs):
    parts, (cot_up, cot_far, cot_diag, cot, gu_c, down, resid_ref, normed_ref, pack_ref) = refs[:4], refs[4:]
    total = tok[...].astype(F32)
    for k, w in enumerate(parts):
        total = total + dot_nn(mixed[:, at(idx[FS + k], w.shape[0])], w[...])
    resid_ref[...] = total
    normed = (total * fold(total)).astype(BF)
    normed_ref[...] = normed
    rows = normed.shape[0]
    pack_ref[0:rows, :] = normed
    for i, ref in enumerate((cot_up, cot_far, cot_diag, cot)):
        pack_ref[(i + 1) * rows : (i + 2) * rows, :] = ref[...]
    n = gu_c.shape[0] // 2
    first = 5 * rows
    pack_ref[first : first + n, 0 : gu_c.shape[1]] = gu_c[n:, :]
    pack_ref[first : first + n, gu_c.shape[1] :] = jnp.zeros((n, pack_ref.shape[1] - gu_c.shape[1]), BF)
    pack_ref[first + n :, :] = down[...]


def columns_kernel(idx, gate_ref, up_ref, gain_ref, own_ref, near_ref, pair_ref, all_ref):
    gain = gain_ref[...].astype(F32)
    n, rows, two = all_ref.shape
    cols = gate_ref.shape[1] // n
    gap = jnp.zeros((rows, two // 2 - cols), BF)
    for j in range(n):
        for part, ref in enumerate((gate_ref, up_ref)):
            block = (ref[:, j * cols : (j + 1) * cols].astype(F32) * gain).astype(BF)
            all_ref[j, :, part * (two // 2) : (part + 1) * (two // 2)] = jnp.concatenate([block, gap], axis=1)
    own_ref[...] = all_ref[idx[BLOCK]]
    near_ref[...] = all_ref[idx[BLOCK] ^ 4]
    pair_ref[0:rows, :] = own_ref[...]
    pair_ref[rows:, :] = near_ref[...]


def assemble_kernel(idx, own, near, far, pack, down_x, down, gu_ref, dn_ref, near_ref):
    near_ref[...] = pack[0 : near_ref.shape[0], :]
    part, n = own.shape
    first = pack.shape[0] - down.shape[0]
    for k, w in enumerate((own[...], near[...], far[0:part, :], pack[first - part : first, 0:n])):
        gu_ref[at(idx[FS + k], part), :] = w
    n = down.shape[0]
    for i, ref in enumerate((down_x, pack, down)):

        @pl.when(idx[DOWN] == i)
        def _(ref=ref):
            dn_ref[0:n, :] = ref[-n:, :]

    dn_ref[n:, :] = jnp.zeros((dn_ref.shape[0] - n, dn_ref.shape[1]), BF)


def rows_of(ref, where, rows):
    return ref[where : where + rows, :]


def unit_kernel(places, n0, n1, c0, c1, w_gu, w_dn, hid_ref, both_ref, dkeep, okeep, send):
    rows = dkeep.shape[0]
    wide = w_dn.shape[0]
    n0, n1, c0, c1 = (rows_of(ref, p, rows) for ref, p in zip((n0, n1, c0, c1), places))
    both = dot_nn(jnp.concatenate([n0, n1], 0), w_gu[...])
    gate, upward = both[:, :wide], both[:, wide:]
    dhid = contract_cols(jnp.concatenate([c0, c1], 0), w_dn[...]).astype(BF).astype(F32)
    sig = jax.nn.sigmoid(gate)
    act = gate * sig
    hid = (act * upward).astype(BF)
    hid_ref[...] = hid
    both_ref[:, :wide] = (dhid * upward * sig * (1.0 + gate * (1.0 - sig))).astype(BF)
    both_ref[:, wide:] = (dhid * act).astype(BF)
    dn = contract_cols(both_ref[...], w_gu[...])
    dkeep[...] = dn[:rows]
    send[0:rows, :] = dn[rows:].astype(BF)
    out = dot_nn(hid, w_dn[...])
    okeep[...] = out[:rows]
    send[rows:, :] = out[rows:].astype(BF)


def relative_columns(idx, shard):
    return [at(2 * idx[xx] + idx[zz], shard) for xx in (X1, X0) for zz in (ZH1, ZH0)]


def outer_kernel(ff8, places, idx, *refs):
    hids, boths, blocks, (send1, keep1, send2, keep2) = refs[0:4], refs[4:8], refs[8:24], refs[24:28]
    rows = hids[0].shape[0] // 2
    shard = send1.shape[1] // 2
    wide = (ff8 + 127) // 128 * 128
    hid = jnp.concatenate([ref[...] for ref in hids], 0)
    both = jnp.concatenate([ref[...] for ref in boths], 0)
    for j, cols in enumerate(relative_columns(idx, shard)):
        there = slice(j % 2 * shard, (j % 2 + 1) * shard)
        values = [ref[p : p + rows, cols] for ref, p in zip(blocks, places)]
        normed = jnp.concatenate([v for i in range(4) for v in values[4 * i : 4 * i + 2]], 0)
        cot = jnp.concatenate([v for i in range(4) for v in values[4 * i + 2 : 4 * i + 4]], 0)
        down = contract_rows(hid, cot)
        gu = contract_rows(both, normed)
        one, two = (send1, send2) if j < 2 else (keep1, keep2)
        one[0:ff8, there] = down[0:ff8].astype(BF)
        one[ff8:, there] = gu[0:ff8].astype(BF)
        two[:, there] = gu[wide : wide + ff8].astype(BF)


def middle_kernel(idx, e_own, far, up, diag, resid_ref, cot, *refs):
    parts, (dresid_ref, dattn_ref, dmixed_ref, sum_ref) = refs[:4], refs[4:]
    e = e_own[...]
    for v in (far, up, diag):
        e = e + v[...].astype(F32)
    resid = resid_ref[...]
    rms = fold(resid)
    n = resid * rms
    en = e * n
    dresid = cot[...].astype(F32) + rms * (e - n * jnp.mean(en, axis=-1, keepdims=True))
    dresid_ref[...] = dresid
    dattn = dresid.astype(BF)
    dattn_ref[...] = dattn
    sum_ref[...] = jnp.broadcast_to(jnp.sum(en, axis=0, keepdims=True), sum_ref.shape)
    for k, w in enumerate(parts):
        dmixed_ref[:, at(idx[FS + k], w.shape[0])] = contract_cols(dattn, w[...]).astype(BF)


def outer_out_kernel(idx, mixed, dattn, send, keep):
    rows = mixed.shape[0]
    shard = send.shape[2]
    for out, ks in ((send, (1, 3)), (keep, (0, 2))):
        for i, k in enumerate(ks):
            right = dattn[:, at(idx[FS + k], shard)]
            for j, yy in enumerate((Y1, Y0)):
                for kz in range(4):
                    left = mixed[:, at(2 * idx[ZS + kz] + idx[yy], rows)]
                    out[i, (4 * j + kz) * rows : (4 * j + kz + 1) * rows, :] = contract_rows(left, right).astype(BF)


def attend_back_kernel(idx, dm_ref, q_ref, lat_ref, wk_ref, wv_ref, probs_ref, out_ref, qs_ref, dlat_ref, send, keep, dq_ref, up_ref, ds_ref, do_ref, dqs_ref):
    rows = dm_ref.shape[0]
    width = GQ * rows
    half = HD // 2
    low = lax.broadcasted_iota(jnp.int32, (rows, 2 * HD), 1) < HD
    for p in range(HEADS // 2):
        cols = slice(p * 2 * HD, (p + 1) * 2 * HD)
        dm = dm_ref[:, cols]
        none = jnp.zeros_like(dm)
        for j, own in enumerate((jnp.where(low, dm, none), jnp.where(low, none, dm))):
            do_ref[(2 * p + j) * rows : (2 * p + j + 1) * rows, :] = contract_cols(own, wv_ref[:, cols]).astype(BF)
    for g in range(GROUPS):
        lat = lat_ref[:, g * LAT_HEAD : (g + 1) * LAT_HEAD]
        for r in range(0, width, 2 * rows):
            band = slice(g * width + r, g * width + r + 2 * rows)
            do = do_ref[band, :]
            delta = jnp.sum(do.astype(F32) * out_ref[band, :].astype(F32), axis=-1, keepdims=True)
            ds_ref[band, :] = (probs_ref[band, :].astype(F32) * (contract_cols(do, lat) - delta)).astype(BF)
        band = slice(g * width, (g + 1) * width)
        dlat_ref[:, g * LAT_HEAD : (g + 1) * LAT_HEAD] = (
            contract_rows(ds_ref[band, :], qs_ref[band, :]) + contract_rows(probs_ref[band, :], do_ref[band, :])
        ).astype(BF)
        dqs_ref[band, :] = (dot_nn(ds_ref[band, :], lat) * SCALE).astype(BF)
    for p in range(HEADS // 2):
        cols = slice(p * 2 * HD, (p + 1) * 2 * HD)
        bands = [slice((2 * p + j) * rows, (2 * p + j + 1) * rows) for j in range(2)]
        a, b = (dot_nn(dqs_ref[band, :], wk_ref[:, cols]) for band in bands)
        dq_ref[:, cols] = jnp.where(low, a, b).astype(BF)
        f, s = divmod(4 * p, 8)
        for j, band in enumerate(bands):
            gk = contract_rows(q_ref[:, cols], dqs_ref[band, :]).astype(BF)
            gv = contract_rows(dm_ref[:, cols], out_ref[band, :]).astype(BF)
            for i in range(2):
                piece = slice((2 * j + i) * half, (2 * j + i + 1) * half)
                up_ref[f, s + 2 * j + i, 0:half, :] = gk[piece, :]
                up_ref[f, s + 2 * j + i, half:HD, :] = gv[piece, :]
    for k in range(4):
        for out, yy in ((send, Y1), (keep, Y0)):
            block = 2 * idx[ZS + k] + idx[yy]
            n = dlat_ref.shape[1]
            out[k * rows : (k + 1) * rows, 0:n] = dlat_ref[at(block, rows), :]
            out[k * rows : (k + 1) * rows, n:] = dq_ref[:, at(block, 2 * HD)]


def bundle_kernel(idx, dlat, na, wlt, dq, wq, ups, sum_ref, e_ref, send, keep, part_ref, sums_ref):
    rows = dq.shape[0]
    e = contract_cols(dq[...], wq[...])
    e_ref[...] = e
    total = jnp.sum(na[at(idx[ROW0] // rows, rows), :].astype(F32) * e, axis=0, keepdims=True)
    for g in range(GROUPS):
        band = slice(g * LAT_HEAD, (g + 1) * LAT_HEAD)
        part = contract_rows(dlat[:, band], na[...])
        part_ref[band, :] = part.astype(BF)
        total = total + jnp.sum(part * wlt[band, :].astype(F32), axis=0, keepdims=True)
    line = lax.broadcasted_iota(jnp.int32, (16, total.shape[1]), 0)
    sums_ref[...] = jnp.where(line == 0, total, jnp.where(line == 1, sum_ref[0:1, :], 0.0)).astype(BF)
    shard = send.shape[3]
    n_lat = part_ref.shape[0] // 8
    for out, ks in ((send, (1, 3)), (keep, (0, 2))):
        for i, k in enumerate(ks):
            cols = at(idx[FS + k], shard)
            for j, yy in enumerate((Y1, Y0)):
                for kz in range(4):
                    s = 2 * idx[ZS + kz] + idx[yy]
                    out[i, 4 * j + kz, 0:HD, :] = ups[idx[FS + k], s]
                    out[i, 4 * j + kz, HD : HD + n_lat, :] = part_ref[at(s, n_lat), cols]
                    out[i, 4 * j + kz, HD + n_lat :, :] = sums_ref[:, cols]


def outer_query_kernel(idx, na, p0, p1, p2, p3, f1, f2, own, near, far, diag, total_ref):
    rows = p0.shape[0]
    wide = 2 * HD
    total = None
    for k, piece in enumerate((p0, p1, p2, p3)):
        first = p0.shape[1] - 2 * wide
        for j, yy in enumerate((Y0, Y1)):
            right = piece[:, first + j * wide : first + (j + 1) * wide]
            term = contract_rows(na[at(2 * idx[ZS + k] + idx[yy], rows), :], right)
            total = term if total is None else total + term
    total_ref[...] = total.astype(BF)
    n = own.shape[0]
    for k, out in ((0, own), (2, far), (3, diag)):
        out[...] = total_ref[at(idx[FS + k], n), :]
    first = 0
    for ref in (f1, f2):
        near[first : first + ref.shape[0], :] = ref[:, 0 : near.shape[1]]
        first += ref.shape[0]
    for i in range(n // rows):
        near[first:, i * wide : (i + 1) * wide] = total_ref[at(idx[FS + 1] * (n // rows) + i, rows), :]


def tokens_kernel(p0, p1, p2, p3, e_ref, wlt, tok, dresid, out_ref):
    n = wlt.shape[0]
    dlat = wide_sum(p0[:, 0:n], p1[:, 0:n]) + wide_sum(p2[:, 0:n], p3[:, 0:n])
    e = e_ref[...] + dot_nn(dlat.astype(BF), wlt[...])
    values = tok[...].astype(F32)
    rms = fold(values)
    n = values * rms
    out_ref[...] = (dresid[...] + rms * (e - n * jnp.mean(e * n, axis=-1, keepdims=True))).astype(BF)


def wide_sum(left, right):
    return left.astype(F32) + right.astype(F32)


def pass_kernel(*refs):
    pass


def half_kernel(both, second):
    second[...] = both[second.shape[0] :, :]


def through(values, deps):
    n = len(values)
    return pl.pallas_call(
        pass_kernel,
        in_specs=[pl.BlockSpec(memory_space=pl.ANY)] * (n + len(deps)),
        out_specs=[pl.BlockSpec(memory_space=pl.ANY)] * n,
        out_shape=[jax.ShapeDtypeStruct(v.shape, v.dtype) for v in values],
        input_output_aliases={i: i for i in range(n)},
        compiler_params=pltpu.CompilerParams(vmem_limit_bytes=MIB),
    )(*values, *deps)


def rows_kernel(*refs):
    keeps, theres, (e0, e1, e2, e3, o0, o_up, o_x) = refs[0:8], refs[8:12], refs[12:19]
    rows = e0.shape[0]
    for i, e in enumerate((e0, e1, e2, e3)):
        e[...] = wide_sum(keeps[i][...], theres[i][0:rows, :]).astype(e.dtype)
    sums = [wide_sum(keeps[4 + i][...], theres[i][rows:, :]) for i in range(4)]
    o0[...] = sums[0]
    o_up[...] = sums[1]
    o_x[0:rows, :] = sums[2].astype(BF)
    o_x[rows:, :] = sums[3].astype(BF)


def sum_kernel(left, right, out):
    out[...] = wide_sum(left[...], right[...]).astype(BF)


def eleventh_kernel(up_keep, up_there, go_keep, go_there, o_up, o_x, up, go_own, go_far, o_send):
    o_send[...] = wide_sum(o_up[...], o_x[o_up.shape[0] :, :]).astype(BF)
    sum_kernel(up_keep, up_there, up)
    go_own[...] = wide_sum(go_keep[0], go_there[0]).astype(BF)
    go_far[...] = wide_sum(go_keep[1], go_there[1]).astype(BF)


def pieces_kernel(keep, there, p0, p1, p2, p3):
    rows, wide = p0.shape
    n = wide - 4 * HD
    for k, out in enumerate((p0, p1, p2, p3)):
        band = slice(k * rows, (k + 1) * rows)
        out[:, 0:n] = wide_sum(keep[band, 0:n], there[band, 0:n]).astype(BF)
        out[:, n : n + 2 * HD] = keep[band, n:]
        out[:, n + 2 * HD : wide] = there[band, n:]


def exchange_kernel(go_own, go_far, b_keep, b_there, b_x, b_xy, y_send, y_keep):
    tall = b_keep.shape[2]
    for j in range(8):
        band = slice(j % 4 * tall, (j % 4 + 1) * tall)
        (y_send, y_keep)[j // 4][band, :] = wide_sum(b_keep[0, j], b_there[0, j]).astype(BF)
        (b_xy, b_x)[j // 4][band, :] = wide_sum(b_keep[1, j], b_there[1, j]).astype(BF)
    half = go_own.shape[0] // 2
    for i, out in enumerate((y_send, y_keep)):
        band = slice(i * half, (i + 1) * half)
        out[4 * tall :, :] = wide_sum(go_own[band, :], go_far[band, :]).astype(BF)


def quarters_kernel(rows, keep, y_there, x_there, xy_there, z0, z1, z2, z3):
    tall = z0.shape[0] - rows
    for k, out in enumerate((z0, z1, z2, z3)):
        band = slice(k * tall, (k + 1) * tall)
        out[0:tall, :] = (wide_sum(keep[band, :], y_there[band, :]) + wide_sum(x_there[band, :], xy_there[band, :])).astype(BF)
        band = slice(4 * tall + k * rows, 4 * tall + (k + 1) * rows)
        out[tall:, :] = wide_sum(keep[band, :], y_there[band, :]).astype(BF)


def swap(value, axis):
    return lax.ppermute(value, axis, [(0, 1), (1, 0)])


def hop(value, k):
    return lax.ppermute(value, "z", [(i, i ^ k) for i in range(4)])


def corner(value):
    return lax.ppermute(value, ("z", "y"), [(i, i ^ 3) for i in range(8)])


def plus(left, right):
    return left.astype(F32) + right.astype(F32)


def fast_body(tokens, attn_gain, w_query, w_latent, w_key_up, w_value_up, w_out, mlp_gain, w_gate, w_up, w_down, lengths, cotangent):
    x, c, z, y = (lax.axis_index(a) for a in ("x", "c", "z", "y"))
    f, s, zl, zh = 2 * x + c, 2 * z + y, lax.rem(z, 2), z // 2
    rows, d = tokens.shape
    shard = d // 4
    half = shard // 2
    ff8 = w_gate.shape[1] // 8
    wide = (ff8 + 127) // 128 * 128
    n_lat = GROUPS * LAT_HEAD
    keys = 8 * rows

    cw = [(RING[i], RING[(i + 1) % 8]) for i in range(8)]
    ccw = [(b, a) for a, b in cw]
    place = jnp.where(y == 0, z, 7 - z)

    def owner(p):
        p = lax.rem(p + 8, 8)
        return jnp.where(p < 4, 2 * p, 15 - 2 * p)

    def ring(value, pairs):
        return lax.ppermute(value, ("z", "y"), pairs)

    def fold_into(gain, weight):
        return (weight.astype(F32) * gain).astype(BF)

    owners = [s, owner(place - 1), owner(place + 1), owner(place - 2), owner(place + 2), owner(place - 3), owner(place + 3), owner(place - 4)]
    idx = jnp.stack(owners + [f, f ^ 1, f ^ 2, f ^ 3, z, z ^ 1, z ^ 2, z ^ 3, y, y ^ 1, zh, zh ^ 1, zl, s * rows, 4 * c + 2 * zl + y, x, x ^ 1, jnp.where(x != c, 0, jnp.where(zl != c, 1, 2))]).astype(jnp.int32)
    gain_a = attn_gain.astype(F32)[:, None]
    gain_m = mlp_gain.astype(F32)[:, None]

    a1, b1 = ring(tokens, cw), ring(tokens, ccw)
    wl_own = fold_into(gain_a, w_latent)
    wl_far, wl_near = swap(wl_own, "x"), swap(wl_own, "c")
    cut = QW * 3 // 4
    a1, b1 = through((a1, b1), (wl_far,))
    a2, b2 = ring(a1, cw), ring(b1, ccw)
    wl_diag = swap(wl_far, "c")
    wb_own = jnp.concatenate([fold_into(gain_a, w_query), w_key_up, w_value_up], axis=1)
    wb_own, wb_a, wb_b = through((wb_own, wb_own[:, :cut], wb_own[:, cut:]), (a1,))
    wb_near, wb_far = swap(wb_own, "c"), [swap(wb_a, "x")]
    gu_own, gu_near, gu_far = call(columns_kernel, 1, [((shard, 2 * wide), BF)] * 2 + [((2 * shard, 2 * wide), BF)], [((8, shard, 2 * wide), BF)], limit=16)(
        idx, w_gate, w_up, mlp_gain[:, None], deps=(a1,)
    )
    gu_near = swap(gu_near, "c")
    a2, b2 = through((a2, b2), (wb_far[0], gu_own))
    a3, b3 = ring(a2, cw), ring(b2, ccw)
    wo_own = through((w_out,), (a2,))[0]
    wo_far, wo_near = swap(wo_own, "x"), swap(wo_own, "c")
    a3, wb_b = through((a3, wb_b), (b3, wo_far, gu_near))
    down = lax.dynamic_slice_in_dim(w_down, y * ff8, ff8, 0)
    a4 = ring(a3, cw)
    wb_far.append(swap(wb_b, "x"))
    wb_diag, wo_diag = [swap(v, "c") for v in wb_far], swap(wo_far, "c")

    a4, gu_far, cot = through((a4, gu_far, cotangent), (wb_far[1], wo_diag))
    gu_far = swap(gu_far, "x")
    cot_far, cot_up, cot_diag = swap(cot, "y"), hop(cot, 1), corner(cot)
    mixed, probs, outs, qs, queries, na_all, lat_all, w_q, w_key, w_value, w_lat_t = attend(
        idx, lengths, (tokens, a1, b1, a2, b2, a3, b3, a4), (wl_own, wl_near, wl_far, wl_diag), (wb_own, wb_near, *wb_far, *wb_diag)
    )
    w_os = (w_out, wo_near, wo_far, wo_diag)
    resid, normed, pack = call(project_kernel, 1, [((rows, d), F32), ((rows, d), BF), ((5 * rows + shard + ff8, d), BF)])(
        idx, mixed, tokens, *w_os, cot_up, cot_far, cot_diag, cot, gu_far, down
    )

    pack = swap(pack, "c")
    nm_far, nm_up, nm_diag = swap(normed, "y"), hop(normed, 1), corner(normed)
    down_x = through((down,), (normed,))[0]
    pairs = []
    for xx in range(2):
        for zz in range(4):
            pairs.append((((1 - xx) * 2 + zz % 2) * 4 + zz, (xx * 2 + 1 - xx) * 4 + zz))
    down_x = lax.ppermute(down_x, ("x", "c", "z"), pairs)
    w_gu, w_dn, near = call(assemble_kernel, 1, [((d, 2 * wide), BF), ((wide, d), BF), ((5 * rows, d), BF)])(
        idx, gu_own, gu_near, gu_far, pack, down_x, down
    )

    def unit(places, *args, deps=()):
        shapes = [((2 * rows, wide), BF), ((2 * rows, 2 * wide), BF), ((rows, d), F32), ((rows, d), F32), ((2 * rows, d), BF)]
        return call(functools.partial(unit_kernel, places), 0, shapes)(*args, w_gu, w_dn, deps=deps)

    at_own, at_up, at_far, at_diag = (0, 0, 0, 4 * rows), (0, 0, 0, rows), (0, 0, 0, 2 * rows), (0, 0, 0, 3 * rows)
    own_rows = (normed, near, cot, near)
    own = unit(at_own, *own_rows)
    nm_far = through((nm_far,), (w_dn,))[0]
    nm_far2 = swap(nm_far, "c")
    far_rows = (nm_far, nm_far2, cot_far, near)
    far = unit(at_far, *far_rows, deps=(own[0],))
    nm_up = through((nm_up,), (own[0],))[0]
    nm_up2 = swap(nm_up, "c")
    up_rows = (nm_up, nm_up2, cot_up, near)
    up = unit(at_up, *up_rows, deps=(far[0],))
    nm_diag = through((nm_diag,), (own[0],))[0]
    nm_diag2 = swap(nm_diag, "c")
    diag_rows = (nm_diag, nm_diag2, cot_diag, near)
    diag = unit(at_diag, *diag_rows, deps=(up[0],))
    near2, up2, far2, diag2 = (swap(v[4], "c") for v in (own, up, far, diag))
    units = (own, up, far, diag)
    shapes = [((rows, d), F32)] + [((rows, d), BF)] * 3 + [((rows, d), F32)] * 2 + [((2 * rows, d), BF)]
    e_own, *early, o_own, o_up, o_x = call(rows_kernel, 0, shapes)(*[v[2] for v in units], *[v[3] for v in units], near2, up2, far2, diag2)
    d_up, d_far, d_diag = hop(early[0], 1), swap(early[1], "y"), corner(early[2])
    shapes = [((2 * ff8, 2 * shard), BF)] * 2 + [((ff8, 2 * shard), BF)] * 2
    at_all, all_rows = at_own + at_up + at_far + at_diag, own_rows + up_rows + far_rows + diag_rows
    y1_send, y1_keep, y2_send, y2_keep = call(functools.partial(outer_kernel, ff8, at_all), 1, shapes, limit=24)(
        idx, *[v[0] for v in units], *[v[1] for v in units], *all_rows
    )
    y1_there = swap(y1_send, "x")
    dresid, dattn, dmixed, v_m = call(middle_kernel, 1, [((rows, d), F32), ((rows, d), BF), ((rows, QW), BF), ((8, d), F32)])(
        idx, e_own, d_far, d_up, d_diag, resid, cotangent, *w_os
    )

    def home(value):
        pairs = []
        for i in range(8):
            cc, hh, ll = i // 4, i // 2 % 2, i % 2
            pairs.append((i, hh * 4 + 2 * cc + ll))
        return lax.ppermute(value, ("c", "z"), pairs)

    go_send, go_keep = call(outer_out_kernel, 1, [((2, QW, shard), BF)] * 2)(idx, mixed, dattn)
    go_there = swap(go_send, "c")
    f1 = home(call(sum_kernel, 0, [((2 * ff8, 2 * shard), BF)])(y1_keep, y1_there, deps=(go_send,))[0])
    o_x = swap(through((o_x,), (go_send,))[0], "y")
    y2_there = swap(through((y2_send,), (go_send,))[0], "x")
    dlat, p_send, p_keep, dq, ups = call(
        attend_back_kernel,
        1,
        [((keys, n_lat), BF)] + [((4 * rows, n_lat + 2 * HD), BF)] * 2 + [((rows, QW), BF), ((4, 8, HD, LAT_HEAD), BF)],
        [((HEADS * rows, keys), BF), ((HEADS * rows, LAT_HEAD), BF), ((HEADS * rows, LAT_HEAD), BF)],
        limit=40,
        far_in=range(1, 8),
    )(idx, dmixed, queries, lat_all, w_key, w_value, probs, outs, qs, deps=(go_send,))
    tall = HD + n_lat // 8 + 16
    e_q, b_send, b_keep = call(
        bundle_kernel,
        1,
        [((rows, d), F32), ((2, 8, tall, shard), BF), ((2, 8, tall, shard), BF)],
        [((n_lat, d), BF), ((16, d), BF)],
        limit=24,
        far_in=(1, 2, 4),
    )(idx, dlat, na_all, w_lat_t, dq, w_q, ups, v_m)
    f2, go_own, go_far, o_send = call(eleventh_kernel, 0, [((ff8, 2 * shard), BF)] + [((QW, shard), BF)] * 2 + [((rows, d), BF)])(
        y2_keep, y2_there, go_keep, go_there, o_up, o_x, deps=(b_send, f1)
    )
    b_send = through((b_send,), (go_far,))[0]
    p_there = swap(p_send, "y")
    f2, o_there = home(f2), hop(o_send, 1)
    go_far, b_there = swap(go_far, "x"), swap(b_send, "c")
    flat = ((4 * tall, shard), BF)
    tower = ((4 * tall + QW // 2, shard), BF)
    n_p = n_lat + 4 * HD
    p0, p1, p2, p3 = call(pieces_kernel, 0, [((rows, n_p), BF)] * 4)(p_keep, p_there, deps=(b_there,))
    b_x, b_xy, y_send, y_keep = call(exchange_kernel, 0, [flat, flat, tower, tower])(
        go_own, go_far, b_keep, b_there, deps=(f2, o_there)
    )
    pieces = (p0, hop(p1, 1), hop(p2, 2), hop(p3, 3))
    b_x, y_there = swap(b_x, "x"), swap(y_send, "y")
    b_xy = lax.ppermute(b_xy, ("x", "y"), [(i, i ^ 3) for i in range(4)])
    z0, z1, z2, z3 = call(functools.partial(quarters_kernel, rows), 0, [((tall + rows, shard), BF)] * 4)(
        y_keep, y_there, b_x, b_xy
    )
    last = z0.astype(F32) + hop(z1, 1) + hop(z2, 2) + hop(z3, 3)
    quarter = ((shard, 2 * HD), BF)
    gq, near, gq_far, gq_diag = call(
        outer_query_kernel, 1, [quarter, ((3 * ff8 + rows, shard), BF), quarter, quarter], [((d, 2 * HD), BF)], far_in=(0,)
    )(idx, na_all, *pieces, f1, f2, deps=(z0,))
    near, gq_far, gq_diag = swap(near, "c"), swap(gq_far, "x"), lax.ppermute(gq_diag, ("x", "c"), [(i, i ^ 3) for i in range(4)])
    tokens_grad = call(tokens_kernel, 0, [((rows, d), BF)])(*pieces, e_q, w_lat_t, tokens, dresid, deps=(gq,))[0]
    gq_near = jnp.concatenate([near[3 * ff8 :, i * 2 * HD : (i + 1) * 2 * HD] for i in range(shard // rows)], 0)
    grad_query = (plus(gq, gq_near) + plus(gq_far, gq_diag)) * gain_a
    output = (resid + o_own + o_x[:rows] + o_there).astype(BF)
    grad_down = plus(f1[:ff8, shard:], near[:ff8])
    grad_gate = plus(f1[ff8:, shard:], near[ff8 : 2 * ff8]).T * gain_m
    grad_up = plus(f2[:, shard:], near[2 * ff8 : 3 * ff8]).T * gain_m
    grad_out = last[tall:]
    eighth = HD // 2
    n_small = n_lat // 8
    grad_key_up = last[:eighth].T
    grad_value_up = last[eighth:HD].T
    grad_latent = last[HD : HD + n_small].T * gain_a
    own_gain = shard // 8
    pair = lax.dynamic_slice(last, (HD + n_small, s * own_gain), (2, own_gain))
    grad_attn_gain = pair[0] / lax.dynamic_slice_in_dim(gain_a[:, 0], s * own_gain, own_gain)
    grad_mlp_gain = pair[1] / lax.dynamic_slice_in_dim(gain_m[:, 0], s * own_gain, own_gain)
    return (
        output,
        tokens_grad,
        grad_attn_gain,
        grad_query,
        grad_latent,
        grad_key_up,
        grad_value_up,
        grad_out,
        grad_mlp_gain,
        grad_gate,
        grad_up,
        grad_down,
    )


def fast_solution(mesh):
    mesh = Mesh(mesh.devices.reshape(2, 2, 4, 2), ("x", "c", "z", "y"))
    f, s = ("x", "c"), ("z", "y")
    a = f + s
    in_specs = (P(a, None), P(f), P(f, None), P(f, None), P(None, f), P(None, f), P(f, None), P(f), P(f, None), P(f, None), P(f, None), P(f, None), P(a, None))
    out_specs = (P(a, None), P(a, None), P(a), P(f, s), P(f, s), P(None, a), P(None, a), P(s, f), P(a), P(f, s), P(f, s), P(s, f))
    return jax.shard_map(fast_body, mesh=mesh, in_specs=in_specs, out_specs=out_specs, check_vma=False)


def solution(mesh):
    if mesh.shape["fsdp"] == 4 and mesh.shape["seq"] == 8:
        return fast_solution(mesh)
    in_specs = (
        P(("fsdp", "seq"), None),
        P("fsdp"),
        P("fsdp", None),
        P("fsdp", None),
        P(None, "fsdp"),
        P(None, "fsdp"),
        P("fsdp", None),
        P("fsdp"),
        P("fsdp", None),
        P("fsdp", None),
        P("fsdp", None),
        P("fsdp", None),
        P(("fsdp", "seq"), None),
    )
    out_specs = (
        P(("fsdp", "seq"), None),
        P(("fsdp", "seq"), None),
        P(("fsdp", "seq")),
        P("fsdp", "seq"),
        P("fsdp", "seq"),
        P(None, ("fsdp", "seq")),
        P(None, ("fsdp", "seq")),
        P("seq", "fsdp"),
        P(("fsdp", "seq")),
        P("fsdp", "seq"),
        P("fsdp", "seq"),
        P("seq", "fsdp"),
    )
    return jax.shard_map(body, mesh=mesh, in_specs=in_specs, out_specs=out_specs, check_vma=False)
```

```python
import functools

import jax
import jax.numpy as jnp
from jax import lax
from jax.experimental import pallas as pl
from jax.experimental.pallas import tpu as pltpu
from jax.sharding import Mesh
from jax.sharding import PartitionSpec as P

HEADS = 16
HD = 64
GROUPS = 2
LAT_HEAD = 256
KEYBLK = 1024
QW = 1024
GQ = 8


epsilon = 1e-06


def normalize(values, gain):
    return values * lax.rsqrt(jnp.mean(values * values, axis=-1, keepdims=True) + epsilon) * gain


def doc_numbers(lengths_row, count):
    bounds = jnp.cumsum(lengths_row)
    places = jnp.arange(count, dtype=jnp.int32)
    return jnp.sum((places[:, None] >= bounds[None, :-1]).astype(jnp.int32), axis=1)


def contract_rows(left, right):
    return lax.dot_general(
        left, right, (((0,), (0,)), ((), ())), preferred_element_type=jnp.float32
    )


def contract_cols(left, right):
    return lax.dot_general(
        left, right, (((1,), (1,)), ((), ())), preferred_element_type=jnp.float32
    )


def split_parts(values):
    upper = values.astype(jnp.bfloat16)
    lower = (values - upper.astype(jnp.float32)).astype(jnp.bfloat16)
    return (upper, lower)


def gated_unit(gate_pre, upward):
    return jax.nn.silu(gate_pre) * upward


def body(
    tokens,
    attn_gain,
    w_query,
    w_latent,
    w_key_up,
    w_value_up,
    w_out,
    mlp_gain,
    w_gate,
    w_up,
    w_down,
    lengths,
    cotangent,
):
    attn_gain, w_query, w_latent, w_key_up, w_value_up, w_out, mlp_gain, w_gate, w_up, w_down = (
        lax.all_gather(attn_gain, "fsdp", axis=0, tiled=True),
        lax.all_gather(w_query, "fsdp", axis=0, tiled=True),
        lax.all_gather(w_latent, "fsdp", axis=0, tiled=True),
        lax.all_gather(w_key_up, "fsdp", axis=1, tiled=True),
        lax.all_gather(w_value_up, "fsdp", axis=1, tiled=True),
        lax.all_gather(w_out, "fsdp", axis=0, tiled=True),
        lax.all_gather(mlp_gain, "fsdp", axis=0, tiled=True),
        lax.all_gather(w_gate, "fsdp", axis=0, tiled=True),
        lax.all_gather(w_up, "fsdp", axis=0, tiled=True),
        lax.all_gather(w_down, "fsdp", axis=0, tiled=True),
    )
    row_count = tokens.shape[0]
    seq_rank = lax.axis_index("seq")
    stream_len = row_count * lax.axis_size("seq")
    head_width = GQ * HD
    doc_ids = doc_numbers(lengths[0], stream_len)
    row_start = seq_rank * row_count
    own_docs = lax.dynamic_slice_in_dim(doc_ids, row_start, row_count)
    own_places = row_start + jnp.arange(row_count, dtype=jnp.int32)
    block_count = (row_start + row_count - 1) // KEYBLK + 1
    tokens_f = tokens.astype(jnp.float32)
    gain_a = attn_gain.astype(jnp.float32)
    gain_m = mlp_gain.astype(jnp.float32)
    normed = normalize(tokens_f, gain_a).astype(jnp.bfloat16)
    queries = jnp.dot(normed, w_query, preferred_element_type=jnp.float32).astype(jnp.bfloat16)
    latent = jnp.dot(normed, w_latent, preferred_element_type=jnp.float32).astype(jnp.bfloat16)
    gathered = lax.all_gather(latent, "seq", axis=0, tiled=True)
    query_heads = queries.reshape(row_count, HEADS, HD)

    def key_block(source, block_idx, group_idx, with_values):
        latent_part = lax.dynamic_slice(
            source, (block_idx * KEYBLK, group_idx * LAT_HEAD), (KEYBLK, LAT_HEAD)
        )
        low_col = group_idx * head_width
        key_rows = (
            jnp.dot(
                latent_part,
                w_key_up[:, low_col : low_col + head_width],
                preferred_element_type=jnp.float32,
            )
            .astype(jnp.bfloat16)
            .reshape(KEYBLK, GQ, HD)
        )
        value_rows = None
        if with_values:
            value_rows = (
                jnp.dot(
                    latent_part,
                    w_value_up[:, low_col : low_col + head_width],
                    preferred_element_type=jnp.float32,
                )
                .astype(jnp.bfloat16)
                .reshape(KEYBLK, GQ, HD)
            )
        key_docs = lax.dynamic_slice_in_dim(doc_ids, block_idx * KEYBLK, KEYBLK)
        key_places = block_idx * KEYBLK + jnp.arange(KEYBLK, dtype=jnp.int32)
        allowed = (own_docs[:, None] == key_docs[None, :]) & (
            own_places[:, None] >= key_places[None, :]
        )
        return (latent_part, key_rows, value_rows, allowed)

    def block_scores(group_idx, key_rows):
        group_query = query_heads[:, group_idx * GQ : (group_idx + 1) * GQ]
        return (
            jnp.einsum("qhd,khd->hqk", group_query, key_rows, preferred_element_type=jnp.float32)
            * 0.125
        )

    def first_pass(block_idx, carried):
        row_max, row_total = carried
        max_list = []
        total_list = []
        for group_idx in range(GROUPS):
            _, key_rows, _, allowed = key_block(gathered, block_idx, group_idx, False)
            masked = jnp.where(allowed[None], block_scores(group_idx, key_rows), -1e30)
            old_max = row_max[group_idx * GQ : (group_idx + 1) * GQ]
            new_max = jnp.maximum(old_max, jnp.max(masked, axis=-1))
            row_mass = jnp.sum(
                jnp.where(allowed[None], jnp.exp(masked - new_max[:, :, None]), 0.0), axis=-1
            )
            max_list.append(new_max)
            total_list.append(
                row_total[group_idx * GQ : (group_idx + 1) * GQ] * jnp.exp(old_max - new_max)
                + row_mass
            )
        return (jnp.concatenate(max_list, axis=0), jnp.concatenate(total_list, axis=0))

    start_max = jnp.full((HEADS, row_count), -1e30, jnp.float32)
    start_total = jnp.zeros((HEADS, row_count), jnp.float32)
    row_max, row_total = lax.fori_loop(0, block_count, first_pass, (start_max, start_total))
    logsum = row_max + jnp.log(row_total)

    def block_probs(group_idx, key_rows, allowed):
        group_logsum = logsum[group_idx * GQ : (group_idx + 1) * GQ]
        return jnp.where(
            allowed[None],
            jnp.exp(block_scores(group_idx, key_rows) - group_logsum[:, :, None]),
            0.0,
        )

    def second_pass(block_idx, carried):
        rounded_sum, exact_sum = carried
        rounded_list = []
        exact_list = []
        for group_idx in range(GROUPS):
            _, key_rows, value_rows, allowed = key_block(gathered, block_idx, group_idx, True)
            attn_probs = block_probs(group_idx, key_rows, allowed)
            probs_upper, probs_lower = split_parts(attn_probs)
            rounded_part = jnp.einsum(
                "hqk,khd->qhd", probs_upper, value_rows, preferred_element_type=jnp.float32
            )
            rounded_list.append(rounded_part)
            exact_list.append(
                rounded_part
                + jnp.einsum(
                    "hqk,khd->qhd", probs_lower, value_rows, preferred_element_type=jnp.float32
                )
            )
        return (
            rounded_sum + jnp.concatenate(rounded_list, axis=1),
            exact_sum + jnp.concatenate(exact_list, axis=1),
        )

    head_zeros = jnp.zeros((row_count, HEADS, HD), jnp.float32)
    rounded_sum, exact_sum = lax.fori_loop(0, block_count, second_pass, (head_zeros, head_zeros))
    mixed = rounded_sum.reshape(row_count, QW).astype(jnp.bfloat16)
    resid = tokens_f + jnp.dot(mixed, w_out, preferred_element_type=jnp.float32)
    normed_m = normalize(resid, gain_m).astype(jnp.bfloat16)
    gate_pre = jnp.dot(normed_m, w_gate, preferred_element_type=jnp.float32)
    upward = jnp.dot(normed_m, w_up, preferred_element_type=jnp.float32)
    hidden = gated_unit(gate_pre, upward).astype(jnp.bfloat16)
    output = (resid + jnp.dot(hidden, w_down, preferred_element_type=jnp.float32)).astype(
        jnp.bfloat16
    )
    dhidden = contract_cols(cotangent, w_down).astype(jnp.bfloat16)
    _, pull_unit = jax.vjp(gated_unit, gate_pre, upward)
    dgate, dupward = pull_unit(dhidden.astype(jnp.float32))
    dgate = dgate.astype(jnp.bfloat16)
    dupward = dupward.astype(jnp.bfloat16)
    dnormed_m = contract_cols(dgate, w_gate) + contract_cols(dupward, w_up)
    _, pull_norm_m = jax.vjp(normalize, resid, gain_m)
    dresid_norm, grad_mlp_gain = pull_norm_m(dnormed_m)
    dresid = cotangent.astype(jnp.float32) + dresid_norm
    dattn = dresid.astype(jnp.bfloat16)
    dmixed = contract_cols(dattn, w_out).astype(jnp.bfloat16)
    grad_heads = dmixed.reshape(row_count, HEADS, HD)
    row_delta = jnp.einsum("qhd,qhd->hq", grad_heads.astype(jnp.float32), exact_sum)
    source = gathered

    def backward_pass(block_idx, carried):
        dqueries, dlatent, grad_ku, grad_vu = carried
        query_list = []
        fresh_latent = []
        for group_idx in range(GROUPS):
            latent_part, key_rows, value_rows, allowed = key_block(
                source, block_idx, group_idx, True
            )
            low_col = group_idx * head_width
            group_query = query_heads[:, group_idx * GQ : (group_idx + 1) * GQ]
            group_grad = grad_heads[:, group_idx * GQ : (group_idx + 1) * GQ]
            attn_probs = block_probs(group_idx, key_rows, allowed)
            prob_grad = jnp.einsum(
                "qhd,khd->hqk", group_grad, value_rows, preferred_element_type=jnp.float32
            )
            group_delta = row_delta[group_idx * GQ : (group_idx + 1) * GQ]
            score_grad = (attn_probs * (prob_grad - group_delta[:, :, None])).astype(jnp.bfloat16)
            query_list.append(
                jnp.einsum("hqk,khd->qhd", score_grad, key_rows, preferred_element_type=jnp.float32)
                * 0.125
            )
            key_grad = (
                jnp.einsum(
                    "hqk,qhd->khd", score_grad, group_query, preferred_element_type=jnp.float32
                )
                * 0.125
            ).reshape(KEYBLK, head_width)
            value_grad = jnp.einsum(
                "hqk,qhd->khd",
                attn_probs.astype(jnp.bfloat16),
                group_grad,
                preferred_element_type=jnp.float32,
            ).reshape(KEYBLK, head_width)
            key_upper, key_lower = split_parts(key_grad)
            value_upper, value_lower = split_parts(value_grad)
            key_weight = w_key_up[:, low_col : low_col + head_width]
            value_weight = w_value_up[:, low_col : low_col + head_width]
            latent_grad = (
                contract_cols(key_upper, key_weight)
                + contract_cols(key_lower, key_weight)
                + contract_cols(value_upper, value_weight)
                + contract_cols(value_lower, value_weight)
            )
            fresh_latent.append(
                lax.dynamic_update_slice_in_dim(
                    dlatent[group_idx], latent_grad, block_idx * KEYBLK, 0
                )
            )
            grad_ku = grad_ku.at[:, low_col : low_col + head_width].add(
                contract_rows(latent_part, key_upper) + contract_rows(latent_part, key_lower)
            )
            grad_vu = grad_vu.at[:, low_col : low_col + head_width].add(
                contract_rows(latent_part, value_upper) + contract_rows(latent_part, value_lower)
            )
        return (
            dqueries + jnp.concatenate(query_list, axis=1),
            tuple(fresh_latent),
            grad_ku,
            grad_vu,
        )

    latent_zeros = tuple(
        (jnp.zeros((stream_len, LAT_HEAD), jnp.float32) for group_idx in range(GROUPS))
    )
    weight_zeros = jnp.zeros((LAT_HEAD, QW), jnp.float32)
    dqueries, dlatent, grad_key_up, grad_value_up = lax.fori_loop(
        0, block_count, backward_pass, (head_zeros, latent_zeros, weight_zeros, weight_zeros)
    )
    dqueries = dqueries.reshape(row_count, QW).astype(jnp.bfloat16)
    shares = (
        lax.psum_scatter(dlatent[0], "seq", scatter_dimension=0, tiled=True),
        lax.psum_scatter(dlatent[1], "seq", scatter_dimension=0, tiled=True),
    )
    dlatent_own = jnp.concatenate(shares, axis=1).astype(jnp.bfloat16)
    dnormed = contract_cols(dqueries, w_query) + contract_cols(dlatent_own, w_latent)
    _, pull_norm_a = jax.vjp(normalize, tokens_f, gain_a)
    dtokens_norm, grad_attn_gain = pull_norm_a(dnormed)
    tokens_grad = (dresid + dtokens_norm).astype(jnp.bfloat16)
    normed_all, normed_m_all, cotangent_all, dattn_all = (
        lax.all_gather(normed, "seq", axis=0, tiled=True),
        lax.all_gather(normed_m, "seq", axis=0, tiled=True),
        lax.all_gather(cotangent, "seq", axis=0, tiled=True),
        lax.all_gather(dattn, "seq", axis=0, tiled=True),
    )
    hidden_cols, dgate_cols, dupward_cols, mixed_cols, dquery_cols, dlatent_cols = (
        lax.all_to_all(hidden, "seq", split_axis=1, concat_axis=0, tiled=True),
        lax.all_to_all(dgate, "seq", split_axis=1, concat_axis=0, tiled=True),
        lax.all_to_all(dupward, "seq", split_axis=1, concat_axis=0, tiled=True),
        lax.all_to_all(mixed, "seq", split_axis=1, concat_axis=0, tiled=True),
        lax.all_to_all(dqueries, "seq", split_axis=1, concat_axis=0, tiled=True),
        lax.all_to_all(dlatent_own, "seq", split_axis=1, concat_axis=0, tiled=True),
    )
    part_query = contract_rows(normed_all, dquery_cols)
    part_latent = contract_rows(normed_all, dlatent_cols)
    part_out = contract_rows(mixed_cols, dattn_all)
    part_gate = contract_rows(normed_m_all, dgate_cols)
    part_up = contract_rows(normed_m_all, dupward_cols)
    part_down = contract_rows(hidden_cols, cotangent_all)
    grad_query, grad_latent, grad_out, grad_gate, grad_up, grad_down = (
        lax.psum_scatter(
            part_query.astype(jnp.bfloat16), "fsdp", scatter_dimension=0, tiled=True
        ).astype(jnp.float32),
        lax.psum_scatter(
            part_latent.astype(jnp.bfloat16), "fsdp", scatter_dimension=0, tiled=True
        ).astype(jnp.float32),
        lax.psum_scatter(
            part_out.astype(jnp.bfloat16), "fsdp", scatter_dimension=1, tiled=True
        ).astype(jnp.float32),
        lax.psum_scatter(
            part_gate.astype(jnp.bfloat16), "fsdp", scatter_dimension=0, tiled=True
        ).astype(jnp.float32),
        lax.psum_scatter(
            part_up.astype(jnp.bfloat16), "fsdp", scatter_dimension=0, tiled=True
        ).astype(jnp.float32),
        lax.psum_scatter(
            part_down.astype(jnp.bfloat16), "fsdp", scatter_dimension=1, tiled=True
        ).astype(jnp.float32),
    )
    small_sent = (
        lax.psum_scatter(grad_attn_gain, ("fsdp", "seq"), scatter_dimension=0, tiled=True),
        lax.psum_scatter(grad_key_up, ("fsdp", "seq"), scatter_dimension=1, tiled=True),
        lax.psum_scatter(grad_value_up, ("fsdp", "seq"), scatter_dimension=1, tiled=True),
        lax.psum_scatter(grad_mlp_gain, ("fsdp", "seq"), scatter_dimension=0, tiled=True),
    )
    return (
        output,
        tokens_grad,
        small_sent[0],
        grad_query,
        grad_latent,
        small_sent[1],
        small_sent[2],
        grad_out,
        small_sent[3],
        grad_gate,
        grad_up,
        grad_down,
    )


BF = jnp.bfloat16
F32 = jnp.float32
NEG = -1e30
SCALE = 0.125
RING = (0, 2, 4, 6, 7, 5, 3, 1)
MIB = 2**20

FS, ZS, Y0, Y1, ZH0, ZH1, ZL, ROW0, BLOCK, X0, X1, DOWN = 8, 12, 16, 17, 18, 19, 20, 21, 22, 23, 24, 25


def dot_nn(left, right):
    return lax.dot_general(left, right, (((1,), (0,)), ((), ())), preferred_element_type=F32)


def fold(total):
    return lax.rsqrt(jnp.mean(total * total, axis=-1, keepdims=True) + epsilon)


def at(index, size):
    return pl.ds(pl.multiple_of(index * size, size), size)


class Lazy:
    def __init__(self, ref, copy):
        self.ref, self.copy, self.shape = ref, copy, ref.shape

    def __getitem__(self, index):
        if self.copy is not None:
            self.copy.wait()
            self.copy = None
        return self.ref[index]


class Late:
    def __init__(self, ref, out, sems, parts):
        self.ref, self.out, self.sems, self.parts, self.shape, self.copies = ref, out, sems, parts, ref.shape, []

    def __getitem__(self, index):
        return self.ref[index]

    def __setitem__(self, index, value):
        self.ref[index] = value

    def flush(self):
        n = self.shape[0] // self.parts
        band = pl.ds(len(self.copies) * n, n)
        copy = pltpu.make_async_copy(self.ref.at[band], self.out.at[band], self.sems[len(self.copies)])
        copy.start()
        self.copies.append(copy)


def call(kernel, n_smem, outs, scratch=(), limit=16, flops=1, far_in=(), far_out=(), parts=1, split=()):
    far_in, far_out = tuple(far_in), tuple(far_out)
    n_out, n_far, n_sems = len(outs), len(far_in) + len(far_out), len(far_in) + parts * len(far_out)

    def run(*args, deps=()):
        n_in = len(args) - n_smem

        def body(*refs):
            smem, ins, results = refs[:n_smem], list(refs[n_smem : n_smem + n_in]), list(refs[n_smem + n_in + len(deps) : n_smem + n_in + len(deps) + n_out])
            rest = refs[n_smem + n_in + len(deps) + n_out :]
            sems = rest[-1]
            far, own = rest[len(scratch) : len(scratch) + n_far], rest[: len(scratch)]
            for k, i in enumerate(far_in):
                copy = pltpu.make_async_copy(ins[i], far[k], sems.at[k])
                copy.start()
                ins[i] = Lazy(far[k], copy)
            late = []
            for k, i in enumerate(far_out):
                own_sems = [sems.at[len(far_in) + parts * k + p] for p in range(parts)]
                results[i] = Late(far[len(far_in) + k], results[i], own_sems, parts if i in split else 1)
                late.append(results[i])
            kernel(*smem, *ins, *results, *own)
            for i in far_in:
                if ins[i].copy is not None:
                    ins[i].copy.wait()
            for v in late:
                while len(v.copies) < v.parts:
                    v.flush()
            for v in late:
                for copy in v.copies:
                    copy.wait()

        spec = lambda i, far: pl.BlockSpec(memory_space=pl.ANY if i in far else pltpu.VMEM)
        shapes = [pltpu.VMEM(shape, dtype) for shape, dtype in scratch]
        shapes += [pltpu.VMEM(args[n_smem + i].shape, args[n_smem + i].dtype) for i in far_in]
        shapes += [pltpu.VMEM(*outs[i]) for i in far_out]
        return pl.pallas_call(
            body,
            in_specs=[pl.BlockSpec(memory_space=pltpu.SMEM)] * n_smem + [spec(i, far_in) for i in range(n_in)] + [pl.BlockSpec(memory_space=pl.ANY)] * len(deps),
            out_specs=[spec(i, far_out) for i in range(n_out)],
            out_shape=[jax.ShapeDtypeStruct(shape, dtype) for shape, dtype in outs],
            scratch_shapes=shapes + [pltpu.SemaphoreType.DMA((max(1, n_sems),))],
            compiler_params=pltpu.CompilerParams(vmem_limit_bytes=limit * MIB),
            cost_estimate=pl.CostEstimate(flops=flops, bytes_accessed=0, transcendentals=0),
        )(*args, *deps)

    return run


def attend_kernel(idx, lens, *refs):
    tok, wl, wb = refs[0:8], refs[8:12], refs[12:18]
    mixed_ref, probs_ref, out_ref, qs_ref, q_ref, na_ref, lat_ref, wq_ref, wk_ref, wv_ref, wlt_ref, bias_ref = refs[18:30]
    rows, d = tok[0].shape
    keys = 8 * rows
    part = wl[0].shape[0]
    width = GQ * rows
    for i in range(8):
        values = tok[i][...].astype(F32)
        na_ref[at(idx[i], rows), :] = (values * fold(values)).astype(BF)
    na_ref.flush()
    for k in range(4):
        wlt_ref[:, at(idx[FS + k], part)] = wl[k][...].T
    wlt_ref.flush()
    lat_ref[...] = contract_cols(na_ref[...], wlt_ref[...]).astype(BF)
    lat_ref.flush()
    for k in range(4):
        here = at(idx[FS + k], part)
        if k < 2:
            wq_ref[here, :] = wb[k][:, 0:QW]
            wk_ref[:, here] = wb[k][:, QW : QW + LAT_HEAD]
            wv_ref[:, here] = wb[k][:, QW + LAT_HEAD : QW + 2 * LAT_HEAD]
        else:
            first, second = wb[2 * k - 2], wb[2 * k - 1]
            cut = first.shape[1]
            wq_ref[here, 0:cut] = first[...]
            wq_ref[here, cut:QW] = second[:, 0 : QW - cut]
            wk_ref[:, here] = second[:, QW - cut : QW - cut + LAT_HEAD]
            wv_ref[:, here] = second[:, QW - cut + LAT_HEAD : QW - cut + 2 * LAT_HEAD]
    q_ref[...] = dot_nn(na_ref[at(idx[0], rows), :], wq_ref[...]).astype(BF)
    for ref in (wq_ref, wk_ref, wv_ref, q_ref):
        ref.flush()
    place = lax.broadcasted_iota(jnp.int32, (rows, keys), 1)
    own = idx[ROW0] + lax.broadcasted_iota(jnp.int32, (rows, keys), 0)
    first = jnp.zeros((rows, keys), jnp.int32)
    edge = 0
    for i in range(lens.shape[1] - 1):
        edge = edge + lens[0, i]
        first = jnp.where(own >= edge, edge, first)
    bias = jnp.where((place >= first) & (place <= own), 0.0, NEG)
    bias_ref[0:rows, :] = bias
    bias_ref[rows : 2 * rows, :] = bias
    low = lax.broadcasted_iota(jnp.int32, (rows, 2 * HD), 1) < HD
    for p in range(HEADS // 2):
        cols = slice(p * 2 * HD, (p + 1) * 2 * HD)
        q = q_ref[:, cols]
        none = jnp.zeros_like(q)
        for j, own_q in enumerate((jnp.where(low, q, none), jnp.where(low, none, q))):
            qs_ref[(2 * p + j) * rows : (2 * p + j + 1) * rows, :] = (contract_cols(own_q, wk_ref[:, cols]) * SCALE).astype(BF)
    for g in range(GROUPS):
        lat = lat_ref[:, g * LAT_HEAD : (g + 1) * LAT_HEAD]
        for r in range(0, width, 2 * rows):
            band = slice(g * width + r, g * width + r + 2 * rows)
            scores = contract_cols(qs_ref[band, :], lat) + bias_ref[...]
            mass = jnp.exp(scores - jnp.max(scores, axis=-1, keepdims=True))
            probs_ref[band, :] = (mass * (1.0 / jnp.sum(mass, axis=-1, keepdims=True))).astype(BF)
        band = slice(g * width, (g + 1) * width)
        out_ref[band, :] = dot_nn(probs_ref[band, :], lat).astype(BF)
        for ref in (probs_ref, qs_ref, out_ref):
            ref.flush()
    for p in range(HEADS // 2):
        cols = slice(p * 2 * HD, (p + 1) * 2 * HD)
        a, b = (dot_nn(out_ref[(2 * p + j) * rows : (2 * p + j + 1) * rows, :], wv_ref[:, cols]) for j in range(2))
        mixed_ref[:, cols] = jnp.where(low, a, b).astype(BF)


def attend(idx, lens, blocks, w_lats, w_bigs, deps=()):
    rows, d = blocks[0].shape
    keys, n_lat = 8 * rows, GROUPS * LAT_HEAD
    outs = [(rows, QW), (HEADS * rows, keys), (HEADS * rows, LAT_HEAD), (HEADS * rows, LAT_HEAD), (rows, QW)]
    outs += [(keys, d), (keys, n_lat), (d, QW), (LAT_HEAD, QW), (LAT_HEAD, QW), (n_lat, d)]
    macs = 2 * HEADS * rows * keys * LAT_HEAD + keys * d * n_lat
    return call(
        attend_kernel, 2, [(v, BF) for v in outs], [((2 * rows, keys), F32)], limit=60,
        far_in=range(18), far_out=range(1, 11), parts=GROUPS, split=(1, 2, 3),
    )(
        idx, lens, *blocks, *w_lats, *w_bigs, deps=deps
    )


def project_kernel(idx, mixed, tok, *refs):
    parts, (cot_up, cot_far, cot_diag, cot, gu_c, down, resid_ref, normed_ref, pack_ref) = refs[:4], refs[4:]
    total = tok[...].astype(F32)
    for k, w in enumerate(parts):
        total = total + dot_nn(mixed[:, at(idx[FS + k], w.shape[0])], w[...])
    resid_ref[...] = total
    normed = (total * fold(total)).astype(BF)
    normed_ref[...] = normed
    rows = normed.shape[0]
    pack_ref[0:rows, :] = normed
    for i, ref in enumerate((cot_up, cot_far, cot_diag, cot)):
        pack_ref[(i + 1) * rows : (i + 2) * rows, :] = ref[...]
    n = gu_c.shape[0] // 2
    first = 5 * rows
    pack_ref[first : first + n, 0 : gu_c.shape[1]] = gu_c[n:, :]
    pack_ref[first : first + n, gu_c.shape[1] :] = jnp.zeros((n, pack_ref.shape[1] - gu_c.shape[1]), BF)
    pack_ref[first + n :, :] = down[...]


def columns_kernel(idx, gate_ref, up_ref, gain_ref, own_ref, near_ref, pair_ref, all_ref):
    gain = gain_ref[...].astype(F32)
    n, rows, two = all_ref.shape
    cols = gate_ref.shape[1] // n
    gap = jnp.zeros((rows, two // 2 - cols), BF)
    for j in range(n):
        for part, ref in enumerate((gate_ref, up_ref)):
            block = (ref[:, j * cols : (j + 1) * cols].astype(F32) * gain).astype(BF)
            all_ref[j, :, part * (two // 2) : (part + 1) * (two // 2)] = jnp.concatenate([block, gap], axis=1)
    own_ref[...] = all_ref[idx[BLOCK]]
    near_ref[...] = all_ref[idx[BLOCK] ^ 4]
    pair_ref[0:rows, :] = own_ref[...]
    pair_ref[rows:, :] = near_ref[...]


def assemble_kernel(idx, own, near, far, pack, down_x, down, gu_ref, dn_ref, near_ref):
    near_ref[...] = pack[0 : near_ref.shape[0], :]
    part, n = own.shape
    first = pack.shape[0] - down.shape[0]
    for k, w in enumerate((own[...], near[...], far[0:part, :], pack[first - part : first, 0:n])):
        gu_ref[at(idx[FS + k], part), :] = w
    n = down.shape[0]
    for i, ref in enumerate((down_x, pack, down)):

        @pl.when(idx[DOWN] == i)
        def _(ref=ref):
            dn_ref[0:n, :] = ref[-n:, :]

    dn_ref[n:, :] = jnp.zeros((dn_ref.shape[0] - n, dn_ref.shape[1]), BF)


def rows_of(ref, where, rows):
    return ref[where : where + rows, :]


def unit_kernel(places, n0, n1, c0, c1, w_gu, w_dn, hid_ref, both_ref, dkeep, okeep, send):
    rows = dkeep.shape[0]
    wide = w_dn.shape[0]
    n0, n1, c0, c1 = (rows_of(ref, p, rows) for ref, p in zip((n0, n1, c0, c1), places))
    both = dot_nn(jnp.concatenate([n0, n1], 0), w_gu[...])
    gate, upward = both[:, :wide], both[:, wide:]
    dhid = contract_cols(jnp.concatenate([c0, c1], 0), w_dn[...]).astype(BF).astype(F32)
    sig = jax.nn.sigmoid(gate)
    act = gate * sig
    hid = (act * upward).astype(BF)
    hid_ref[...] = hid
    both_ref[:, :wide] = (dhid * upward * sig * (1.0 + gate * (1.0 - sig))).astype(BF)
    both_ref[:, wide:] = (dhid * act).astype(BF)
    dn = contract_cols(both_ref[...], w_gu[...])
    dkeep[...] = dn[:rows]
    send[0:rows, :] = dn[rows:].astype(BF)
    out = dot_nn(hid, w_dn[...])
    okeep[...] = out[:rows]
    send[rows:, :] = out[rows:].astype(BF)


def relative_columns(idx, shard):
    return [at(2 * idx[xx] + idx[zz], shard) for xx in (X1, X0) for zz in (ZH1, ZH0)]


def outer_kernel(ff8, places, idx, *refs):
    hids, boths, blocks, (send1, keep1, send2, keep2) = refs[0:4], refs[4:8], refs[8:24], refs[24:28]
    rows = hids[0].shape[0] // 2
    shard = send1.shape[1] // 2
    wide = (ff8 + 127) // 128 * 128
    hid = jnp.concatenate([ref[...] for ref in hids], 0)
    both = jnp.concatenate([ref[...] for ref in boths], 0)
    for j, cols in enumerate(relative_columns(idx, shard)):
        there = slice(j % 2 * shard, (j % 2 + 1) * shard)
        values = [ref[p : p + rows, cols] for ref, p in zip(blocks, places)]
        normed = jnp.concatenate([v for i in range(4) for v in values[4 * i : 4 * i + 2]], 0)
        cot = jnp.concatenate([v for i in range(4) for v in values[4 * i + 2 : 4 * i + 4]], 0)
        down = contract_rows(hid, cot)
        gu = contract_rows(both, normed)
        one, two = (send1, send2) if j < 2 else (keep1, keep2)
        one[0:ff8, there] = down[0:ff8].astype(BF)
        one[ff8:, there] = gu[0:ff8].astype(BF)
        two[:, there] = gu[wide : wide + ff8].astype(BF)


def middle_kernel(idx, e_own, far, up, diag, resid_ref, cot, *refs):
    parts, (dresid_ref, dattn_ref, dmixed_ref, sum_ref) = refs[:4], refs[4:]
    e = e_own[...]
    for v in (far, up, diag):
        e = e + v[...].astype(F32)
    resid = resid_ref[...]
    rms = fold(resid)
    n = resid * rms
    en = e * n
    dresid = cot[...].astype(F32) + rms * (e - n * jnp.mean(en, axis=-1, keepdims=True))
    dresid_ref[...] = dresid
    dattn = dresid.astype(BF)
    dattn_ref[...] = dattn
    sum_ref[...] = jnp.broadcast_to(jnp.sum(en, axis=0, keepdims=True), sum_ref.shape)
    for k, w in enumerate(parts):
        dmixed_ref[:, at(idx[FS + k], w.shape[0])] = contract_cols(dattn, w[...]).astype(BF)


def outer_out_kernel(idx, mixed, dattn, send, keep):
    rows = mixed.shape[0]
    shard = send.shape[2]
    for out, ks in ((send, (1, 3)), (keep, (0, 2))):
        for i, k in enumerate(ks):
            right = dattn[:, at(idx[FS + k], shard)]
            for j, yy in enumerate((Y1, Y0)):
                for kz in range(4):
                    left = mixed[:, at(2 * idx[ZS + kz] + idx[yy], rows)]
                    out[i, (4 * j + kz) * rows : (4 * j + kz + 1) * rows, :] = contract_rows(left, right).astype(BF)


def attend_back_kernel(idx, dm_ref, q_ref, lat_ref, wk_ref, wv_ref, probs_ref, out_ref, qs_ref, dlat_ref, send, keep, dq_ref, up_ref, ds_ref, do_ref, dqs_ref):
    rows = dm_ref.shape[0]
    width = GQ * rows
    half = HD // 2
    low = lax.broadcasted_iota(jnp.int32, (rows, 2 * HD), 1) < HD
    for p in range(HEADS // 2):
        cols = slice(p * 2 * HD, (p + 1) * 2 * HD)
        dm = dm_ref[:, cols]
        none = jnp.zeros_like(dm)
        for j, own in enumerate((jnp.where(low, dm, none), jnp.where(low, none, dm))):
            do_ref[(2 * p + j) * rows : (2 * p + j + 1) * rows, :] = contract_cols(own, wv_ref[:, cols]).astype(BF)
    for g in range(GROUPS):
        lat = lat_ref[:, g * LAT_HEAD : (g + 1) * LAT_HEAD]
        for r in range(0, width, 2 * rows):
            band = slice(g * width + r, g * width + r + 2 * rows)
            do = do_ref[band, :]
            delta = jnp.sum(do.astype(F32) * out_ref[band, :].astype(F32), axis=-1, keepdims=True)
            ds_ref[band, :] = (probs_ref[band, :].astype(F32) * (contract_cols(do, lat) - delta)).astype(BF)
        band = slice(g * width, (g + 1) * width)
        dlat_ref[:, g * LAT_HEAD : (g + 1) * LAT_HEAD] = (
            contract_rows(ds_ref[band, :], qs_ref[band, :]) + contract_rows(probs_ref[band, :], do_ref[band, :])
        ).astype(BF)
        dqs_ref[band, :] = (dot_nn(ds_ref[band, :], lat) * SCALE).astype(BF)
    for p in range(HEADS // 2):
        cols = slice(p * 2 * HD, (p + 1) * 2 * HD)
        bands = [slice((2 * p + j) * rows, (2 * p + j + 1) * rows) for j in range(2)]
        a, b = (dot_nn(dqs_ref[band, :], wk_ref[:, cols]) for band in bands)
        dq_ref[:, cols] = jnp.where(low, a, b).astype(BF)
        f, s = divmod(4 * p, 8)
        for j, band in enumerate(bands):
            gk = contract_rows(q_ref[:, cols], dqs_ref[band, :]).astype(BF)
            gv = contract_rows(dm_ref[:, cols], out_ref[band, :]).astype(BF)
            for i in range(2):
                piece = slice((2 * j + i) * half, (2 * j + i + 1) * half)
                up_ref[f, s + 2 * j + i, 0:half, :] = gk[piece, :]
                up_ref[f, s + 2 * j + i, half:HD, :] = gv[piece, :]
    for k in range(4):
        for out, yy in ((send, Y1), (keep, Y0)):
            block = 2 * idx[ZS + k] + idx[yy]
            n = dlat_ref.shape[1]
            out[k * rows : (k + 1) * rows, 0:n] = dlat_ref[at(block, rows), :]
            out[k * rows : (k + 1) * rows, n:] = dq_ref[:, at(block, 2 * HD)]


def bundle_kernel(idx, dlat, na, wlt, dq, wq, ups, sum_ref, e_ref, send, keep, part_ref, sums_ref):
    rows = dq.shape[0]
    e = contract_cols(dq[...], wq[...])
    e_ref[...] = e
    total = jnp.sum(na[at(idx[ROW0] // rows, rows), :].astype(F32) * e, axis=0, keepdims=True)
    for g in range(GROUPS):
        band = slice(g * LAT_HEAD, (g + 1) * LAT_HEAD)
        part = contract_rows(dlat[:, band], na[...])
        part_ref[band, :] = part.astype(BF)
        total = total + jnp.sum(part * wlt[band, :].astype(F32), axis=0, keepdims=True)
    line = lax.broadcasted_iota(jnp.int32, (16, total.shape[1]), 0)
    sums_ref[...] = jnp.where(line == 0, total, jnp.where(line == 1, sum_ref[0:1, :], 0.0)).astype(BF)
    shard = send.shape[3]
    n_lat = part_ref.shape[0] // 8
    for out, ks in ((send, (1, 3)), (keep, (0, 2))):
        for i, k in enumerate(ks):
            cols = at(idx[FS + k], shard)
            for j, yy in enumerate((Y1, Y0)):
                for kz in range(4):
                    s = 2 * idx[ZS + kz] + idx[yy]
                    out[i, 4 * j + kz, 0:HD, :] = ups[idx[FS + k], s]
                    out[i, 4 * j + kz, HD : HD + n_lat, :] = part_ref[at(s, n_lat), cols]
                    out[i, 4 * j + kz, HD + n_lat :, :] = sums_ref[:, cols]


def outer_query_kernel(idx, na, p0, p1, p2, p3, f1, f2, own, near, far, diag, total_ref):
    rows = p0.shape[0]
    wide = 2 * HD
    total = None
    for k, piece in enumerate((p0, p1, p2, p3)):
        first = p0.shape[1] - 2 * wide
        for j, yy in enumerate((Y0, Y1)):
            right = piece[:, first + j * wide : first + (j + 1) * wide]
            term = contract_rows(na[at(2 * idx[ZS + k] + idx[yy], rows), :], right)
            total = term if total is None else total + term
    total_ref[...] = total.astype(BF)
    n = own.shape[0]
    for k, out in ((0, own), (2, far), (3, diag)):
        out[...] = total_ref[at(idx[FS + k], n), :]
    first = 0
    for ref in (f1, f2):
        near[first : first + ref.shape[0], :] = ref[:, 0 : near.shape[1]]
        first += ref.shape[0]
    for i in range(n // rows):
        near[first:, i * wide : (i + 1) * wide] = total_ref[at(idx[FS + 1] * (n // rows) + i, rows), :]


def tokens_kernel(p0, p1, p2, p3, e_ref, wlt, tok, dresid, out_ref):
    n = wlt.shape[0]
    dlat = wide_sum(p0[:, 0:n], p1[:, 0:n]) + wide_sum(p2[:, 0:n], p3[:, 0:n])
    e = e_ref[...] + dot_nn(dlat.astype(BF), wlt[...])
    values = tok[...].astype(F32)
    rms = fold(values)
    n = values * rms
    out_ref[...] = (dresid[...] + rms * (e - n * jnp.mean(e * n, axis=-1, keepdims=True))).astype(BF)


def wide_sum(left, right):
    return left.astype(F32) + right.astype(F32)


def pass_kernel(*refs):
    pass


def half_kernel(both, second):
    second[...] = both[second.shape[0] :, :]


def through(values, deps):
    n = len(values)
    return pl.pallas_call(
        pass_kernel,
        in_specs=[pl.BlockSpec(memory_space=pl.ANY)] * (n + len(deps)),
        out_specs=[pl.BlockSpec(memory_space=pl.ANY)] * n,
        out_shape=[jax.ShapeDtypeStruct(v.shape, v.dtype) for v in values],
        input_output_aliases={i: i for i in range(n)},
        compiler_params=pltpu.CompilerParams(vmem_limit_bytes=MIB),
    )(*values, *deps)


def rows_kernel(*refs):
    keeps, theres, (e0, e1, e2, e3, o0, o_up, o_x) = refs[0:8], refs[8:12], refs[12:19]
    rows = e0.shape[0]
    for i, e in enumerate((e0, e1, e2, e3)):
        e[...] = wide_sum(keeps[i][...], theres[i][0:rows, :]).astype(e.dtype)
    sums = [wide_sum(keeps[4 + i][...], theres[i][rows:, :]) for i in range(4)]
    o0[...] = sums[0]
    o_up[...] = sums[1]
    o_x[0:rows, :] = sums[2].astype(BF)
    o_x[rows:, :] = sums[3].astype(BF)


def sum_kernel(left, right, out):
    out[...] = wide_sum(left[...], right[...]).astype(BF)


def eleventh_kernel(up_keep, up_there, go_keep, go_there, o_up, o_x, up, go_own, go_far, o_send):
    o_send[...] = wide_sum(o_up[...], o_x[o_up.shape[0] :, :]).astype(BF)
    sum_kernel(up_keep, up_there, up)
    go_own[...] = wide_sum(go_keep[0], go_there[0]).astype(BF)
    go_far[...] = wide_sum(go_keep[1], go_there[1]).astype(BF)


def pieces_kernel(keep, there, p0, p1, p2, p3):
    rows, wide = p0.shape
    n = wide - 4 * HD
    for k, out in enumerate((p0, p1, p2, p3)):
        band = slice(k * rows, (k + 1) * rows)
        out[:, 0:n] = wide_sum(keep[band, 0:n], there[band, 0:n]).astype(BF)
        out[:, n : n + 2 * HD] = keep[band, n:]
        out[:, n + 2 * HD : wide] = there[band, n:]


def exchange_kernel(go_own, go_far, b_keep, b_there, b_x, b_xy, y_send, y_keep):
    tall = b_keep.shape[2]
    for j in range(8):
        band = slice(j % 4 * tall, (j % 4 + 1) * tall)
        (y_send, y_keep)[j // 4][band, :] = wide_sum(b_keep[0, j], b_there[0, j]).astype(BF)
        (b_xy, b_x)[j // 4][band, :] = wide_sum(b_keep[1, j], b_there[1, j]).astype(BF)
    half = go_own.shape[0] // 2
    for i, out in enumerate((y_send, y_keep)):
        band = slice(i * half, (i + 1) * half)
        out[4 * tall :, :] = wide_sum(go_own[band, :], go_far[band, :]).astype(BF)


def quarters_kernel(rows, keep, y_there, x_there, xy_there, z0, z1, z2, z3):
    tall = z0.shape[0] - rows
    for k, out in enumerate((z0, z1, z2, z3)):
        band = slice(k * tall, (k + 1) * tall)
        out[0:tall, :] = (wide_sum(keep[band, :], y_there[band, :]) + wide_sum(x_there[band, :], xy_there[band, :])).astype(BF)
        band = slice(4 * tall + k * rows, 4 * tall + (k + 1) * rows)
        out[tall:, :] = wide_sum(keep[band, :], y_there[band, :]).astype(BF)


def swap(value, axis):
    return lax.ppermute(value, axis, [(0, 1), (1, 0)])


def hop(value, k):
    return lax.ppermute(value, "z", [(i, i ^ k) for i in range(4)])


def corner(value):
    return lax.ppermute(value, ("z", "y"), [(i, i ^ 3) for i in range(8)])


def plus(left, right):
    return left.astype(F32) + right.astype(F32)


def fast_body(tokens, attn_gain, w_query, w_latent, w_key_up, w_value_up, w_out, mlp_gain, w_gate, w_up, w_down, lengths, cotangent):
    x, c, z, y = (lax.axis_index(a) for a in ("x", "c", "z", "y"))
    f, s, zl, zh = 2 * x + c, 2 * z + y, lax.rem(z, 2), z // 2
    rows, d = tokens.shape
    shard = d // 4
    half = shard // 2
    ff8 = w_gate.shape[1] // 8
    wide = (ff8 + 127) // 128 * 128
    n_lat = GROUPS * LAT_HEAD
    keys = 8 * rows

    cw = [(RING[i], RING[(i + 1) % 8]) for i in range(8)]
    ccw = [(b, a) for a, b in cw]
    place = jnp.where(y == 0, z, 7 - z)

    def owner(p):
        p = lax.rem(p + 8, 8)
        return jnp.where(p < 4, 2 * p, 15 - 2 * p)

    def ring(value, pairs):
        return lax.ppermute(value, ("z", "y"), pairs)

    def fold_into(gain, weight):
        return (weight.astype(F32) * gain).astype(BF)

    owners = [s, owner(place - 1), owner(place + 1), owner(place - 2), owner(place + 2), owner(place - 3), owner(place + 3), owner(place - 4)]
    idx = jnp.stack(owners + [f, f ^ 1, f ^ 2, f ^ 3, z, z ^ 1, z ^ 2, z ^ 3, y, y ^ 1, zh, zh ^ 1, zl, s * rows, 4 * c + 2 * zl + y, x, x ^ 1, jnp.where(x != c, 0, jnp.where(zl != c, 1, 2))]).astype(jnp.int32)
    gain_a = attn_gain.astype(F32)[:, None]
    gain_m = mlp_gain.astype(F32)[:, None]

    a1, b1 = ring(tokens, cw), ring(tokens, ccw)
    wl_own = fold_into(gain_a, w_latent)
    wl_far, wl_near = swap(wl_own, "x"), swap(wl_own, "c")
    cut = QW * 3 // 4
    a1, b1 = through((a1, b1), (wl_far,))
    a2, b2 = ring(a1, cw), ring(b1, ccw)
    wl_diag = swap(wl_far, "c")
    wb_own = jnp.concatenate([fold_into(gain_a, w_query), w_key_up, w_value_up], axis=1)
    wb_own, wb_a, wb_b = through((wb_own, wb_own[:, :cut], wb_own[:, cut:]), (a1,))
    wb_near, wb_far = swap(wb_own, "c"), [swap(wb_a, "x")]
    gu_own, gu_near, gu_far = call(columns_kernel, 1, [((shard, 2 * wide), BF)] * 2 + [((2 * shard, 2 * wide), BF)], [((8, shard, 2 * wide), BF)], limit=16)(
        idx, w_gate, w_up, mlp_gain[:, None], deps=(a1,)
    )
    gu_near = swap(gu_near, "c")
    a2, b2 = through((a2, b2), (wb_far[0], gu_own))
    a3, b3 = ring(a2, cw), ring(b2, ccw)
    wo_own = through((w_out,), (a2,))[0]
    wo_far, wo_near = swap(wo_own, "x"), swap(wo_own, "c")
    a3, wb_b = through((a3, wb_b), (b3, wo_far, gu_near))
    down = lax.dynamic_slice_in_dim(w_down, y * ff8, ff8, 0)
    a4 = ring(a3, cw)
    wb_far.append(swap(wb_b, "x"))
    wb_diag, wo_diag = [swap(v, "c") for v in wb_far], swap(wo_far, "c")

    a4, gu_far, cot = through((a4, gu_far, cotangent), (wb_far[1], wo_diag))
    gu_far = swap(gu_far, "x")
    cot_far, cot_up, cot_diag = swap(cot, "y"), hop(cot, 1), corner(cot)
    mixed, probs, outs, qs, queries, na_all, lat_all, w_q, w_key, w_value, w_lat_t = attend(
        idx, lengths, (tokens, a1, b1, a2, b2, a3, b3, a4), (wl_own, wl_near, wl_far, wl_diag), (wb_own, wb_near, *wb_far, *wb_diag)
    )
    w_os = (w_out, wo_near, wo_far, wo_diag)
    resid, normed, pack = call(project_kernel, 1, [((rows, d), F32), ((rows, d), BF), ((5 * rows + shard + ff8, d), BF)])(
        idx, mixed, tokens, *w_os, cot_up, cot_far, cot_diag, cot, gu_far, down
    )

    pack = swap(pack, "c")
    nm_far, nm_up, nm_diag = swap(normed, "y"), hop(normed, 1), corner(normed)
    down_x = through((down,), (normed,))[0]
    pairs = []
    for xx in range(2):
        for zz in range(4):
            pairs.append((((1 - xx) * 2 + zz % 2) * 4 + zz, (xx * 2 + 1 - xx) * 4 + zz))
    down_x = lax.ppermute(down_x, ("x", "c", "z"), pairs)
    w_gu, w_dn, near = call(assemble_kernel, 1, [((d, 2 * wide), BF), ((wide, d), BF), ((5 * rows, d), BF)])(
        idx, gu_own, gu_near, gu_far, pack, down_x, down
    )

    def unit(places, *args, deps=()):
        shapes = [((2 * rows, wide), BF), ((2 * rows, 2 * wide), BF), ((rows, d), F32), ((rows, d), F32), ((2 * rows, d), BF)]
        return call(functools.partial(unit_kernel, places), 0, shapes)(*args, w_gu, w_dn, deps=deps)

    at_own, at_up, at_far, at_diag = (0, 0, 0, 4 * rows), (0, 0, 0, rows), (0, 0, 0, 2 * rows), (0, 0, 0, 3 * rows)
    own_rows = (normed, near, cot, near)
    own = unit(at_own, *own_rows)
    nm_far = through((nm_far,), (w_dn,))[0]
    nm_far2 = swap(nm_far, "c")
    far_rows = (nm_far, nm_far2, cot_far, near)
    far = unit(at_far, *far_rows, deps=(own[0],))
    nm_up = through((nm_up,), (own[0],))[0]
    nm_up2 = swap(nm_up, "c")
    up_rows = (nm_up, nm_up2, cot_up, near)
    up = unit(at_up, *up_rows, deps=(far[0],))
    nm_diag = through((nm_diag,), (own[0],))[0]
    nm_diag2 = swap(nm_diag, "c")
    diag_rows = (nm_diag, nm_diag2, cot_diag, near)
    diag = unit(at_diag, *diag_rows, deps=(up[0],))
    near2, up2, far2, diag2 = (swap(v[4], "c") for v in (own, up, far, diag))
    units = (own, up, far, diag)
    shapes = [((rows, d), F32)] + [((rows, d), BF)] * 3 + [((rows, d), F32)] * 2 + [((2 * rows, d), BF)]
    e_own, *early, o_own, o_up, o_x = call(rows_kernel, 0, shapes)(*[v[2] for v in units], *[v[3] for v in units], near2, up2, far2, diag2)
    d_up, d_far, d_diag = hop(early[0], 1), swap(early[1], "y"), corner(early[2])
    shapes = [((2 * ff8, 2 * shard), BF)] * 2 + [((ff8, 2 * shard), BF)] * 2
    at_all, all_rows = at_own + at_up + at_far + at_diag, own_rows + up_rows + far_rows + diag_rows
    y1_send, y1_keep, y2_send, y2_keep = call(functools.partial(outer_kernel, ff8, at_all), 1, shapes, limit=24)(
        idx, *[v[0] for v in units], *[v[1] for v in units], *all_rows
    )
    y1_there = swap(y1_send, "x")
    dresid, dattn, dmixed, v_m = call(middle_kernel, 1, [((rows, d), F32), ((rows, d), BF), ((rows, QW), BF), ((8, d), F32)])(
        idx, e_own, d_far, d_up, d_diag, resid, cotangent, *w_os
    )

    def home(value):
        pairs = []
        for i in range(8):
            cc, hh, ll = i // 4, i // 2 % 2, i % 2
            pairs.append((i, hh * 4 + 2 * cc + ll))
        return lax.ppermute(value, ("c", "z"), pairs)

    go_send, go_keep = call(outer_out_kernel, 1, [((2, QW, shard), BF)] * 2)(idx, mixed, dattn)
    go_there = swap(go_send, "c")
    f1 = home(call(sum_kernel, 0, [((2 * ff8, 2 * shard), BF)])(y1_keep, y1_there, deps=(go_send,))[0])
    o_x = swap(through((o_x,), (go_send,))[0], "y")
    y2_there = swap(through((y2_send,), (go_send,))[0], "x")
    dlat, p_send, p_keep, dq, ups = call(
        attend_back_kernel,
        1,
        [((keys, n_lat), BF)] + [((4 * rows, n_lat + 2 * HD), BF)] * 2 + [((rows, QW), BF), ((4, 8, HD, LAT_HEAD), BF)],
        [((HEADS * rows, keys), BF), ((HEADS * rows, LAT_HEAD), BF), ((HEADS * rows, LAT_HEAD), BF)],
        limit=40,
        far_in=range(1, 8),
    )(idx, dmixed, queries, lat_all, w_key, w_value, probs, outs, qs, deps=(go_send,))
    tall = HD + n_lat // 8 + 16
    e_q, b_send, b_keep = call(
        bundle_kernel,
        1,
        [((rows, d), F32), ((2, 8, tall, shard), BF), ((2, 8, tall, shard), BF)],
        [((n_lat, d), BF), ((16, d), BF)],
        limit=24,
        far_in=(1, 2, 4),
    )(idx, dlat, na_all, w_lat_t, dq, w_q, ups, v_m)
    f2, go_own, go_far, o_send = call(eleventh_kernel, 0, [((ff8, 2 * shard), BF)] + [((QW, shard), BF)] * 2 + [((rows, d), BF)])(
        y2_keep, y2_there, go_keep, go_there, o_up, o_x, deps=(b_send, f1)
    )
    b_send = through((b_send,), (go_far,))[0]
    p_there = swap(p_send, "y")
    f2, o_there = home(f2), hop(o_send, 1)
    go_far, b_there = swap(go_far, "x"), swap(b_send, "c")
    flat = ((4 * tall, shard), BF)
    tower = ((4 * tall + QW // 2, shard), BF)
    n_p = n_lat + 4 * HD
    p0, p1, p2, p3 = call(pieces_kernel, 0, [((rows, n_p), BF)] * 4)(p_keep, p_there, deps=(b_there,))
    b_x, b_xy, y_send, y_keep = call(exchange_kernel, 0, [flat, flat, tower, tower])(
        go_own, go_far, b_keep, b_there, deps=(f2, o_there)
    )
    pieces = (p0, hop(p1, 1), hop(p2, 2), hop(p3, 3))
    b_x, y_there = swap(b_x, "x"), swap(y_send, "y")
    b_xy = lax.ppermute(b_xy, ("x", "y"), [(i, i ^ 3) for i in range(4)])
    z0, z1, z2, z3 = call(functools.partial(quarters_kernel, rows), 0, [((tall + rows, shard), BF)] * 4, far_in=(0,))(
        y_keep, y_there, b_x, b_xy
    )
    last = z0.astype(F32) + hop(z1, 1) + hop(z2, 2) + hop(z3, 3)
    quarter = ((shard, 2 * HD), BF)
    gq, near, gq_far, gq_diag = call(
        outer_query_kernel, 1, [quarter, ((3 * ff8 + rows, shard), BF), quarter, quarter], [((d, 2 * HD), BF)], far_in=(0,)
    )(idx, na_all, *pieces, f1, f2, deps=(z0,))
    near, gq_far, gq_diag = swap(near, "c"), swap(gq_far, "x"), lax.ppermute(gq_diag, ("x", "c"), [(i, i ^ 3) for i in range(4)])
    tokens_grad = call(tokens_kernel, 0, [((rows, d), BF)])(*pieces, e_q, w_lat_t, tokens, dresid, deps=(gq,))[0]
    gq_near = jnp.concatenate([near[3 * ff8 :, i * 2 * HD : (i + 1) * 2 * HD] for i in range(shard // rows)], 0)
    grad_query = (plus(gq, gq_near) + plus(gq_far, gq_diag)) * gain_a
    output = (resid + o_own + o_x[:rows] + o_there).astype(BF)
    grad_down = plus(f1[:ff8, shard:], near[:ff8])
    grad_gate = plus(f1[ff8:, shard:], near[ff8 : 2 * ff8]).T * gain_m
    grad_up = plus(f2[:, shard:], near[2 * ff8 : 3 * ff8]).T * gain_m
    grad_out = last[tall:]
    eighth = HD // 2
    n_small = n_lat // 8
    grad_key_up = last[:eighth].T
    grad_value_up = last[eighth:HD].T
    grad_latent = last[HD : HD + n_small].T * gain_a
    own_gain = shard // 8
    pair = lax.dynamic_slice(last, (HD + n_small, s * own_gain), (2, own_gain))
    grad_attn_gain = pair[0] / lax.dynamic_slice_in_dim(gain_a[:, 0], s * own_gain, own_gain)
    grad_mlp_gain = pair[1] / lax.dynamic_slice_in_dim(gain_m[:, 0], s * own_gain, own_gain)
    return (
        output,
        tokens_grad,
        grad_attn_gain,
        grad_query,
        grad_latent,
        grad_key_up,
        grad_value_up,
        grad_out,
        grad_mlp_gain,
        grad_gate,
        grad_up,
        grad_down,
    )


def fast_solution(mesh):
    mesh = Mesh(mesh.devices.reshape(2, 2, 4, 2), ("x", "c", "z", "y"))
    f, s = ("x", "c"), ("z", "y")
    a = f + s
    in_specs = (P(a, None), P(f), P(f, None), P(f, None), P(None, f), P(None, f), P(f, None), P(f), P(f, None), P(f, None), P(f, None), P(f, None), P(a, None))
    out_specs = (P(a, None), P(a, None), P(a), P(f, s), P(f, s), P(None, a), P(None, a), P(s, f), P(a), P(f, s), P(f, s), P(s, f))
    return jax.shard_map(fast_body, mesh=mesh, in_specs=in_specs, out_specs=out_specs, check_vma=False)


def solution(mesh):
    if mesh.shape["fsdp"] == 4 and mesh.shape["seq"] == 8:
        return fast_solution(mesh)
    in_specs = (
        P(("fsdp", "seq"), None),
        P("fsdp"),
        P("fsdp", None),
        P("fsdp", None),
        P(None, "fsdp"),
        P(None, "fsdp"),
        P("fsdp", None),
        P("fsdp"),
        P("fsdp", None),
        P("fsdp", None),
        P("fsdp", None),
        P("fsdp", None),
        P(("fsdp", "seq"), None),
    )
    out_specs = (
        P(("fsdp", "seq"), None),
        P(("fsdp", "seq"), None),
        P(("fsdp", "seq")),
        P("fsdp", "seq"),
        P("fsdp", "seq"),
        P(None, ("fsdp", "seq")),
        P(None, ("fsdp", "seq")),
        P("seq", "fsdp"),
        P(("fsdp", "seq")),
        P("fsdp", "seq"),
        P("fsdp", "seq"),
        P("seq", "fsdp"),
    )
    return jax.shard_map(body, mesh=mesh, in_specs=in_specs, out_specs=out_specs, check_vma=False)
```
